32 devices in a mesh: row: 4 (over y, x), col: 8 (over z, core).
Axes of the slice: x: 2, y: 2, z: 4, core: 2. Of those that a mesh axis runs over, the one named last changes fastest.
Arguments:
- features: bfloat16 [8, 128, 64, 1024], P('row', 'col'), may hold values from -6 to 6
- tissue: int32 [8, 128, 64], P('row', 'col'), may hold values 0 or 1
- probe: float32 [8, 128, 4096], P('row', 'col'), may hold values from -6 to 6
Outputs:
- basis: float32 [8, 128, 4096], P('row', 'col')
The draws below stay inside these ranges and needn't reach their ends.
All inputs are finite; a program needn't handle non-finite values. No bound on the sum of `tissue` on one device may be relied on, other than what follows from the above.
Results may differ from the reference program's by a relative error of at most 0.00091.
Values may be sent and summed in bfloat16 or wider, within the bound.
No kernel may reach another device: no remote copies, remote signals or barrier semaphores. Data moves between devices by JAX's collectives and lax.ppermute only.
A program may use at most 128 MiB of HBM per device.

```python
import math
import jax
import jax.numpy as jnp
from jax import lax

D = 1024
PATCH = 64
RANK = 64
ITERS = 3
NR = 8
NC = 128


def with_ends(values, rng, low, high):
    spot = [jax.random.randint(jax.random.fold_in(rng, axis), (), 0, length) for axis, length in enumerate(values.shape)]
    main_axis = values.shape.index(max(values.shape))
    next_to = spot[:main_axis] + [(spot[main_axis] + 1) % values.shape[main_axis]] + spot[main_axis + 1:]
    return values.at[tuple(spot)].set(low).at[tuple(next_to)].set(high)


def block_scale(rng, extent, pieces, least, top_value):
    loudness = 1.0
    for dim, blocks in pieces:
        draws = jax.random.uniform(jax.random.fold_in(jax.random.fold_in(rng, 6), dim), (blocks,), jnp.float32, least / len(pieces), top_value / len(pieces))
        loudness = loudness * jnp.repeat(jnp.exp(draws), extent[dim] // blocks).reshape((-1,) + (1,) * (len(extent) - 1 - dim))
    return loudness


def centred(own_key, extent, spread, most, split=(), kind=jnp.bfloat16):
    level = block_scale(own_key, extent, split, -0.22, 0.18) if split else 1.0
    drawn = jax.random.normal(own_key, extent, jnp.float32) * spread * level
    return jnp.minimum(jnp.maximum(drawn, -most), most).astype(kind)


def setup_inputs(seed: int = 0) -> dict:
    key_of = jax.random.split(jax.random.key(seed), 4)
    features = centred(key_of[0], (NR, NC, PATCH, D), 1.0, 6.0, ((0, 4), (1, 8)))
    tissue = with_ends((jax.random.randint(key_of[1], (NR, NC, PATCH), 0, 4) < 3).astype(jnp.int32), jax.random.fold_in(key_of[1], 1), 0, 1)
    probe = centred(key_of[2], (NR, NC, PATCH * RANK), 1.0, 6.0, ((0, 4), (1, 8)), jnp.float32)
    return dict(features=features, tissue=tissue, probe=probe)


AFFINITY_TEMP = 4.0

def normalized(features):
    values = features.astype(jnp.float32)
    scaled = values * lax.rsqrt(lax.optimization_barrier(jnp.sum(values * values, axis=-1, keepdims=True)) + 1e-06)
    return scaled.astype(jnp.bfloat16)

def reference(features, tissue, probe):
    unit = normalized(features)
    tissue_float = tissue.astype(jnp.float32)
    padded = jnp.pad(unit, ((1, 1), (1, 1), (0, 0), (0, 0)))
    padded_mask = jnp.pad(tissue_float, ((1, 1), (1, 1), (0, 0)))

    def tile_row(start):
        rows = lax.dynamic_slice_in_dim(padded, start, 3, 0).astype(jnp.float32)
        masks = lax.dynamic_slice_in_dim(padded_mask, start, 3, 0)
        centre = rows[1, 1:NC + 1]
        central_mask = masks[1, 1:NC + 1]
        blocks = []
        for shift_row in range(3):
            for shift_col in range(3):
                other = rows[shift_row, shift_col:shift_col + NC]
                neighbour_mask = masks[shift_row, shift_col:shift_col + NC]
                affinity_scores = jnp.einsum('cpd,cqd->cpq', centre, other, precision=lax.Precision.HIGHEST)
                affinity_weights = central_mask[:, :, None] * neighbour_mask[:, None, :] * jnp.exp(AFFINITY_TEMP * (affinity_scores - 1.0))
                blocks.append(affinity_weights)
        return jnp.concatenate(blocks, axis=2)
    affinity = lax.map(tile_row, jnp.arange(NR, dtype=jnp.int32))
    degree = 1.0 + lax.optimization_barrier(jnp.sum(affinity, axis=-1))
    inverse_root = lax.rsqrt(degree)
    panel = probe.reshape(NR, NC, PATCH, RANK)
    for step in range(ITERS):
        carried = inverse_root[..., None] * panel
        padded_panel = jnp.pad(carried, ((1, 1), (1, 1), (0, 0), (0, 0)))
        summed = jnp.zeros((NR, NC, PATCH, RANK), jnp.float32)
        for shift_row in range(3):
            for shift_col in range(3):
                which = 3 * shift_row + shift_col
                block = affinity[:, :, :, which * PATCH:(which + 1) * PATCH]
                source = padded_panel[shift_row:shift_row + NR, shift_col:shift_col + NC]
                summed = summed + jnp.einsum('abpq,abqk->abpk', block, source, precision=lax.Precision.HIGHEST)
        image = panel + inverse_root[..., None] * summed
        flat = image.reshape(-1, RANK)
        gram_matrix = jnp.dot(flat.T.astype(jnp.float32), flat.astype(jnp.float32), precision=lax.Precision.HIGHEST, preferred_element_type=jnp.float32)
        lower = jnp.linalg.cholesky(gram_matrix)
        solved = jax.scipy.linalg.solve_triangular(lower, flat.T, lower=True)
        panel = solved.T.reshape(NR, NC, PATCH, RANK)
    factor = math.sqrt(float(NR * NC * PATCH))
    return (factor * panel).reshape(NR, NC, PATCH * RANK)
```

```python
import functools
import math

import jax
import jax.numpy as jnp
from jax import lax
from jax.experimental import pallas as pl
from jax.experimental.pallas import tpu as pltpu
from jax.sharding import PartitionSpec as P

RANK = 64
ITERS = 3
AFFINITY_TEMP = 4.0

GHOST = ITERS + 1
TINY = 1e-30
VMEM_BYTES = 56 * 1024 * 1024
FLOOR = math.exp(-AFFINITY_TEMP)
ABT = (((1,), (1,)), ((), ()))
ATB = (((0,), (0,)), ((), ()))

f32 = jnp.float32
bf16 = jnp.bfloat16


def kernel_call(body, out_shape, scratch=(), cost=0):
    return pl.pallas_call(
        body,
        out_shape=out_shape,
        scratch_shapes=list(scratch),
        compiler_params=pltpu.CompilerParams(vmem_limit_bytes=VMEM_BYTES),
        cost_estimate=pl.CostEstimate(flops=cost, bytes_accessed=1 << 20, transcendentals=0),
    )


def sds(shape, dtype):
    return jax.ShapeDtypeStruct(shape, dtype)


def iota(shape, dim):
    return lax.broadcasted_iota(jnp.int32, shape, dim)


def identity(n):
    return iota((n, n), 0) == iota((n, n), 1)


def to_lanes(column, eye):
    return jnp.sum(jnp.where(eye, column, 0.0), axis=0, keepdims=True)


def to_sublanes(row, eye):
    return jnp.sum(jnp.where(eye, row, 0.0), axis=1, keepdims=True)


def unit_and_mask(block):
    values = block.astype(f32)
    scaled = values * lax.rsqrt(jnp.sum(values * values, axis=-1, keepdims=True) + 1e-06)
    return scaled.astype(bf16), (values[:, :1] != 0.0).astype(f32)


def affinity_of(left, right):
    scores = lax.dot_general(left, right, ABT, preferred_element_type=f32)
    return jnp.exp(AFFINITY_TEMP * scores - AFFINITY_TEMP)


def masked_sum(weights, mask):
    absent = mask.shape[0] - jnp.sum(mask, axis=0, keepdims=True)
    return jnp.sum(weights, axis=1, keepdims=True) - FLOOR * absent


def packed(block):
    half = block.shape[0] // 2
    return jnp.concatenate([block[:half], block[half:]], axis=1)


def unpacked(block):
    return jnp.concatenate([block[:, :RANK], block[:, RANK:]], axis=0)


def pair_of(values):
    high = values.astype(bf16)
    return high, (values - high.astype(f32)).astype(bf16)


def own_kernel(n, x_ref, xl_ref, xr_ref, p_ref, m_ref, u1_ref, stat_ref, pay_ref, unit_ref, mask_ref):
    rows, cols, patch, width = x_ref.shape
    both = rows * patch
    eye = identity(both)
    small_eye = identity(patch)

    def normalise(ref, index, e):
        for row in range(rows):
            unit, mask = unit_and_mask(ref[row, index])
            start = pl.multiple_of(e * both + row * patch, patch)
            unit_ref[pl.ds(start, patch), :] = unit
            mask_ref[pl.ds(start, patch), :] = mask
            if row == rows - 1:
                u1_ref[e] = unit

    def loop(ref, count, first):
        def step(i, carry):
            normalise(ref, i, first + i)
            return carry

        lax.fori_loop(0, count, step, 0)

    loop(xl_ref, GHOST, 0)
    loop(x_ref, cols, GHOST)
    loop(xr_ref, GHOST, GHOST + cols)
    tail = (n - 2) * patch // 2
    pay_ref[tail:, :] = jnp.zeros((pay_ref.shape[0] - tail, 2 * RANK), bf16)

    def band(e, carry):
        around = pl.ds(pl.multiple_of((e - 1) * both, both), 3 * both)
        here = pl.ds(pl.multiple_of(e * both, both), both)
        weights = affinity_of(unit_ref[here, :], unit_ref[around, :])
        degree = masked_sum(weights, mask_ref[around, :])
        centre = weights[:, both : 2 * both]
        diagonal = jnp.sum(jnp.where(eye, centre, 0.0), axis=1, keepdims=True)
        m_ref[e, :, :both] = weights[:, :both].astype(bf16)
        m_ref[e, :, both : 2 * both] = jnp.where(eye, 0.0, centre).astype(bf16)
        m_ref[e, :, 2 * both :] = weights[:, 2 * both :].astype(bf16)
        stat_ref[e, :, 0:1] = degree
        stat_ref[e, :, 1:2] = diagonal
        stat_ref[e, :, 2:3] = mask_ref[here, :]
        return carry

    lax.fori_loop(1, n - 1, band, 0)
    for e in range(1, n - 1):
        high, low = pair_of(to_lanes(stat_ref[e, :patch, 0:1], small_eye))
        pay_ref[tail + e : tail + e + 1, :patch] = high
        pay_ref[tail + 32 + e : tail + 33 + e, :patch] = low
        at = (e - 1) * patch // 2
        pay_ref[at : at + patch // 2, :] = packed(p_ref[0, e]).astype(bf16)


def payload_rows(n, patch):
    return (n - 2) * patch // 2 + 64


def own_affinity(x, xl, xr, panel):
    rows, cols, patch, width = x.shape
    n = cols + 2 * GHOST
    both = rows * patch
    return kernel_call(
        functools.partial(own_kernel, n),
        (
            sds((n, both, 3 * both), bf16),
            sds((n, patch, width), bf16),
            sds((n, both, 128), f32),
            sds((payload_rows(n, patch), 2 * RANK), bf16),
        ),
        [pltpu.VMEM((n * both, width), bf16), pltpu.VMEM((n * both, 1), f32)],
        cost=2 * n * both * 3 * both * width,
    )(x, xl, xr, panel)


def cross_columns(columns, sources, u1_ref, unit_ref, mask_ref, v_ref, w_ref, stat_ref):
    patch = u1_ref.shape[1]
    needed = sorted({c for e in columns for c in (e - 1, e, e + 1)})
    for c in needed:
        ref, index = sources[c]
        unit, mask = unit_and_mask(ref[index])
        unit_ref[c * patch : (c + 1) * patch, :] = unit
        mask_ref[c * patch : (c + 1) * patch, :] = mask
    for place, e in enumerate(columns):
        around = slice((e - 1) * patch, (e + 2) * patch)
        here = slice(e * patch, (e + 1) * patch)
        above = u1_ref[e - 1 : e + 2].reshape(3 * patch, u1_ref.shape[2])
        down = affinity_of(u1_ref[e], unit_ref[around, :])
        up = affinity_of(unit_ref[here, :], above)
        v_ref[place] = down.astype(bf16)
        w_ref[place] = up.astype(bf16)
        stat_ref[place, :, 0:1] = masked_sum(down, mask_ref[around, :])
        stat_ref[place, :, 1:2] = jnp.sum(up, axis=1, keepdims=True)
        stat_ref[place, :, 2:3] = mask_ref[here, :]


def edge_columns(n):
    return list(range(1, 2 * GHOST - 1)) + list(range(n - 2 * GHOST + 1, n - 1))


def middle_columns(n):
    return list(range(2 * GHOST - 1, n - 2 * GHOST + 1))


def below_sources(n, bl_ref, be_ref, bm_ref, br_ref):
    sources = {}
    for c in range(n):
        if c < GHOST:
            sources[c] = (bl_ref, c)
        elif c < 2 * GHOST:
            sources[c] = (be_ref, c - GHOST)
        elif c < n - 2 * GHOST:
            sources[c] = (bm_ref, c - 2 * GHOST)
        elif c < n - GHOST:
            sources[c] = (be_ref, c - (n - 2 * GHOST) + GHOST)
        else:
            sources[c] = (br_ref, c - (n - GHOST))
    return sources


def edge_kernel(n, bl_ref, be_ref, br_ref, u1_ref, v_ref, w_ref, stat_ref, unit_ref, mask_ref):
    sources = below_sources(n, bl_ref, be_ref, None, br_ref)
    cross_columns(edge_columns(n), sources, u1_ref, unit_ref, mask_ref, v_ref, w_ref, stat_ref)


def cross_shapes(count, patch):
    return (
        sds((count, patch, 3 * patch), bf16),
        sds((count, patch, 3 * patch), bf16),
        sds((count, patch, 128), f32),
    )


def cross_scratch(n, patch, width):
    return [pltpu.VMEM((n * patch, width), bf16), pltpu.VMEM((n * patch, 1), f32)]


def edge_affinity(bl, be, br, u1):
    n, patch, width = u1.shape
    count = len(edge_columns(n))
    return kernel_call(
        functools.partial(edge_kernel, n),
        cross_shapes(count, patch),
        cross_scratch(n, patch, width),
        cost=4 * count * patch * 3 * patch * width,
    )(bl, be, br, u1)


def place_of(n):
    edge, middle = edge_columns(n), middle_columns(n)
    return {e: (0, i) for i, e in enumerate(edge)} | {e: (1, i) for i, e in enumerate(middle)}


def middle_kernel(
    n,
    be_ref, bm_ref, u1_ref, va_ref, wa_ref, sa_ref, stat_ref, p_ref, got_ref,
    v_ref, w_ref, u0_ref, u2_ref, t_ref, pay_ref,
    unit_ref, mask_ref, sb_ref,
):
    patch = u1_ref.shape[1]
    both = 2 * patch
    half = patch // 2
    sources = below_sources(n, None, be_ref, bm_ref, None)
    cross_columns(middle_columns(n), sources, u1_ref, unit_ref, mask_ref, v_ref, w_ref, sb_ref)
    where = place_of(n)
    stats, ups = (sa_ref, sb_ref), (wa_ref, w_ref)
    eye = identity(patch)
    tail = (n - 2) * half
    got_tail = (n - 2) * half
    pay_ref[...] = jnp.zeros(pay_ref.shape, bf16)
    for e in range(1, n - 1):
        which, i = where[e]
        own_mask = stat_ref[e - 1 : e + 2, patch:, 2:3].reshape(3 * patch, 1)
        absent = 3 * patch - jnp.sum(own_mask, axis=0, keepdims=True)
        shared = stats[which][i, :, 1:2] - FLOOR * absent
        scale = lax.rsqrt(1.0 + stat_ref[e, patch:, 0:1] + stats[which][i, :, 0:1])
        t_own = stat_ref[e, patch:, 2:3] * scale
        t_ref[e, :, 0:1] = t_own
        u0_ref[e] = (t_own * p_ref[1, e]).astype(bf16)
        high = got_ref[got_tail + e : got_tail + e + 1, :patch].astype(f32)
        low = got_ref[got_tail + 32 + e : got_tail + 33 + e, :patch].astype(f32)
        partial = to_sublanes(high + low, eye)
        t_below = stats[which][i, :, 2:3] * lax.rsqrt(1.0 + partial + shared)
        theirs = unpacked(got_ref[(e - 1) * half : e * half, :].astype(f32))
        u2_ref[e] = (t_below * theirs).astype(bf16)
        high, low = pair_of(to_lanes(shared, eye))
        pay_ref[tail + e : tail + e + 1, :patch] = high
        pay_ref[tail + 32 + e : tail + 33 + e, :patch] = low
    for e in range(2, n - 2):
        which, i = where[e]
        source = u0_ref[e - 1 : e + 2].reshape(3 * patch, RANK)
        product = jnp.dot(ups[which][i], source, preferred_element_type=f32)
        pay_ref[(e - 1) * half : e * half, :] = packed(product).astype(bf16)


def middle_affinity(be, bm, u1, va, wa, sa, stat, panel, got):
    n, patch, width = u1.shape
    count = len(middle_columns(n))
    v, w, s = cross_shapes(count, patch)
    return kernel_call(
        functools.partial(middle_kernel, n),
        (
            v,
            w,
            sds((n, patch, RANK), bf16),
            sds((n, patch, RANK), bf16),
            sds((n, patch, 128), f32),
            sds((payload_rows(n, patch), 2 * RANK), bf16),
        ),
        cross_scratch(n, patch, width) + [pltpu.VMEM(s.shape, f32)],
        cost=4 * count * patch * 3 * patch * width,
    )(be, bm, u1, va, wa, sa, stat, panel, got)


def send_products(payload_ref, u_ref, ups, where, low, high, first):
    patch = u_ref.shape[1] // 2
    half = patch // 2
    for e in range(low, high):
        which, i = where[e]
        source = u_ref[e - 1 : e + 2, patch:, :].reshape(3 * patch, RANK)
        product = jnp.dot(ups[which][i], source, preferred_element_type=f32)
        payload_ref[(e - first) * half : (e - first + 1) * half, :] = packed(product).astype(bf16)


def first_kernel(
    n,
    got_ref, stat_ref, t_ref, u0_ref, u2_ref, p_ref, m_ref, va_ref, wa_ref, vb_ref, wb_ref,
    y_ref, u_ref, tt_ref, up_ref, down_ref,
    start_ref,
):
    patch = u0_ref.shape[1]
    half = patch // 2
    both = 2 * patch
    eye = identity(patch)
    where = place_of(n)
    downs, ups = (va_ref, vb_ref), (wa_ref, wb_ref)
    tail = (n - 2) * half
    for e in range(1, n - 1):
        high = got_ref[tail + e : tail + e + 1, :patch].astype(f32)
        low = got_ref[tail + 32 + e : tail + 33 + e, :patch].astype(f32)
        degree = 1.0 + stat_ref[e, :patch, 0:1] + to_sublanes(high + low, eye)
        t_own = stat_ref[e, :patch, 2:3] * lax.rsqrt(degree)
        tt_ref[e, :patch, 0:1] = t_own
        tt_ref[e, patch:, 0:1] = t_ref[e, :, 0:1]
        tt_ref[e, :, 1:2] = stat_ref[e, :, 1:2]
        start_ref[e, :patch, :] = (t_own * p_ref[0, e]).astype(bf16)
        start_ref[e, patch:, :] = u0_ref[e]
    for e in range(2, n - 2):
        which, i = where[e]
        source = start_ref[e - 1 : e + 2].reshape(3 * both, RANK)
        total = jnp.dot(m_ref[e], source, preferred_element_type=f32)
        below = u2_ref[e - 1 : e + 2].reshape(3 * patch, RANK)
        lower = jnp.dot(downs[which][i], below, preferred_element_type=f32)
        upper = unpacked(got_ref[(e - 1) * half : e * half, :].astype(f32))
        total = total + jnp.concatenate([upper, lower], axis=0)
        old = jnp.concatenate([p_ref[0, e], p_ref[1, e]], axis=0)
        scale, diagonal = tt_ref[e, :, 0:1], tt_ref[e, :, 1:2]
        image = old * (1.0 + scale * scale * diagonal) + scale * total
        y_ref[e] = image
        u_ref[e] = (scale * image).astype(bf16)
        up_ref[(e - 2) * half : (e - 1) * half, :] = packed(scale[:patch] * image[:patch]).astype(bf16)
    send_products(down_ref, u_ref, ups, where, 3, n - 3, 3)


def first_iteration(got, stat, t, u0, u2, panel, m, va, wa, vb, wb):
    n, patch, _ = u0.shape
    both = 2 * patch
    half = patch // 2
    return kernel_call(
        functools.partial(first_kernel, n),
        (
            sds((n, both, RANK), f32),
            sds((n, both, RANK), bf16),
            sds((n, both, 128), f32),
            sds(((n - 4) * half, 2 * RANK), bf16),
            sds(((n - 6) * half, 2 * RANK), bf16),
        ),
        [pltpu.VMEM((n, both, RANK), bf16)],
        cost=2 * n * both * 3 * both * RANK,
    )(got, stat, t, u0, u2, panel, m, va, wa, vb, wb)


def local_kernel(low, high, m_ref, u_ref, z_ref):
    both = m_ref.shape[1]
    for e in range(low, high):
        source = u_ref[e - 1 : e + 2].reshape(3 * both, RANK)
        z_ref[e] = jnp.dot(m_ref[e], source, preferred_element_type=f32)


def local_products(low, high, m, u):
    n, both, _ = m.shape
    return kernel_call(
        functools.partial(local_kernel, low, high),
        sds((n, both, RANK), f32),
        cost=2 * n * both * 3 * both * RANK,
    )(m, u)


def joined(e, low, where, downs, z_ref, below_ref, above_ref, y_ref, tt_ref):
    both = y_ref.shape[1]
    patch = both // 2
    half = patch // 2
    which, i = where[e]
    near = [unpacked(below_ref[(c - low + 1) * half : (c - low + 2) * half, :]) for c in (e - 1, e, e + 1)]
    lower = jnp.dot(downs[which][i], jnp.concatenate(near, axis=0), preferred_element_type=f32)
    upper = unpacked(above_ref[(e - low) * half : (e - low + 1) * half, :].astype(f32))
    total = z_ref[e] + jnp.concatenate([upper, lower], axis=0)
    scale, diagonal = tt_ref[e, :, 0:1], tt_ref[e, :, 1:2]
    return y_ref[e] * (1.0 + scale * scale * diagonal) + scale * total, scale


def middle_step_kernel(
    n, low,
    below_ref, above_ref, z_ref, y_ref, tt_ref, va_ref, wa_ref, vb_ref, wb_ref,
    new_ref, u_ref, up_ref, down_ref,
):
    patch = y_ref.shape[1] // 2
    half = patch // 2
    where = place_of(n)
    for e in range(low, n - low):
        image, scale = joined(e, low, where, (va_ref, vb_ref), z_ref, below_ref, above_ref, y_ref, tt_ref)
        new_ref[e] = image
        u_ref[e] = (scale * image).astype(bf16)
        up_ref[(e - low) * half : (e - low + 1) * half, :] = packed(scale[:patch] * image[:patch]).astype(bf16)
    send_products(down_ref, u_ref, (wa_ref, wb_ref), where, low + 1, n - low - 1, low + 1)


def middle_step(low, below, above, z, y, tt, va, wa, vb, wb):
    n, both, _ = y.shape
    half = both // 4
    return kernel_call(
        functools.partial(middle_step_kernel, n, low),
        (
            sds((n, both, RANK), f32),
            sds((n, both, RANK), bf16),
            sds(((n - 2 * low) * half, 2 * RANK), bf16),
            sds(((n - 2 * low - 2) * half, 2 * RANK), bf16),
        ),
        cost=2 * n * both * both * RANK,
    )(below, above, z, y, tt, va, wa, vb, wb)


def last_step_kernel(n, low, below_ref, above_ref, z_ref, y_ref, tt_ref, va_ref, vb_ref, new_ref, gram_ref, side_ref):
    patch = y_ref.shape[1] // 2
    where = place_of(n)
    for e in range(low, n - low):
        image, _ = joined(e, low, where, (va_ref, vb_ref), z_ref, below_ref, above_ref, y_ref, tt_ref)
        new_ref[0, e - low] = image[:patch]
        new_ref[1, e - low] = image[patch:]
        side_ref[(e - low) * patch : (e - low + 1) * patch, :] = jnp.concatenate(
            [image[:patch], image[patch:]], axis=1
        )
    side = side_ref[...]
    gram = lax.dot_general(side, side, ATB, precision=lax.Precision.HIGHEST, preferred_element_type=f32)
    gram_ref[...] = packed(gram[:RANK, :RANK] + gram[RANK:, RANK:])


def last_step(low, below, above, z, y, tt, va, vb):
    n, both, _ = y.shape
    patch = both // 2
    cols = n - 2 * low
    return kernel_call(
        functools.partial(last_step_kernel, n, low),
        (sds((2, cols, patch, RANK), f32), sds((RANK // 2, 2 * RANK), f32)),
        [pltpu.VMEM((cols * patch, 2 * RANK), f32)],
        cost=2 * n * both * both * RANK,
    )(below, above, z, y, tt, va, vb)


def inverse_factor(gram):
    size = gram.shape[0]
    step = 4
    row = iota((size, 2 * size), 0)
    lane = iota((size, 2 * size), 1)
    table = jnp.concatenate([gram, identity(size).astype(f32)], axis=1)
    for k in range(0, size, step):
        cols = [jnp.broadcast_to(table[:, k + i : k + i + 1], table.shape) for i in range(step)]
        lines = [table[k + i : k + i + 1, :] for i in range(step)]
        for i in range(step):
            inverse = 1.0 / cols[i][k + i : k + i + 1, :]
            for j in range(i + 1, step):
                lines[j] = lines[j] - lines[i] * (cols[i][k + j : k + j + 1, :] * inverse)
                cols[j] = cols[j] - cols[i] * (cols[j][k + i : k + i + 1, :] * inverse)
            table = table - jnp.where(row > k + i, cols[i], 0.0) * (lines[i] * inverse)
    pivots = jnp.sum(jnp.where(row == lane, table, 0.0), axis=1, keepdims=True)
    return table[:, size:] * lax.rsqrt(pivots)


def finish_kernel(factor, count, *refs):
    parts, y_ref, out_ref = refs[:count], refs[count], refs[count + 1]
    total = parts[0][...]
    for part in parts[1:]:
        total = total + part[...]
    inverse = factor * inverse_factor(unpacked(total))
    zero = jnp.zeros_like(inverse)
    wide = jnp.concatenate(
        [jnp.concatenate([inverse, zero], axis=1), jnp.concatenate([zero, inverse], axis=1)], axis=0
    )
    for q in range(y_ref.shape[1] // (2 * RANK)):
        span = slice(q * 2 * RANK, (q + 1) * 2 * RANK)
        out_ref[:, span] = lax.dot_general(
            y_ref[:, span], wide, ABT, precision=lax.Precision.HIGHEST, preferred_element_type=f32
        )


def finish(factor, parts, y):
    return kernel_call(
        functools.partial(finish_kernel, factor, len(parts)),
        sds(y.shape, f32),
        cost=2 * y.shape[0] * y.shape[1] * RANK,
    )(*parts, y)


def exchange_stages():
    stages = []
    for axis in ("col", "row"):
        size = lax.axis_size(axis)
        bit = 1
        if axis == "col":
            stages.append((axis, size, [1]))
            bit = 2
        while bit < size:
            if 2 * bit < size:
                stages.append((axis, size, [bit, 2 * bit, 3 * bit]))
                bit *= 4
            else:
                stages.append((axis, size, [bit]))
                bit *= 2
    return stages


def summed_parts(gram):
    stages = exchange_stages()
    for place, (axis, size, partners) in enumerate(stages):
        parts = [gram] + [
            lax.ppermute(gram, axis, [(i, i ^ p) for i in range(size)]) for p in partners
        ]
        if place == len(stages) - 1:
            return parts
        gram = parts[0]
        for part in parts[1:]:
            gram = gram + part


def passed_along(shard, axis, by):
    count = lax.axis_size(axis)
    pairs = [(i, i + by) for i in range(count) if 0 <= i + by < count]
    return lax.ppermute(shard, axis, pairs)


def local(features, tissue, probe):
    tile_rows, tile_cols, patches, width = features.shape
    first = iota(features.shape, 3) == 0
    marked = jnp.where(first & (features == 0), jnp.asarray(TINY, bf16), features)
    marked = jnp.where(tissue[..., None] != 0, marked, jnp.zeros((), bf16))
    edges = jnp.concatenate([marked[0, :GHOST], marked[0, -GHOST:]], axis=0)
    below_edges = passed_along(edges, "row", -1)
    from_left = passed_along(marked[:, -GHOST:], "col", 1)
    from_right = passed_along(marked[:, :GHOST], "col", -1)
    below_middle = passed_along(marked[0, GHOST:-GHOST], "row", -1)
    probe_left = passed_along(probe[:, -GHOST:], "col", 1)
    probe_right = passed_along(probe[:, :GHOST], "col", -1)
    panel = jnp.concatenate([probe_left, probe, probe_right], axis=1)
    n = panel.shape[1]
    panel = panel.reshape(tile_rows, n, patches, RANK)

    m, u1, stat, payload = own_affinity(marked, from_left, from_right, panel)
    got_below = passed_along(payload, "row", -1)
    below_left = passed_along(below_edges[GHOST:], "col", 1)
    below_right = passed_along(below_edges[:GHOST], "col", -1)
    va, wa, sa = edge_affinity(below_left, below_edges, below_right, u1)
    vb, wb, u0, u2, t, payload = middle_affinity(
        below_edges, below_middle, u1, va, wa, sa, stat, panel, got_below
    )
    got_above = passed_along(payload, "row", 1)
    y, u, tt, up, down = first_iteration(got_above, stat, t, u0, u2, panel, m, va, wa, vb, wb)
    below, above = passed_along(up, "row", -1), passed_along(down, "row", 1)
    z = local_products(3, n - 3, m, u)
    y, u, up, down = middle_step(3, below, above, z, y, tt, va, wa, vb, wb)
    below, above = passed_along(up, "row", -1), passed_along(down, "row", 1)
    z = local_products(4, n - 4, m, u)
    y, gram = last_step(4, below, above, z, y, tt, va, vb)

    parts = summed_parts(gram)
    flat = y.reshape(tile_rows * tile_cols, patches * RANK)
    total = tile_rows * lax.axis_size("row") * tile_cols * lax.axis_size("col") * patches
    out = finish(math.sqrt(float(total)), parts, flat)
    return out.reshape(tile_rows, tile_cols, patches * RANK)


def solution(mesh):
    placed = (P("row", "col", None, None), P("row", "col", None), P("row", "col", None))
    return jax.shard_map(
        local, mesh=mesh, in_specs=placed, out_specs=P("row", "col", None), check_vma=False
    )
```

```python
import functools
import math

import jax
import jax.numpy as jnp
from jax import lax
from jax.experimental import pallas as pl
from jax.experimental.pallas import tpu as pltpu
from jax.sharding import PartitionSpec as P

RANK = 64
ITERS = 3
AFFINITY_TEMP = 4.0

GHOST = ITERS + 1
EDGE = 5
TINY = 1e-30
VMEM_BYTES = 16 * 1024 * 1024
FLOOR = math.exp(-AFFINITY_TEMP)
ABT = (((1,), (1,)), ((), ()))
ATB = (((0,), (0,)), ((), ()))

f32 = jnp.float32
bf16 = jnp.bfloat16


def kernel_call(body, out_shape, scratch=(), cost=0):
    return pl.pallas_call(
        body,
        out_shape=out_shape,
        scratch_shapes=list(scratch),
        compiler_params=pltpu.CompilerParams(vmem_limit_bytes=VMEM_BYTES),
        cost_estimate=pl.CostEstimate(flops=cost, bytes_accessed=1 << 20, transcendentals=0),
    )


def sds(shape, dtype):
    return jax.ShapeDtypeStruct(shape, dtype)


def iota(shape, dim):
    return lax.broadcasted_iota(jnp.int32, shape, dim)


def identity(n):
    return iota((n, n), 0) == iota((n, n), 1)


def unit_and_mask(block):
    values = block.astype(f32)
    scaled = values * lax.rsqrt(jnp.sum(values * values, axis=-1, keepdims=True) + 1e-06)
    return scaled.astype(bf16), (values[:, :1] != 0.0).astype(f32)


def affinity_of(left, right):
    scores = lax.dot_general(left, right, ABT, preferred_element_type=f32)
    return jnp.exp(AFFINITY_TEMP * scores - AFFINITY_TEMP)


def at_lane(lane, e, column, table):
    return jnp.where(lane == e, column, table)


def absent_near(mask, width):
    count = jnp.sum(mask, axis=0, keepdims=True)
    return width - (pltpu.roll(count, 1, 1) + count + pltpu.roll(count, 127, 1))


def packed(block):
    half = block.shape[0] // 2
    return jnp.concatenate([block[:half], block[half:]], axis=1)


def unpacked(block):
    return jnp.concatenate([block[:, :RANK], block[:, RANK:]], axis=0)


def panel_at(panel, row, e):
    left_ref, own_ref, right_ref = panel
    own = own_ref.shape[1]
    if GHOST <= e < GHOST + own:
        return own_ref[row, e - GHOST]
    both = (left_ref[row, e] if e < GHOST else right_ref[row, e - GHOST - own]).astype(f32)
    return both[:, :RANK] + both[:, RANK:]


def pair_of(values):
    high = values.astype(bf16)
    return high, (values - high.astype(f32)).astype(bf16)


def by_sublane(tissue):
    mask = (tissue != 0).astype(bf16)
    return lax.dot_general(mask, identity(mask.shape[0]).astype(bf16), ATB, preferred_element_type=f32)


def marked(tile, column):
    zero = (iota(tile.shape, 1) == 0) & (tile == 0)
    return jnp.where(zero, jnp.asarray(TINY, bf16), tile) * column.astype(bf16)


def mark_row_kernel(x_ref, tissue_ref, edge_ref, middle_ref, tile_ref, mask_ref, sem_ref):
    cols = x_ref.shape[1]
    copies = [pltpu.make_async_copy(x_ref.at[0, c], tile_ref.at[c], sem_ref.at[c]) for c in range(cols)]
    mask_copy = pltpu.make_async_copy(tissue_ref.at[0], mask_ref, sem_ref.at[cols])
    mask_copy.start()
    for copy in copies:
        copy.start()
    mask_copy.wait()
    mask = by_sublane(mask_ref[...])
    for c in range(cols):
        copies[c].wait()
        tile = marked(tile_ref[c], mask[:, c : c + 1])
        if c < EDGE:
            edge_ref[c] = tile
        elif c < cols - EDGE:
            middle_ref[c - EDGE] = tile
        else:
            edge_ref[c - cols + 2 * EDGE] = tile


def mark_row(x, tissue):
    rows, cols, patch, width = x.shape
    vmem = pl.BlockSpec(memory_space=pltpu.VMEM)
    hbm = pl.BlockSpec(memory_space=pltpu.HBM)
    return pl.pallas_call(
        mark_row_kernel,
        in_specs=[hbm, hbm],
        out_specs=[vmem] * 2,
        out_shape=(
            sds((2 * EDGE, patch, width), bf16),
            sds((cols - 2 * EDGE, patch, width), bf16),
        ),
        scratch_shapes=[
            pltpu.VMEM((cols, patch, width), bf16),
            pltpu.VMEM((cols, patch), jnp.int32),
            pltpu.SemaphoreType.DMA((cols + 1,)),
        ],
        compiler_params=pltpu.CompilerParams(vmem_limit_bytes=VMEM_BYTES),
    )(pltpu.with_memory_space_constraint(x, pltpu.HBM), pltpu.with_memory_space_constraint(tissue, pltpu.HBM))


def mark_ends_kernel(first_ref, last_ref, tissue_ref, after_ref, left_ref, right_ref):
    rows, count, patch, width = first_ref.shape
    cols = tissue_ref.shape[1]
    for row in range(rows):
        mask = by_sublane(tissue_ref[row])
        for c in range(count):
            left_ref[row, c] = marked(first_ref[row, c], mask[:, c : c + 1])
            at = cols - count + c
            right_ref[row, c] = marked(last_ref[row, c], mask[:, at : at + 1])


def mark_ends(x, tissue, after):
    rows, cols, patch, width = x.shape
    shape = (rows, GHOST, patch, width)
    return pl.pallas_call(
        mark_ends_kernel,
        grid=(1,),
        in_specs=[
            pl.BlockSpec(shape, lambda i: (0, 0, 0, 0)),
            pl.BlockSpec(shape, lambda i: (0, cols // GHOST - 1, 0, 0)),
            pl.BlockSpec((rows, cols, patch), lambda i: (0, 0, 0)),
            pl.BlockSpec(memory_space=pl.ANY),
        ],
        out_specs=[pl.BlockSpec(shape, lambda i: (0, 0, 0, 0))] * 2,
        out_shape=(sds(shape, bf16), sds(shape, bf16)),
        compiler_params=pltpu.CompilerParams(vmem_limit_bytes=VMEM_BYTES),
    )(x, x, tissue, after)


def units_kernel(n, x_ref, tissue_ref, probe_ref, after_ref, unit0_ref, unit1_ref, left_ref, right_ref):
    rows, cols, patch, width = x_ref.shape
    for row, unit_ref in ((0, unit0_ref), (1, unit1_ref)):
        mask = by_sublane(tissue_ref[row]).astype(bf16)
        for c in range(cols):
            unit, _ = unit_and_mask(x_ref[row, c])
            at = (GHOST + c) * patch
            unit_ref[at : at + patch, :] = unit * mask[:, c : c + 1]
        for c in range(GHOST):
            left_ref[row, c] = jnp.concatenate(pair_of(probe_ref[row, c]), axis=1)
            right_ref[row, c] = jnp.concatenate(pair_of(probe_ref[row, cols - GHOST + c]), axis=1)


def own_units(x, tissue, probe, after):
    rows, cols, patch, width = x.shape
    n = cols + 2 * GHOST
    vmem = pl.BlockSpec(memory_space=pltpu.VMEM)
    side = sds((rows, GHOST, patch, 2 * RANK), bf16)
    unit = sds((n * patch, width), bf16)
    return pl.pallas_call(
        functools.partial(units_kernel, n),
        in_specs=[vmem, vmem, vmem, pl.BlockSpec(memory_space=pl.ANY)],
        out_specs=[vmem] * 4,
        out_shape=(unit, unit, side, side),
        compiler_params=pltpu.CompilerParams(vmem_limit_bytes=VMEM_BYTES),
    )(x, tissue, probe, after)


def bands(ranges, patch, unit0_ref, unit1_ref, m_ref, degree, diagonal):
    both = 2 * patch
    shape = (both, 3 * both)
    patch_of = iota(shape, 0)
    own = iota(shape, 1) == jnp.where(patch_of < patch, patch_of + patch, patch_of + 3 * patch)
    lane = iota((both, 128), 1)

    def band(e, carry):
        degree, diagonal = carry
        around = pl.ds(pl.multiple_of((e - 1) * patch, patch), 3 * patch)
        here = pl.ds(pl.multiple_of(e * patch, patch), patch)
        left = jnp.concatenate([unit0_ref[here, :], unit1_ref[here, :]], axis=0)
        right = jnp.concatenate([unit0_ref[around, :], unit1_ref[around, :]], axis=0)
        weights = affinity_of(left, right)
        others = jnp.where(own, 0.0, weights)
        m_ref[e] = others.astype(bf16)
        itself = jnp.sum(weights - others, axis=1, keepdims=True)
        degree = at_lane(lane, e, jnp.sum(weights, axis=1, keepdims=True), degree)
        diagonal = at_lane(lane, e, itself, diagonal)
        return degree, diagonal

    carry = (degree, diagonal)
    for low, high in ranges:
        carry = lax.fori_loop(low, high, band, carry)
    return carry


def inside_kernel(n, unit0_ref, unit1_ref, m_ref, sum_ref):
    patch = m_ref.shape[1] // 2
    empty = jnp.zeros((2 * patch, 128), f32)
    sum_ref[0], sum_ref[1] = bands([(GHOST + 1, n - GHOST - 1)], patch, unit0_ref, unit1_ref, m_ref, empty, empty)


def inside_affinity(unit0, unit1, patch):
    n = unit0.shape[0] // patch
    both = 2 * patch
    return pl.pallas_call(
        functools.partial(inside_kernel, n),
        out_shape=(sds((n, both, 3 * both), bf16), sds((2, both, 128), f32)),
        compiler_params=pltpu.CompilerParams(vmem_limit_bytes=VMEM_BYTES),
    )(unit0, unit1)


def outside_kernel(
    n,
    start0_ref, start1_ref, some_ref, xl_ref, xr_ref, tissue_ref, sum_ref, pl_ref, p_ref, pr_ref,
    unit0_ref, unit1_ref, m_ref, stat_ref, pay_ref,
):
    rows, count, patch, width = xl_ref.shape
    cols = n - 2 * count
    both = rows * patch
    lane = iota((patch, 128), 1)

    masks = []
    for row, unit_ref in ((0, unit0_ref), (1, unit1_ref)):
        own_mask = by_sublane(tissue_ref[row])
        mask = jnp.zeros((patch, 128), f32)
        for e in range(n):
            if e < count:
                unit, column = unit_and_mask(xl_ref[row, e])
            elif e < count + cols:
                unit, column = None, own_mask[:, e - count : e - count + 1]
            else:
                unit, column = unit_and_mask(xr_ref[row, e - count - cols])
            mask = at_lane(lane, e, column, mask)
            if unit is not None:
                unit_ref[e * patch : (e + 1) * patch, :] = unit
        masks.append(mask)
    mask = jnp.concatenate(masks, axis=0)
    ranges = [(1, GHOST + 1), (n - GHOST - 1, n - 1)]
    degree, diagonal = bands(ranges, patch, unit0_ref, unit1_ref, m_ref, sum_ref[0], sum_ref[1])
    degree = degree - FLOOR * absent_near(mask, 3 * both)
    stat_ref[0] = degree
    stat_ref[1] = diagonal
    stat_ref[2] = mask
    half = patch // 2
    tail = (n - 2) * half
    for e in range(1, n - 1):
        pay_ref[(e - 1) * half : e * half, :] = packed(panel_at((pl_ref, p_ref, pr_ref), 0, e)).astype(bf16)
    pay_ref[tail : tail + patch, :], pay_ref[tail + patch :, :] = pair_of(degree[:patch])


def payload_rows(columns, patch):
    return columns * patch // 2 + 2 * patch


def outside_affinity(unit0, unit1, m, xl, xr, tissue, sums, panel):
    n, both, _ = m.shape
    payload = sds((payload_rows(n - 2, both // 2), 2 * RANK), bf16)
    unit = sds(unit0.shape, bf16)
    return pl.pallas_call(
        functools.partial(outside_kernel, n),
        out_shape=(unit, unit, sds(m.shape, bf16), sds((3, both, 128), f32), payload),
        input_output_aliases={0: 0, 1: 1, 2: 2},
        compiler_params=pltpu.CompilerParams(vmem_limit_bytes=VMEM_BYTES),
    )(unit0, unit1, m, xl, xr, tissue, sums, *panel)


def cut_kernel(be_ref, after_ref, left_ref, right_ref):
    left_ref[...] = be_ref[:GHOST]
    right_ref[...] = be_ref[be_ref.shape[0] - GHOST :]


def cut(be, after):
    vmem = pl.BlockSpec(memory_space=pltpu.VMEM)
    side = sds((GHOST,) + be.shape[1:], be.dtype)
    return pl.pallas_call(
        cut_kernel,
        in_specs=[vmem, pl.BlockSpec(memory_space=pl.ANY)],
        out_specs=[vmem] * 2,
        out_shape=(side, side),
        compiler_params=pltpu.CompilerParams(vmem_limit_bytes=VMEM_BYTES),
    )(be, after)


def cross_columns(patch, columns, sources, own_ref, unit_ref, v_ref, w_ref, sums):
    lane = iota((patch, 128), 1)
    down_sum, up_sum, mask = sums
    needed = sorted({c for e in columns for c in (e - 1, e, e + 1)})
    for c in needed:
        ref, index = sources[c]
        unit, column = unit_and_mask(ref[index])
        unit_ref[c * patch : (c + 1) * patch, :] = unit
        mask = at_lane(lane, c, column, mask)
    for place, e in enumerate(columns):
        around = slice((e - 1) * patch, (e + 2) * patch)
        here = slice(e * patch, (e + 1) * patch)
        down = affinity_of(own_ref[here, :], unit_ref[around, :])
        up = affinity_of(unit_ref[here, :], own_ref[around, :])
        v_ref[place] = down.astype(bf16)
        w_ref[place] = up.astype(bf16)
        down_sum = at_lane(lane, e, jnp.sum(down, axis=1, keepdims=True), down_sum)
        up_sum = at_lane(lane, e, jnp.sum(up, axis=1, keepdims=True), up_sum)
    return down_sum, up_sum, mask


def edge_columns(n):
    return list(range(1, GHOST + EDGE - 1)) + list(range(n - GHOST - EDGE + 1, n - 1))


def middle_columns(n):
    return list(range(GHOST + EDGE - 1, n - GHOST - EDGE + 1))


def inner(columns, low, high):
    return [e for e in columns if low <= e < high and e - 1 in columns and e + 1 in columns]


def place_of(n):
    edge, middle = edge_columns(n), middle_columns(n)
    return {e: (0, i) for i, e in enumerate(edge)} | {e: (1, i) for i, e in enumerate(middle)}


def below_sources(n, bl_ref, be_ref, bm_ref, br_ref):
    sources = {}
    for c in range(n):
        if c < GHOST:
            sources[c] = (bl_ref, c)
        elif c < GHOST + EDGE:
            sources[c] = (be_ref, c - GHOST)
        elif c < n - GHOST - EDGE:
            sources[c] = (bm_ref, c - GHOST - EDGE)
        elif c < n - GHOST:
            sources[c] = (be_ref, c - (n - GHOST) + 2 * EDGE)
        else:
            sources[c] = (br_ref, c - (n - GHOST))
    return sources


def scale_of(stat_ref, sums):
    down_sum, _, mask = sums
    patch = mask.shape[0]
    degree = 1.0 + stat_ref[0, patch:] + down_sum - FLOOR * absent_near(mask, 3 * patch)
    return stat_ref[2, patch:] * lax.rsqrt(degree)


def products(columns, where, ups, u_ref, pay_ref, first):
    half = u_ref.shape[1] // 2
    for e in columns:
        which, i = where[e]
        source = u_ref[e - 1 : e + 2].reshape(3 * u_ref.shape[1], RANK)
        product = jnp.dot(ups[which][i], source, preferred_element_type=f32)
        pay_ref[(e - first) * half : (e - first + 1) * half, :] = packed(product).astype(bf16)


def edge_kernel(n, bl_ref, be_ref, br_ref, u1_ref, stat_ref, pl_ref, p_ref, pr_ref, v_ref, w_ref, sum_ref, u0_ref, pay_ref, unit_ref):
    patch = be_ref.shape[1]
    sources = below_sources(n, bl_ref, be_ref, None, br_ref)
    columns = edge_columns(n)
    empty = jnp.zeros((patch, 128), f32)
    sums = cross_columns(patch, columns, sources, u1_ref, unit_ref, v_ref, w_ref, (empty, empty, empty))
    for i in range(3):
        sum_ref[i] = sums[i]
    scale = scale_of(stat_ref, sums)
    for e in columns:
        u0_ref[e] = (scale[:, e : e + 1] * panel_at((pl_ref, p_ref, pr_ref), 1, e)).astype(bf16)
    products(inner(columns, 2, n - 2), place_of(n), (w_ref, None), u0_ref, pay_ref, 2)


def edge_affinity(bl, be, br, u1, stat, panel):
    _, patch, width = be.shape
    n = u1.shape[0] // patch
    count = len(edge_columns(n))
    return kernel_call(
        functools.partial(edge_kernel, n),
        (
            sds((count, patch, 3 * patch), bf16),
            sds((count, patch, 3 * patch), bf16),
            sds((3, patch, 128), f32),
            sds((n, patch, RANK), bf16),
            sds(((n - 4) * patch // 2, 2 * RANK), bf16),
        ),
        [pltpu.VMEM((n * patch, width), bf16)],
        cost=4 * count * patch * 3 * patch * width,
    )(bl, be, br, u1, stat, *panel)


def middle_kernel(
    n,
    be_ref, bm_ref, u1_ref, stat_ref, pl_ref, p_ref, pr_ref, sa_ref, ua_ref, wa_ref, paya_ref,
    v_ref, w_ref, sum_ref, u0_ref, t_ref, pay_ref,
    unit_ref,
):
    patch = be_ref.shape[1]
    half = patch // 2
    sources = below_sources(n, None, be_ref, bm_ref, None)
    columns = middle_columns(n)
    before = tuple(sa_ref[i] for i in range(3))
    sums = cross_columns(patch, columns, sources, u1_ref, unit_ref, v_ref, w_ref, before)
    scale = scale_of(stat_ref, sums)
    t_ref[...] = scale
    shared = sums[1] - FLOOR * absent_near(stat_ref[2, patch:], 3 * patch)
    sum_ref[0] = shared
    sum_ref[1] = sums[2]
    edges = edge_columns(n)
    for e in edges:
        u0_ref[e] = ua_ref[e]
    for e in columns:
        u0_ref[e] = (scale[:, e : e + 1] * panel_at((pl_ref, p_ref, pr_ref), 1, e)).astype(bf16)
    done = inner(edges, 2, n - 2)
    for e in done:
        pay_ref[(e - 2) * half : (e - 1) * half, :] = paya_ref[(e - 2) * half : (e - 1) * half, :]
    products([e for e in range(2, n - 2) if e not in done], place_of(n), (wa_ref, w_ref), u0_ref, pay_ref, 2)
    tail = (n - 4) * half
    pay_ref[tail : tail + patch, :], pay_ref[tail + patch :, :] = pair_of(shared)


def middle_affinity(be, bm, u1, stat, panel, sa, ua, wa, paya):
    _, patch, width = be.shape
    n = u1.shape[0] // patch
    count = len(middle_columns(n))
    return kernel_call(
        functools.partial(middle_kernel, n),
        (
            sds((count, patch, 3 * patch), bf16),
            sds((count, patch, 3 * patch), bf16),
            sds((2, patch, 128), f32),
            sds((n, patch, RANK), bf16),
            sds((patch, 128), f32),
            sds((payload_rows(n - 4, patch), 2 * RANK), bf16),
        ),
        [pltpu.VMEM((n * patch, width), bf16)],
        cost=4 * count * patch * 3 * patch * width,
    )(be, bm, u1, stat, *panel, sa, ua, wa, paya)


def before_first_kernel(n, got_ref, sum_ref, u0_ref, m_ref, va_ref, vb_ref, z_ref, u2_ref):
    patch = u0_ref.shape[1]
    half = patch // 2
    both = 2 * patch
    where = place_of(n)
    tail = (n - 2) * half
    partial = got_ref[tail : tail + patch, :].astype(f32) + got_ref[tail + patch :, :].astype(f32)
    scale = sum_ref[1] * lax.rsqrt(1.0 + partial + sum_ref[0])
    for e in range(1, n - 1):
        theirs = unpacked(got_ref[(e - 1) * half : e * half, :].astype(f32))
        u2_ref[e] = (scale[:, e : e + 1] * theirs).astype(bf16)
    for e in range(2, n - 2):
        which, i = where[e]
        own = u0_ref[e - 1 : e + 2].reshape(3 * patch, RANK)
        total = jnp.dot(m_ref[e, :, 3 * patch :], own, preferred_element_type=f32)
        below = u2_ref[e - 1 : e + 2].reshape(3 * patch, RANK)
        lower = jnp.dot((va_ref, vb_ref)[which][i], below, preferred_element_type=f32)
        z_ref[e, :patch] = total[:patch]
        z_ref[e, patch:] = total[patch:] + lower


def before_first(got, sums, u0, m, va, vb):
    n, patch, _ = u0.shape
    return kernel_call(
        functools.partial(before_first_kernel, n),
        sds((n, 2 * patch, RANK), f32),
        [pltpu.VMEM((n, patch, RANK), bf16)],
        cost=2 * n * 2 * patch * 3 * patch * RANK,
    )(got, sums, u0, m, va, vb)


def first_kernel(
    n,
    got_ref, stat_ref, t_ref, z_ref, pl_ref, p_ref, pr_ref, m_ref, wa_ref, wb_ref,
    y_ref, u_ref, tt_ref, up_ref, down_ref,
    start_ref,
):
    panel = (pl_ref, p_ref, pr_ref)
    patch = t_ref.shape[0]
    half = patch // 2
    tail = (n - 4) * half
    partial = got_ref[tail : tail + patch, :].astype(f32) + got_ref[tail + patch :, :].astype(f32)
    upper_scale = stat_ref[2, :patch] * lax.rsqrt(1.0 + stat_ref[0, :patch] + partial)
    scale = jnp.concatenate([upper_scale, t_ref[...]], axis=0)
    gain = 1.0 + scale * scale * stat_ref[1]
    tt_ref[0] = scale
    tt_ref[1] = gain
    for e in range(1, n - 1):
        start_ref[e] = (upper_scale[:, e : e + 1] * panel_at(panel, 0, e)).astype(bf16)
    for e in range(2, n - 2):
        own = start_ref[e - 1 : e + 2].reshape(3 * patch, RANK)
        total = z_ref[e] + jnp.dot(m_ref[e, :, : 3 * patch], own, preferred_element_type=f32)
        upper = unpacked(got_ref[(e - 2) * half : (e - 1) * half, :].astype(f32))
        for row in range(2):
            span = slice(row * patch, (row + 1) * patch)
            piece = total[span] + upper if row == 0 else total[span]
            t = scale[span, e : e + 1]
            image = panel_at(panel, row, e) * gain[span, e : e + 1] + t * piece
            y_ref[row, e] = image
            scaled = t * image
            u_ref[row, e] = scaled.astype(bf16)
            if row == 0:
                up_ref[(e - 2) * half : (e - 1) * half, :] = packed(scaled).astype(bf16)
    products(range(3, n - 3), place_of(n), (wa_ref, wb_ref), u_ref.at[1], down_ref, 3)


def first_iteration(got, stat, t, z, panel, m, wa, wb):
    n, both, _ = z.shape
    patch = both // 2
    half = patch // 2
    return kernel_call(
        functools.partial(first_kernel, n),
        (
            sds((2, n, patch, RANK), f32),
            sds((2, n, patch, RANK), bf16),
            sds((2, both, 128), f32),
            sds(((n - 4) * half, 2 * RANK), bf16),
            sds(((n - 6) * half, 2 * RANK), bf16),
        ),
        [pltpu.VMEM((n, patch, RANK), bf16)],
        cost=2 * n * both * 3 * patch * RANK,
    )(got, stat, t, z, *panel, m, wa, wb)


def local_kernel(low, high, m_ref, u_ref, z_ref):
    patch = u_ref.shape[2]
    for e in range(low, high):
        upper = u_ref[0, e - 1 : e + 2].reshape(3 * patch, RANK)
        lower = u_ref[1, e - 1 : e + 2].reshape(3 * patch, RANK)
        z_ref[e] = jnp.dot(m_ref[e], jnp.concatenate([upper, lower], axis=0), preferred_element_type=f32)


def local_products(low, high, m, u):
    n, both, _ = m.shape
    return kernel_call(
        functools.partial(local_kernel, low, high),
        sds((n, both, RANK), f32),
        cost=2 * n * both * 3 * both * RANK,
    )(m, u)


def joined(e, low, where, downs, near, z_ref, above_ref, y_ref, scale, gain):
    patch = y_ref.shape[2]
    half = patch // 2
    which, i = where[e]
    below = jnp.concatenate([near[e - 1], near[e], near[e + 1]], axis=0)
    lower = z_ref[e, patch:] + jnp.dot(downs[which][i], below, preferred_element_type=f32)
    upper = z_ref[e, :patch] + unpacked(above_ref[(e - low) * half : (e - low + 1) * half, :].astype(f32))
    images = []
    for row, piece in ((0, upper), (1, lower)):
        span = slice(row * patch, (row + 1) * patch)
        images.append(y_ref[row, e] * gain[span, e : e + 1] + scale[span, e : e + 1] * piece)
    return images


def halo(n, low, half, below_ref):
    return {
        e: unpacked(below_ref[(e - low + 1) * half : (e - low + 2) * half, :]) for e in range(low - 1, n - low + 1)
    }


def middle_step_kernel(
    n, low,
    below_ref, above_ref, z_ref, y_ref, tt_ref, va_ref, wa_ref, vb_ref, wb_ref,
    new_ref, u_ref, up_ref, down_ref,
):
    patch = y_ref.shape[2]
    half = patch // 2
    where = place_of(n)
    scale, gain = tt_ref[0], tt_ref[1]
    near = halo(n, low, half, below_ref)
    for e in range(low, n - low):
        images = joined(e, low, where, (va_ref, vb_ref), near, z_ref, above_ref, y_ref, scale, gain)
        for row in range(2):
            new_ref[row, e] = images[row]
            scaled = scale[row * patch : (row + 1) * patch, e : e + 1] * images[row]
            u_ref[row, e] = scaled.astype(bf16)
            if row == 0:
                up_ref[(e - low) * half : (e - low + 1) * half, :] = packed(scaled).astype(bf16)
    products(range(low + 1, n - low - 1), where, (wa_ref, wb_ref), u_ref.at[1], down_ref, low + 1)


def middle_step(low, below, above, z, y, tt, va, wa, vb, wb):
    _, n, patch, _ = y.shape
    half = patch // 2
    return kernel_call(
        functools.partial(middle_step_kernel, n, low),
        (
            sds((2, n, patch, RANK), f32),
            sds((2, n, patch, RANK), bf16),
            sds(((n - 2 * low) * half, 2 * RANK), bf16),
            sds(((n - 2 * low - 2) * half, 2 * RANK), bf16),
        ),
        cost=8 * n * patch * patch * RANK,
    )(below, above, z, y, tt, va, wa, vb, wb)


def last_step_kernel(n, low, below_ref, above_ref, z_ref, y_ref, tt_ref, va_ref, vb_ref, new_ref, gram_ref, side_ref):
    patch = y_ref.shape[2]
    where = place_of(n)
    scale, gain = tt_ref[0], tt_ref[1]
    near = halo(n, low, patch // 2, below_ref)
    wide = 2 * RANK
    for e in range(low, n - low):
        images = joined(e, low, where, (va_ref, vb_ref), near, z_ref, above_ref, y_ref, scale, gain)
        for row in range(2):
            new_ref[row, e - low] = images[row]
        span = slice((e - low) * patch, (e - low + 1) * patch)
        side_ref[span, :wide], side_ref[span, wide:] = pair_of(jnp.concatenate(images, axis=1))
    side = side_ref[...]
    gram = lax.dot_general(side, side, ATB, preferred_element_type=f32)
    gram = gram[:wide] + gram[wide:]
    gram = gram[:, :wide] + gram[:, wide:]
    gram_ref[...] = packed(gram[:RANK, :RANK] + gram[RANK:, RANK:])


def last_step(low, below, above, z, y, tt, va, vb):
    _, n, patch, _ = y.shape
    cols = n - 2 * low
    return kernel_call(
        functools.partial(last_step_kernel, n, low),
        (sds((2, cols, patch, RANK), f32), sds((RANK // 2, 2 * RANK), f32)),
        [pltpu.VMEM((cols * patch, 4 * RANK), bf16)],
        cost=8 * n * patch * patch * RANK,
    )(below, above, z, y, tt, va, vb)


def inverse_factor(gram):
    size = gram.shape[0]
    step = 4
    row = iota((size, 2 * size), 0)
    lane = iota((size, 2 * size), 1)
    table = jnp.concatenate([gram, identity(size).astype(f32)], axis=1)
    for k in range(0, size, step):
        cols = [jnp.broadcast_to(table[:, k + i : k + i + 1], table.shape) for i in range(step)]
        lines = [table[k + i : k + i + 1, :] for i in range(step)]
        for i in range(step):
            inverse = 1.0 / cols[i][k + i : k + i + 1, :]
            for j in range(i + 1, step):
                lines[j] = lines[j] - lines[i] * (cols[i][k + j : k + j + 1, :] * inverse)
                cols[j] = cols[j] - cols[i] * (cols[j][k + i : k + i + 1, :] * inverse)
            table = table - jnp.where(row > k + i, cols[i], 0.0) * (lines[i] * inverse)
    pivots = jnp.sum(jnp.where(row == lane, table, 0.0), axis=1, keepdims=True)
    return table[:, size:] * lax.rsqrt(pivots)


def finish_kernel(factor, count, *refs):
    parts, y_ref, out_ref = refs[:count], refs[count], refs[count + 1]
    total = parts[0][...]
    for part in parts[1:]:
        total = total + part[...]
    inverse = factor * inverse_factor(unpacked(total))
    zero = jnp.zeros_like(inverse)
    both = jnp.concatenate(
        [jnp.concatenate([inverse, zero], axis=1), jnp.concatenate([zero, inverse], axis=1)], axis=0
    )
    wide = 2 * RANK
    tiles, width = y_ref.shape
    pieces = [y_ref[:, q * wide : (q + 1) * wide] for q in range(width // wide)]
    y_high, y_low = pair_of(jnp.concatenate(pieces, axis=0))
    t_high, t_low = pair_of(both)

    def times(a, b):
        return lax.dot_general(a, b, ABT, preferred_element_type=f32)

    out = times(y_high, t_high) + (times(y_low, t_high) + times(y_high, t_low))
    for q in range(width // wide):
        out_ref[:, q * wide : (q + 1) * wide] = out[q * tiles : (q + 1) * tiles]


def finish(factor, parts, y):
    return kernel_call(
        functools.partial(finish_kernel, factor, len(parts)),
        sds(y.shape, f32),
        cost=2 * y.shape[0] * y.shape[1] * RANK,
    )(*parts, y)


def exchange_stages():
    stages = []
    for axis in ("col", "row"):
        size = lax.axis_size(axis)
        bit = 1
        if axis == "col":
            stages.append((axis, size, [1]))
            bit = 2
        while bit < size:
            if 2 * bit < size:
                stages.append((axis, size, [bit, 2 * bit, 3 * bit]))
                bit *= 4
            else:
                stages.append((axis, size, [bit]))
                bit *= 2
    return stages


def summed_parts(gram):
    stages = exchange_stages()
    for place, (axis, size, partners) in enumerate(stages):
        parts = [gram] + [
            lax.ppermute(gram, axis, [(i, i ^ p) for i in range(size)]) for p in partners
        ]
        if place == len(stages) - 1:
            return parts
        gram = parts[0]
        for part in parts[1:]:
            gram = gram + part


def passed_along(shard, axis, by):
    count = lax.axis_size(axis)
    pairs = [(i, i + by) for i in range(count) if 0 <= i + by < count]
    return lax.ppermute(shard, axis, pairs)


def local(features, tissue, probe):
    tile_rows, tile_cols, patches, width = features.shape
    edges, middle = mark_row(features, tissue)
    below_edges = passed_along(edges, "row", -1)
    below_middle = passed_along(middle, "row", -1)
    own_panel = probe.reshape(tile_rows, tile_cols, patches, RANK)
    unit0, unit1, probe_left, probe_right = own_units(features, tissue, own_panel, middle)
    left_end, right_end = mark_ends(features, tissue, edges)
    from_left = passed_along(right_end, "col", 1)
    from_right = passed_along(left_end, "col", -1)
    probe_left, probe_right = passed_along(probe_right, "col", 1), passed_along(probe_left, "col", -1)
    panel = (probe_left, own_panel, probe_right)
    m, sums = inside_affinity(unit0, unit1, patches)
    _, u1, m, stat, payload = outside_affinity(unit0, unit1, m, from_left, from_right, tissue, sums, panel)
    got_below = passed_along(payload, "row", -1)
    below_left, below_right = cut(below_edges, stat)
    below_left, below_right = passed_along(below_right, "col", 1), passed_along(below_left, "col", -1)
    va, wa, sa, ua, paya = edge_affinity(below_left, below_edges, below_right, u1, stat, panel)
    vb, wb, sums, u0, t, payload = middle_affinity(below_edges, below_middle, u1, stat, panel, sa, ua, wa, paya)
    got_above = passed_along(payload, "row", 1)
    z = before_first(got_below, sums, u0, m, va, vb)
    y, u, tt, up, down = first_iteration(got_above, stat, t, z, panel, m, wa, wb)
    below, above = passed_along(up, "row", -1), passed_along(down, "row", 1)
    n = tile_cols + 2 * GHOST
    z = local_products(3, n - 3, m, u)
    y, u, up, down = middle_step(3, below, above, z, y, tt, va, wa, vb, wb)
    below, above = passed_along(up, "row", -1), passed_along(down, "row", 1)
    z = local_products(4, n - 4, m, u)
    y, gram = last_step(4, below, above, z, y, tt, va, vb)

    parts = summed_parts(gram)
    flat = y.reshape(tile_rows * tile_cols, patches * RANK)
    total = tile_rows * lax.axis_size("row") * tile_cols * lax.axis_size("col") * patches
    out = finish(math.sqrt(float(total)), parts, flat)
    return out.reshape(tile_rows, tile_cols, patches * RANK)


def solution(mesh):
    placed = (P("row", "col", None, None), P("row", "col", None), P("row", "col", None))
    return jax.shard_map(
        local, mesh=mesh, in_specs=placed, out_specs=P("row", "col", None), check_vma=False
    )
```

```python
import functools
import math

import jax
import jax.numpy as jnp
from jax import lax
from jax.experimental import pallas as pl
from jax.experimental.pallas import tpu as pltpu
from jax.sharding import PartitionSpec as P

RANK = 64
ITERS = 3
AFFINITY_TEMP = 4.0

GHOST = ITERS + 1
EDGE = 4
TINY = 1e-30
VMEM_BYTES = 16 * 1024 * 1024
FLOOR = math.exp(-AFFINITY_TEMP)
ABT = (((1,), (1,)), ((), ()))
ATB = (((0,), (0,)), ((), ()))

f32 = jnp.float32
bf16 = jnp.bfloat16


def kernel_call(body, out_shape, scratch=(), cost=0):
    return pl.pallas_call(
        body,
        out_shape=out_shape,
        scratch_shapes=list(scratch),
        compiler_params=pltpu.CompilerParams(vmem_limit_bytes=VMEM_BYTES),
        cost_estimate=pl.CostEstimate(flops=cost, bytes_accessed=1 << 20, transcendentals=0),
    )


def sds(shape, dtype):
    return jax.ShapeDtypeStruct(shape, dtype)


def iota(shape, dim):
    return lax.broadcasted_iota(jnp.int32, shape, dim)


def identity(n):
    return iota((n, n), 0) == iota((n, n), 1)


def unit_and_mask(block):
    values = block.astype(f32)
    scaled = values * lax.rsqrt(jnp.sum(values * values, axis=-1, keepdims=True) + 1e-06)
    return scaled.astype(bf16), (values[:, :1] != 0.0).astype(f32)


def affinity_of(left, right):
    scores = lax.dot_general(left, right, ABT, preferred_element_type=f32)
    return jnp.exp(AFFINITY_TEMP * scores - AFFINITY_TEMP)


def at_lane(lane, e, column, table):
    return jnp.where(lane == e, column, table)


def absent_near(mask, width):
    count = jnp.sum(mask, axis=0, keepdims=True)
    return width - (pltpu.roll(count, 1, 1) + count + pltpu.roll(count, 127, 1))


def packed(block):
    half = block.shape[0] // 2
    return jnp.concatenate([block[:half], block[half:]], axis=1)


def unpacked(block):
    return jnp.concatenate([block[:, :RANK], block[:, RANK:]], axis=0)


def panel_at(panel, row, e):
    left_ref, own_ref, right_ref = panel
    own = own_ref.shape[1]
    if GHOST <= e < GHOST + own:
        return own_ref[row, e - GHOST]
    ref, at = (left_ref, e) if e < GHOST else (right_ref, e - GHOST - own)
    both = ref[row, at, :, ref.shape[3] - 2 * RANK :].astype(f32)
    return both[:, :RANK] + both[:, RANK:]


def pair_of(values):
    high = values.astype(bf16)
    return high, (values - high.astype(f32)).astype(bf16)


def by_sublane(tissue):
    mask = (tissue != 0).astype(bf16)
    return lax.dot_general(mask, identity(mask.shape[0]).astype(bf16), ATB, preferred_element_type=f32)


def marked(tile, column):
    zero = (iota(tile.shape, 1) == 0) & (tile == 0)
    return jnp.where(zero, jnp.asarray(TINY, bf16), tile) * column.astype(bf16)


def fetched(sources, slots, sems):
    copies = [pltpu.make_async_copy(source, slot, sems.at[i]) for i, (source, slot) in enumerate(zip(sources, slots))]
    for copy in copies:
        copy.start()
    return copies


def in_hbm(*arrays):
    return tuple(pltpu.with_memory_space_constraint(array, pltpu.HBM) for array in arrays)


VMEM_SPEC = pl.BlockSpec(memory_space=pltpu.VMEM)
HBM_SPEC = pl.BlockSpec(memory_space=pltpu.HBM)
ANY_SPEC = pl.BlockSpec(memory_space=pl.ANY)


def mark_edges_kernel(x_ref, tissue_ref, edge_ref, tile_ref, mask_ref, sems):
    cols = x_ref.shape[1]
    chosen = list(range(EDGE)) + list(range(cols - EDGE, cols))
    sources = [tissue_ref.at[0]] + [x_ref.at[0, c] for c in chosen]
    copies = fetched(sources, [mask_ref] + [tile_ref.at[i] for i in range(len(chosen))], sems)
    copies[0].wait()
    mask = by_sublane(mask_ref[...])
    for i, c in enumerate(chosen):
        copies[i + 1].wait()
        edge_ref[i] = marked(tile_ref[i], mask[:, c : c + 1])


def mark_edges(x, tissue):
    rows, cols, patch, width = x.shape
    shape = (2 * EDGE, patch, width)
    return pl.pallas_call(
        mark_edges_kernel,
        in_specs=[HBM_SPEC, HBM_SPEC],
        out_specs=VMEM_SPEC,
        out_shape=sds(shape, bf16),
        scratch_shapes=[
            pltpu.VMEM(shape, bf16),
            pltpu.VMEM((cols, patch), jnp.int32),
            pltpu.SemaphoreType.DMA((2 * EDGE + 1,)),
        ],
        compiler_params=pltpu.CompilerParams(vmem_limit_bytes=VMEM_BYTES),
    )(*in_hbm(x, tissue))


def mark_rest_kernel(x_ref, tissue_ref, probe_ref, after_ref, left_ref, right_ref, middle_ref, tile_ref, sems):
    rows, cols, patch, width = x_ref.shape
    ends = [(row, c) for row in range(rows) for c in list(range(GHOST)) + list(range(cols - GHOST, cols))]
    chosen = ends + [(0, c) for c in range(EDGE, cols - EDGE)]
    copies = fetched([x_ref.at[row, c] for row, c in chosen], [tile_ref.at[i] for i in range(len(chosen))], sems)
    masks = [by_sublane(tissue_ref[row]) for row in range(rows)]
    for i, (row, c) in enumerate(chosen):
        copies[i].wait()
        tile = marked(tile_ref[i], masks[row][:, c : c + 1])
        if i >= len(ends):
            middle_ref[c - EDGE] = tile
            continue
        side_ref, at = (left_ref, c) if c < GHOST else (right_ref, c - cols + GHOST)
        side_ref[row, at, :, :width] = tile
        side_ref[row, at, :, width:] = jnp.concatenate(pair_of(probe_ref[row, c]), axis=1)


def mark_rest(x, tissue, probe, after):
    rows, cols, patch, width = x.shape
    side = sds((rows, GHOST, patch, width + 2 * RANK), bf16)
    count = 2 * rows * GHOST + cols - 2 * EDGE
    return pl.pallas_call(
        mark_rest_kernel,
        in_specs=[HBM_SPEC, VMEM_SPEC, VMEM_SPEC, ANY_SPEC],
        out_specs=[VMEM_SPEC] * 3,
        out_shape=(side, side, sds((cols - 2 * EDGE, patch, width), bf16)),
        scratch_shapes=[pltpu.VMEM((count, patch, width), bf16), pltpu.SemaphoreType.DMA((count,))],
        compiler_params=pltpu.CompilerParams(vmem_limit_bytes=VMEM_BYTES),
    )(*in_hbm(x), tissue, probe, after)


def units_kernel(n, x_ref, tissue_ref, after_ref, unit0_ref, unit1_ref, tile_ref, sems):
    rows, cols, patch, width = x_ref.shape
    chosen = [(row, c) for row in range(rows) for c in range(cols)]
    copies = fetched([x_ref.at[row, c] for row, c in chosen], [tile_ref.at[i] for i in range(len(chosen))], sems)
    masks = [by_sublane(tissue_ref[row]).astype(bf16) for row in range(rows)]
    for i, (row, c) in enumerate(chosen):
        copies[i].wait()
        unit, _ = unit_and_mask(tile_ref[i])
        at = (GHOST + c) * patch
        (unit0_ref, unit1_ref)[row][at : at + patch, :] = unit * masks[row][:, c : c + 1]


def own_units(x, tissue, after):
    rows, cols, patch, width = x.shape
    n = cols + 2 * GHOST
    unit = sds((n * patch, width), bf16)
    return pl.pallas_call(
        functools.partial(units_kernel, n),
        in_specs=[HBM_SPEC, VMEM_SPEC, ANY_SPEC],
        out_specs=[VMEM_SPEC] * 2,
        out_shape=(unit, unit),
        scratch_shapes=[pltpu.VMEM((rows * cols, patch, width), bf16), pltpu.SemaphoreType.DMA((rows * cols,))],
        compiler_params=pltpu.CompilerParams(vmem_limit_bytes=VMEM_BYTES),
    )(*in_hbm(x), tissue, after)


def bands(ranges, patch, unit0_ref, unit1_ref, m_ref, degree, diagonal):
    both = 2 * patch
    shape = (both, 3 * both)
    patch_of = iota(shape, 0)
    own = iota(shape, 1) == jnp.where(patch_of < patch, patch_of + patch, patch_of + 3 * patch)
    lane = iota((both, 128), 1)

    def band(e, carry):
        degree, diagonal = carry
        around = slice((e - 1) * patch, (e + 2) * patch)
        here = slice(e * patch, (e + 1) * patch)
        left = jnp.concatenate([unit0_ref[here, :], unit1_ref[here, :]], axis=0)
        right = jnp.concatenate([unit0_ref[around, :], unit1_ref[around, :]], axis=0)
        weights = affinity_of(left, right)
        others = jnp.where(own, 0.0, weights)
        m_ref[e] = others.astype(bf16)
        itself = jnp.sum(weights - others, axis=1, keepdims=True)
        degree = at_lane(lane, e, jnp.sum(weights, axis=1, keepdims=True), degree)
        diagonal = at_lane(lane, e, itself, diagonal)
        return degree, diagonal

    carry = (degree, diagonal)
    for low, high in ranges:
        for e in range(low, high):
            carry = band(e, carry)
    return carry


def inside_kernel(n, unit0_ref, unit1_ref, m_ref, sum_ref):
    patch = m_ref.shape[1] // 2
    empty = jnp.zeros((2 * patch, 128), f32)
    sum_ref[0], sum_ref[1] = bands([(GHOST + 1, n - GHOST - 1)], patch, unit0_ref, unit1_ref, m_ref, empty, empty)


def inside_affinity(unit0, unit1, patch):
    n = unit0.shape[0] // patch
    both = 2 * patch
    return pl.pallas_call(
        functools.partial(inside_kernel, n),
        out_shape=(sds((n, both, 3 * both), bf16), sds((2, both, 128), f32)),
        compiler_params=pltpu.CompilerParams(vmem_limit_bytes=VMEM_BYTES),
    )(unit0, unit1)


def outside_kernel(
    n,
    start0_ref, start1_ref, some_ref, tissue_ref, sum_ref, xl_ref, p_ref, xr_ref, after_ref,
    unit0_ref, unit1_ref, m_ref, stat_ref, pay_ref, pl_ref, pr_ref,
):
    rows, count, patch, _ = xl_ref.shape
    width = unit0_ref.shape[1]
    cols = n - 2 * count
    both = rows * patch
    lane = iota((patch, 128), 1)

    masks = []
    for row, unit_ref in ((0, unit0_ref), (1, unit1_ref)):
        own_mask = by_sublane(tissue_ref[row])
        mask = jnp.zeros((patch, 128), f32)
        for e in range(n):
            if e < count:
                unit, column = unit_and_mask(xl_ref[row, e, :, :width])
            elif e < count + cols:
                unit, column = None, own_mask[:, e - count : e - count + 1]
            else:
                unit, column = unit_and_mask(xr_ref[row, e - count - cols, :, :width])
            mask = at_lane(lane, e, column, mask)
            if unit is not None:
                unit_ref[e * patch : (e + 1) * patch, :] = unit
        masks.append(mask)
    mask = jnp.concatenate(masks, axis=0)
    ranges = [(1, GHOST + 1), (n - GHOST - 1, n - 1)]
    degree, diagonal = bands(ranges, patch, unit0_ref, unit1_ref, m_ref, sum_ref[0], sum_ref[1])
    degree = degree - FLOOR * absent_near(mask, 3 * both)
    stat_ref[0] = degree
    stat_ref[1] = diagonal
    stat_ref[2] = mask
    half = patch // 2
    tail = (n - 2) * half
    for e in range(1, n - 1):
        pay_ref[(e - 1) * half : e * half, :] = packed(panel_at((xl_ref, p_ref, xr_ref), 0, e)).astype(bf16)
    pay_ref[tail : tail + patch, :], pay_ref[tail + patch :, :] = pair_of(degree[:patch])
    pl_ref[...] = xl_ref[:, :, :, width:]
    pr_ref[...] = xr_ref[:, :, :, width:]


def payload_rows(columns, patch):
    return columns * patch // 2 + 2 * patch


def outside_affinity(unit0, unit1, m, tissue, sums, panel, after):
    n, both, _ = m.shape
    payload = sds((payload_rows(n - 2, both // 2), 2 * RANK), bf16)
    side = sds(panel[0].shape[:3] + (2 * RANK,), bf16)
    unit = sds(unit0.shape, bf16)
    return pl.pallas_call(
        functools.partial(outside_kernel, n),
        in_specs=[VMEM_SPEC] * 8 + [ANY_SPEC],
        out_specs=[VMEM_SPEC] * 7,
        out_shape=(unit, unit, sds(m.shape, bf16), sds((3, both, 128), f32), payload, side, side),
        input_output_aliases={0: 0, 1: 1, 2: 2},
        compiler_params=pltpu.CompilerParams(vmem_limit_bytes=VMEM_BYTES),
    )(unit0, unit1, m, tissue, sums, *panel, after)


def cut_kernel(be_ref, after_ref, left_ref, right_ref):
    left_ref[...] = be_ref[:GHOST]
    right_ref[...] = be_ref[be_ref.shape[0] - GHOST :]


def cut(be, after):
    vmem = pl.BlockSpec(memory_space=pltpu.VMEM)
    side = sds((GHOST,) + be.shape[1:], be.dtype)
    return pl.pallas_call(
        cut_kernel,
        in_specs=[vmem, pl.BlockSpec(memory_space=pl.ANY)],
        out_specs=[vmem] * 2,
        out_shape=(side, side),
        compiler_params=pltpu.CompilerParams(vmem_limit_bytes=VMEM_BYTES),
    )(be, after)


def cross_columns(patch, columns, sources, own_ref, unit_ref, v_ref, w_ref, sums):
    lane = iota((patch, 128), 1)
    down_sum, up_sum, mask = sums
    needed = sorted({c for e in columns for c in (e - 1, e, e + 1)})
    for c in needed:
        ref, index = sources[c]
        unit, column = unit_and_mask(ref[index])
        unit_ref[c * patch : (c + 1) * patch, :] = unit
        mask = at_lane(lane, c, column, mask)
    for place, e in enumerate(columns):
        around = slice((e - 1) * patch, (e + 2) * patch)
        here = slice(e * patch, (e + 1) * patch)
        down = affinity_of(own_ref[here, :], unit_ref[around, :])
        up = affinity_of(unit_ref[here, :], own_ref[around, :])
        v_ref[place] = down.astype(bf16)
        w_ref[place] = up.astype(bf16)
        down_sum = at_lane(lane, e, jnp.sum(down, axis=1, keepdims=True), down_sum)
        up_sum = at_lane(lane, e, jnp.sum(up, axis=1, keepdims=True), up_sum)
    return down_sum, up_sum, mask


def edge_columns(n):
    return list(range(1, GHOST + EDGE - 1)) + list(range(n - GHOST - EDGE + 1, n - 1))


def middle_columns(n):
    return list(range(GHOST + EDGE - 1, n - GHOST - EDGE + 1))


def inner(columns, low, high):
    return [e for e in columns if low <= e < high and e - 1 in columns and e + 1 in columns]


def place_of(n):
    edge, middle = edge_columns(n), middle_columns(n)
    return {e: (0, i) for i, e in enumerate(edge)} | {e: (1, i) for i, e in enumerate(middle)}


def below_sources(n, bl_ref, be_ref, bm_ref, br_ref):
    sources = {}
    for c in range(n):
        if c < GHOST:
            sources[c] = (bl_ref, c)
        elif c < GHOST + EDGE:
            sources[c] = (be_ref, c - GHOST)
        elif c < n - GHOST - EDGE:
            sources[c] = (bm_ref, c - GHOST - EDGE)
        elif c < n - GHOST:
            sources[c] = (be_ref, c - (n - GHOST) + 2 * EDGE)
        else:
            sources[c] = (br_ref, c - (n - GHOST))
    return sources


def scale_of(stat_ref, sums):
    down_sum, _, mask = sums
    patch = mask.shape[0]
    degree = 1.0 + stat_ref[0, patch:] + down_sum - FLOOR * absent_near(mask, 3 * patch)
    return stat_ref[2, patch:] * lax.rsqrt(degree)


def products(columns, where, ups, u_ref, pay_ref, first):
    half = u_ref.shape[1] // 2
    for e in columns:
        which, i = where[e]
        source = u_ref[e - 1 : e + 2].reshape(3 * u_ref.shape[1], RANK)
        product = jnp.dot(ups[which][i], source, preferred_element_type=f32)
        pay_ref[(e - first) * half : (e - first + 1) * half, :] = packed(product).astype(bf16)


def edge_kernel(n, bl_ref, be_ref, br_ref, u1_ref, stat_ref, pl_ref, p_ref, pr_ref, v_ref, w_ref, sum_ref, u0_ref, pay_ref, unit_ref):
    patch = be_ref.shape[1]
    sources = below_sources(n, bl_ref, be_ref, None, br_ref)
    columns = edge_columns(n)
    empty = jnp.zeros((patch, 128), f32)
    sums = cross_columns(patch, columns, sources, u1_ref, unit_ref, v_ref, w_ref, (empty, empty, empty))
    for i in range(3):
        sum_ref[i] = sums[i]
    scale = scale_of(stat_ref, sums)
    for e in columns:
        u0_ref[e] = (scale[:, e : e + 1] * panel_at((pl_ref, p_ref, pr_ref), 1, e)).astype(bf16)
    products(inner(columns, 2, n - 2), place_of(n), (w_ref, None), u0_ref, pay_ref, 2)


def edge_affinity(bl, be, br, u1, stat, panel):
    _, patch, width = be.shape
    n = u1.shape[0] // patch
    count = len(edge_columns(n))
    return kernel_call(
        functools.partial(edge_kernel, n),
        (
            sds((count, patch, 3 * patch), bf16),
            sds((count, patch, 3 * patch), bf16),
            sds((3, patch, 128), f32),
            sds((n, patch, RANK), bf16),
            sds(((n - 4) * patch // 2, 2 * RANK), bf16),
        ),
        [pltpu.VMEM((n * patch, width), bf16)],
        cost=4 * count * patch * 3 * patch * width,
    )(bl, be, br, u1, stat, *panel)


def middle_kernel(
    n,
    be_ref, bm_ref, u1_ref, stat_ref, pl_ref, p_ref, pr_ref, sa_ref, ua_ref, wa_ref, paya_ref,
    v_ref, w_ref, sum_ref, u0_ref, t_ref, pay_ref,
    unit_ref,
):
    patch = be_ref.shape[1]
    half = patch // 2
    sources = below_sources(n, None, be_ref, bm_ref, None)
    columns = middle_columns(n)
    before = tuple(sa_ref[i] for i in range(3))
    sums = cross_columns(patch, columns, sources, u1_ref, unit_ref, v_ref, w_ref, before)
    scale = scale_of(stat_ref, sums)
    t_ref[...] = scale
    shared = sums[1] - FLOOR * absent_near(stat_ref[2, patch:], 3 * patch)
    sum_ref[0] = shared
    sum_ref[1] = sums[2]
    edges = edge_columns(n)
    for e in edges:
        u0_ref[e] = ua_ref[e]
    for e in columns:
        u0_ref[e] = (scale[:, e : e + 1] * panel_at((pl_ref, p_ref, pr_ref), 1, e)).astype(bf16)
    done = inner(edges, 2, n - 2)
    for e in done:
        pay_ref[(e - 2) * half : (e - 1) * half, :] = paya_ref[(e - 2) * half : (e - 1) * half, :]
    products([e for e in range(2, n - 2) if e not in done], place_of(n), (wa_ref, w_ref), u0_ref, pay_ref, 2)
    tail = (n - 4) * half
    pay_ref[tail : tail + patch, :], pay_ref[tail + patch :, :] = pair_of(shared)


def middle_affinity(be, bm, u1, stat, panel, sa, ua, wa, paya):
    _, patch, width = be.shape
    n = u1.shape[0] // patch
    count = len(middle_columns(n))
    return kernel_call(
        functools.partial(middle_kernel, n),
        (
            sds((count, patch, 3 * patch), bf16),
            sds((count, patch, 3 * patch), bf16),
            sds((2, patch, 128), f32),
            sds((n, patch, RANK), bf16),
            sds((patch, 128), f32),
            sds((payload_rows(n - 4, patch), 2 * RANK), bf16),
        ),
        [pltpu.VMEM((n * patch, width), bf16)],
        cost=4 * count * patch * 3 * patch * width,
    )(be, bm, u1, stat, *panel, sa, ua, wa, paya)


def before_first_kernel(n, got_ref, sum_ref, u0_ref, m_ref, va_ref, vb_ref, z_ref, u2_ref):
    patch = u0_ref.shape[1]
    half = patch // 2
    both = 2 * patch
    where = place_of(n)
    tail = (n - 2) * half
    partial = got_ref[tail : tail + patch, :].astype(f32) + got_ref[tail + patch :, :].astype(f32)
    scale = sum_ref[1] * lax.rsqrt(1.0 + partial + sum_ref[0])
    for e in range(1, n - 1):
        theirs = unpacked(got_ref[(e - 1) * half : e * half, :].astype(f32))
        u2_ref[e] = (scale[:, e : e + 1] * theirs).astype(bf16)
    for e in range(2, n - 2):
        which, i = where[e]
        own = u0_ref[e - 1 : e + 2].reshape(3 * patch, RANK)
        total = jnp.dot(m_ref[e, :, 3 * patch :], own, preferred_element_type=f32)
        below = u2_ref[e - 1 : e + 2].reshape(3 * patch, RANK)
        lower = jnp.dot((va_ref, vb_ref)[which][i], below, preferred_element_type=f32)
        z_ref[e, :patch] = total[:patch]
        z_ref[e, patch:] = total[patch:] + lower


def before_first(got, sums, u0, m, va, vb):
    n, patch, _ = u0.shape
    return kernel_call(
        functools.partial(before_first_kernel, n),
        sds((n, 2 * patch, RANK), f32),
        [pltpu.VMEM((n, patch, RANK), bf16)],
        cost=2 * n * 2 * patch * 3 * patch * RANK,
    )(got, sums, u0, m, va, vb)


def first_kernel(
    n,
    got_ref, stat_ref, t_ref, z_ref, pl_ref, p_ref, pr_ref, m_ref, wa_ref, wb_ref,
    y_ref, u_ref, tt_ref, up_ref, down_ref,
    start_ref,
):
    panel = (pl_ref, p_ref, pr_ref)
    patch = t_ref.shape[0]
    half = patch // 2
    tail = (n - 4) * half
    partial = got_ref[tail : tail + patch, :].astype(f32) + got_ref[tail + patch :, :].astype(f32)
    upper_scale = stat_ref[2, :patch] * lax.rsqrt(1.0 + stat_ref[0, :patch] + partial)
    scale = jnp.concatenate([upper_scale, t_ref[...]], axis=0)
    gain = 1.0 + scale * scale * stat_ref[1]
    tt_ref[0] = scale
    tt_ref[1] = gain
    for e in range(1, n - 1):
        start_ref[e] = (upper_scale[:, e : e + 1] * panel_at(panel, 0, e)).astype(bf16)
    for e in range(2, n - 2):
        own = start_ref[e - 1 : e + 2].reshape(3 * patch, RANK)
        total = z_ref[e] + jnp.dot(m_ref[e, :, : 3 * patch], own, preferred_element_type=f32)
        upper = unpacked(got_ref[(e - 2) * half : (e - 1) * half, :].astype(f32))
        for row in range(2):
            span = slice(row * patch, (row + 1) * patch)
            piece = total[span] + upper if row == 0 else total[span]
            t = scale[span, e : e + 1]
            image = panel_at(panel, row, e) * gain[span, e : e + 1] + t * piece
            y_ref[row, e] = image
            scaled = t * image
            u_ref[row, e] = scaled.astype(bf16)
            if row == 0:
                up_ref[(e - 2) * half : (e - 1) * half, :] = packed(scaled).astype(bf16)
    products(range(3, n - 3), place_of(n), (wa_ref, wb_ref), u_ref.at[1], down_ref, 3)


def first_iteration(got, stat, t, z, panel, m, wa, wb):
    n, both, _ = z.shape
    patch = both // 2
    half = patch // 2
    return kernel_call(
        functools.partial(first_kernel, n),
        (
            sds((2, n, patch, RANK), f32),
            sds((2, n, patch, RANK), bf16),
            sds((2, both, 128), f32),
            sds(((n - 4) * half, 2 * RANK), bf16),
            sds(((n - 6) * half, 2 * RANK), bf16),
        ),
        [pltpu.VMEM((n, patch, RANK), bf16)],
        cost=2 * n * both * 3 * patch * RANK,
    )(got, stat, t, z, *panel, m, wa, wb)


def local_kernel(low, high, m_ref, u_ref, z_ref):
    patch = u_ref.shape[2]
    for e in range(low, high):
        upper = u_ref[0, e - 1 : e + 2].reshape(3 * patch, RANK)
        lower = u_ref[1, e - 1 : e + 2].reshape(3 * patch, RANK)
        z_ref[e] = jnp.dot(m_ref[e], jnp.concatenate([upper, lower], axis=0), preferred_element_type=f32)


def local_products(low, high, m, u):
    n, both, _ = m.shape
    return kernel_call(
        functools.partial(local_kernel, low, high),
        sds((n, both, RANK), f32),
        cost=2 * n * both * 3 * both * RANK,
    )(m, u)


def joined(e, low, where, downs, near, z_ref, above_ref, y_ref, scale, gain):
    patch = y_ref.shape[2]
    half = patch // 2
    which, i = where[e]
    below = jnp.concatenate([near[e - 1], near[e], near[e + 1]], axis=0)
    lower = z_ref[e, patch:] + jnp.dot(downs[which][i], below, preferred_element_type=f32)
    upper = z_ref[e, :patch] + unpacked(above_ref[(e - low) * half : (e - low + 1) * half, :].astype(f32))
    images = []
    for row, piece in ((0, upper), (1, lower)):
        span = slice(row * patch, (row + 1) * patch)
        images.append(y_ref[row, e] * gain[span, e : e + 1] + scale[span, e : e + 1] * piece)
    return images


def halo(n, low, half, below_ref):
    return {
        e: unpacked(below_ref[(e - low + 1) * half : (e - low + 2) * half, :]) for e in range(low - 1, n - low + 1)
    }


def middle_step_kernel(
    n, low,
    below_ref, above_ref, z_ref, y_ref, tt_ref, va_ref, wa_ref, vb_ref, wb_ref,
    new_ref, u_ref, up_ref, down_ref,
):
    patch = y_ref.shape[2]
    half = patch // 2
    where = place_of(n)
    scale, gain = tt_ref[0], tt_ref[1]
    near = halo(n, low, half, below_ref)
    for e in range(low, n - low):
        images = joined(e, low, where, (va_ref, vb_ref), near, z_ref, above_ref, y_ref, scale, gain)
        for row in range(2):
            new_ref[row, e] = images[row]
            scaled = scale[row * patch : (row + 1) * patch, e : e + 1] * images[row]
            u_ref[row, e] = scaled.astype(bf16)
            if row == 0:
                up_ref[(e - low) * half : (e - low + 1) * half, :] = packed(scaled).astype(bf16)
    products(range(low + 1, n - low - 1), where, (wa_ref, wb_ref), u_ref.at[1], down_ref, low + 1)


def middle_step(low, below, above, z, y, tt, va, wa, vb, wb):
    _, n, patch, _ = y.shape
    half = patch // 2
    return kernel_call(
        functools.partial(middle_step_kernel, n, low),
        (
            sds((2, n, patch, RANK), f32),
            sds((2, n, patch, RANK), bf16),
            sds(((n - 2 * low) * half, 2 * RANK), bf16),
            sds(((n - 2 * low - 2) * half, 2 * RANK), bf16),
        ),
        cost=8 * n * patch * patch * RANK,
    )(below, above, z, y, tt, va, wa, vb, wb)


def last_step_kernel(n, low, below_ref, above_ref, z_ref, y_ref, tt_ref, va_ref, vb_ref, new_ref, gram_ref, side_ref):
    patch = y_ref.shape[2]
    where = place_of(n)
    scale, gain = tt_ref[0], tt_ref[1]
    near = halo(n, low, patch // 2, below_ref)
    wide = 2 * RANK
    for e in range(low, n - low):
        images = joined(e, low, where, (va_ref, vb_ref), near, z_ref, above_ref, y_ref, scale, gain)
        for row in range(2):
            new_ref[row, e - low] = images[row]
        span = slice((e - low) * patch, (e - low + 1) * patch)
        side_ref[span, :wide], side_ref[span, wide:] = pair_of(jnp.concatenate(images, axis=1))
    side = side_ref[...]
    gram = lax.dot_general(side, side, ATB, preferred_element_type=f32)
    gram = gram[:wide] + gram[wide:]
    gram = gram[:, :wide] + gram[:, wide:]
    gram_ref[...] = packed(gram[:RANK, :RANK] + gram[RANK:, RANK:])


def last_step(low, below, above, z, y, tt, va, vb):
    _, n, patch, _ = y.shape
    cols = n - 2 * low
    return kernel_call(
        functools.partial(last_step_kernel, n, low),
        (sds((2, cols, patch, RANK), f32), sds((RANK // 2, 2 * RANK), f32)),
        [pltpu.VMEM((cols * patch, 4 * RANK), bf16)],
        cost=8 * n * patch * patch * RANK,
    )(below, above, z, y, tt, va, vb)


def inverse_factor(gram):
    size = gram.shape[0]
    step = 4
    row = iota((size, 2 * size), 0)
    lane = iota((size, 2 * size), 1)
    table = jnp.concatenate([gram, identity(size).astype(f32)], axis=1)
    for k in range(0, size, step):
        cols = [jnp.broadcast_to(table[:, k + i : k + i + 1], table.shape) for i in range(step)]
        lines = [table[k + i : k + i + 1, :] for i in range(step)]
        for i in range(step):
            inverse = 1.0 / cols[i][k + i : k + i + 1, :]
            for j in range(i + 1, step):
                lines[j] = lines[j] - lines[i] * (cols[i][k + j : k + j + 1, :] * inverse)
                cols[j] = cols[j] - cols[i] * (cols[j][k + i : k + i + 1, :] * inverse)
            table = table - jnp.where(row > k + i, cols[i], 0.0) * (lines[i] * inverse)
    pivots = jnp.sum(jnp.where(row == lane, table, 0.0), axis=1, keepdims=True)
    return table[:, size:] * lax.rsqrt(pivots)


def finish_kernel(factor, count, *refs):
    parts, y_ref, out_ref = refs[:count], refs[count], refs[count + 1]
    total = parts[0][...]
    for part in parts[1:]:
        total = total + part[...]
    inverse = factor * inverse_factor(unpacked(total))
    zero = jnp.zeros_like(inverse)
    both = jnp.concatenate(
        [jnp.concatenate([inverse, zero], axis=1), jnp.concatenate([zero, inverse], axis=1)], axis=0
    )
    wide = 2 * RANK
    tiles, width = y_ref.shape
    pieces = [y_ref[:, q * wide : (q + 1) * wide] for q in range(width // wide)]
    y_high, y_low = pair_of(jnp.concatenate(pieces, axis=0))
    t_high, t_low = pair_of(both)

    def times(a, b):
        return lax.dot_general(a, b, ABT, preferred_element_type=f32)

    out = times(y_high, t_high) + (times(y_low, t_high) + times(y_high, t_low))
    for q in range(width // wide):
        out_ref[:, q * wide : (q + 1) * wide] = out[q * tiles : (q + 1) * tiles]


def finish(factor, parts, y):
    return kernel_call(
        functools.partial(finish_kernel, factor, len(parts)),
        sds(y.shape, f32),
        cost=2 * y.shape[0] * y.shape[1] * RANK,
    )(*parts, y)


def exchange_stages():
    stages = []
    for axis in ("col", "row"):
        size = lax.axis_size(axis)
        bit = 1
        if axis == "col":
            stages.append((axis, size, [1]))
            bit = 2
        while bit < size:
            if 2 * bit < size:
                stages.append((axis, size, [bit, 2 * bit, 3 * bit]))
                bit *= 4
            else:
                stages.append((axis, size, [bit]))
                bit *= 2
    return stages


def summed_parts(gram):
    stages = exchange_stages()
    for place, (axis, size, partners) in enumerate(stages):
        parts = [gram] + [
            lax.ppermute(gram, axis, [(i, i ^ p) for i in range(size)]) for p in partners
        ]
        if place == len(stages) - 1:
            return parts
        gram = parts[0]
        for part in parts[1:]:
            gram = gram + part


def passed_along(shard, axis, by):
    count = lax.axis_size(axis)
    pairs = [(i, i + by) for i in range(count) if 0 <= i + by < count]
    return lax.ppermute(shard, axis, pairs)


def local(features, tissue, probe):
    tile_rows, tile_cols, patches, width = features.shape
    edges = mark_edges(features, tissue)
    below_edges = passed_along(edges, "row", -1)
    own_panel = probe.reshape(tile_rows, tile_cols, patches, RANK)
    left_end, right_end, middle = mark_rest(features, tissue, own_panel, edges)
    from_left = passed_along(right_end, "col", 1)
    from_right = passed_along(left_end, "col", -1)
    below_middle = passed_along(middle, "row", -1)
    unit0, unit1 = own_units(features, tissue, left_end)
    m, sums = inside_affinity(unit0, unit1, patches)
    below_left, below_right = cut(below_edges, sums)
    panel = (from_left, own_panel, from_right)
    _, u1, m, stat, payload, *sides = outside_affinity(unit0, unit1, m, tissue, sums, panel, below_left)
    panel = (sides[0], own_panel, sides[1])
    below_left, below_right = passed_along(below_right, "col", 1), passed_along(below_left, "col", -1)
    got_below = passed_along(payload, "row", -1)
    va, wa, sa, ua, paya = edge_affinity(below_left, below_edges, below_right, u1, stat, panel)
    vb, wb, sums, u0, t, payload = middle_affinity(below_edges, below_middle, u1, stat, panel, sa, ua, wa, paya)
    got_above = passed_along(payload, "row", 1)
    z = before_first(got_below, sums, u0, m, va, vb)
    y, u, tt, up, down = first_iteration(got_above, stat, t, z, panel, m, wa, wb)
    below, above = passed_along(up, "row", -1), passed_along(down, "row", 1)
    n = tile_cols + 2 * GHOST
    z = local_products(3, n - 3, m, u)
    y, u, up, down = middle_step(3, below, above, z, y, tt, va, wa, vb, wb)
    below, above = passed_along(up, "row", -1), passed_along(down, "row", 1)
    z = local_products(4, n - 4, m, u)
    y, gram = last_step(4, below, above, z, y, tt, va, vb)

    parts = summed_parts(gram)
    flat = y.reshape(tile_rows * tile_cols, patches * RANK)
    total = tile_rows * lax.axis_size("row") * tile_cols * lax.axis_size("col") * patches
    out = finish(math.sqrt(float(total)), parts, flat)
    return out.reshape(tile_rows, tile_cols, patches * RANK)


def solution(mesh):
    placed = (P("row", "col", None, None), P("row", "col", None), P("row", "col", None))
    return jax.shard_map(
        local, mesh=mesh, in_specs=placed, out_specs=P("row", "col", None), check_vma=False
    )
```

```python
import functools
import math

import jax
import jax.numpy as jnp
from jax import lax
from jax.experimental import pallas as pl
from jax.experimental.pallas import tpu as pltpu
from jax.sharding import PartitionSpec as P

RANK = 64
ITERS = 3
AFFINITY_TEMP = 4.0

GHOST = ITERS + 1
EDGE = 4
TINY = 1e-30
VMEM_BYTES = 16 * 1024 * 1024
FLOOR = math.exp(-AFFINITY_TEMP)
ABT = (((1,), (1,)), ((), ()))
ATB = (((0,), (0,)), ((), ()))

f32 = jnp.float32
bf16 = jnp.bfloat16


def kernel_call(body, out_shape, scratch=()):
    return pl.pallas_call(
        body,
        out_shape=out_shape,
        scratch_shapes=list(scratch),
        compiler_params=pltpu.CompilerParams(vmem_limit_bytes=VMEM_BYTES),
    )


def sds(shape, dtype):
    return jax.ShapeDtypeStruct(shape, dtype)


def iota(shape, dim):
    return lax.broadcasted_iota(jnp.int32, shape, dim)


def identity(n):
    return iota((n, n), 0) == iota((n, n), 1)


def unit_and_mask(block):
    values = block.astype(f32)
    scaled = values * lax.rsqrt(jnp.sum(values * values, axis=-1, keepdims=True) + 1e-06)
    return scaled.astype(bf16), (values[:, :1] != 0.0).astype(f32)


def affinity_of(left, right):
    scores = lax.dot_general(left, right, ABT, preferred_element_type=f32)
    return jnp.exp(AFFINITY_TEMP * scores - AFFINITY_TEMP)


def at_lane(lane, e, column, table):
    return jnp.where(lane == e, column, table)


def absent_near(mask, width):
    count = jnp.sum(mask, axis=0, keepdims=True)
    return width - (pltpu.roll(count, 1, 1) + count + pltpu.roll(count, 127, 1))


def packed(block):
    half = block.shape[0] // 2
    return jnp.concatenate([block[:half], block[half:]], axis=1)


def unpacked(block):
    return jnp.concatenate([block[:, :RANK], block[:, RANK:]], axis=0)


def panel_at(panel, row, e):
    left_ref, own_ref, right_ref = panel
    own = own_ref.shape[1]
    if GHOST <= e < GHOST + own:
        return own_ref[row, e - GHOST]
    ref, at = (left_ref, e) if e < GHOST else (right_ref, e - GHOST - own)
    both = ref[row, at, :, ref.shape[3] - 2 * RANK :].astype(f32)
    return both[:, :RANK] + both[:, RANK:]


def pair_of(values):
    high = values.astype(bf16)
    return high, (values - high.astype(f32)).astype(bf16)


def by_sublane(tissue):
    mask = (tissue != 0).astype(bf16)
    return lax.dot_general(mask, identity(mask.shape[0]).astype(bf16), ATB, preferred_element_type=f32)


def marked(tile, column):
    zero = (iota(tile.shape, 1) == 0) & (tile == 0)
    return jnp.where(zero, jnp.asarray(TINY, bf16), tile) * column.astype(bf16)


def fetched(sources, slots, sems):
    copies = [pltpu.make_async_copy(source, slot, sems.at[i]) for i, (source, slot) in enumerate(zip(sources, slots))]
    for copy in copies:
        copy.start()
    return copies


def in_hbm(*arrays):
    return tuple(pltpu.with_memory_space_constraint(array, pltpu.HBM) for array in arrays)


VMEM_SPEC = pl.BlockSpec(memory_space=pltpu.VMEM)
HBM_SPEC = pl.BlockSpec(memory_space=pltpu.HBM)
ANY_SPEC = pl.BlockSpec(memory_space=pl.ANY)


def mark_edges_kernel(x_ref, tissue_ref, edge_ref, tile_ref, mask_ref, sems):
    cols = x_ref.shape[1]
    chosen = list(range(EDGE)) + list(range(cols - EDGE, cols))
    sources = [tissue_ref.at[0]] + [x_ref.at[0, c] for c in chosen]
    copies = fetched(sources, [mask_ref] + [tile_ref.at[i] for i in range(len(chosen))], sems)
    copies[0].wait()
    mask = by_sublane(mask_ref[...])
    for i, c in enumerate(chosen):
        copies[i + 1].wait()
        edge_ref[i] = marked(tile_ref[i], mask[:, c : c + 1])


def mark_edges(x, tissue):
    rows, cols, patch, width = x.shape
    shape = (2 * EDGE, patch, width)
    return pl.pallas_call(
        mark_edges_kernel,
        in_specs=[HBM_SPEC, HBM_SPEC],
        out_specs=VMEM_SPEC,
        out_shape=sds(shape, bf16),
        scratch_shapes=[
            pltpu.VMEM(shape, bf16),
            pltpu.VMEM((cols, patch), jnp.int32),
            pltpu.SemaphoreType.DMA((2 * EDGE + 1,)),
        ],
        compiler_params=pltpu.CompilerParams(vmem_limit_bytes=VMEM_BYTES),
    )(*in_hbm(x, tissue))


def mark_rest_kernel(x_ref, tissue_ref, probe_ref, after_ref, left_ref, right_ref, middle_ref, tile_ref, sems):
    rows, cols, patch, width = x_ref.shape
    ends = [(row, c) for row in range(rows) for c in list(range(GHOST)) + list(range(cols - GHOST, cols))]
    chosen = ends + [(0, c) for c in range(EDGE, cols - EDGE)]
    copies = fetched([x_ref.at[row, c] for row, c in chosen], [tile_ref.at[i] for i in range(len(chosen))], sems)
    masks = [by_sublane(tissue_ref[row]) for row in range(rows)]
    for i, (row, c) in enumerate(chosen):
        copies[i].wait()
        tile = marked(tile_ref[i], masks[row][:, c : c + 1])
        if i >= len(ends):
            middle_ref[c - EDGE] = tile
            continue
        side_ref, at = (left_ref, c) if c < GHOST else (right_ref, c - cols + GHOST)
        side_ref[row, at, :, :width] = tile
        side_ref[row, at, :, width:] = jnp.concatenate(pair_of(probe_ref[row, c]), axis=1)


def mark_rest(x, tissue, probe, after):
    rows, cols, patch, width = x.shape
    side = sds((rows, GHOST, patch, width + 2 * RANK), bf16)
    count = 2 * rows * GHOST + cols - 2 * EDGE
    return pl.pallas_call(
        mark_rest_kernel,
        in_specs=[HBM_SPEC, VMEM_SPEC, VMEM_SPEC, ANY_SPEC],
        out_specs=[VMEM_SPEC] * 3,
        out_shape=(side, side, sds((cols - 2 * EDGE, patch, width), bf16)),
        scratch_shapes=[pltpu.VMEM((count, patch, width), bf16), pltpu.SemaphoreType.DMA((count,))],
        compiler_params=pltpu.CompilerParams(vmem_limit_bytes=VMEM_BYTES),
    )(*in_hbm(x), tissue, probe, after)


def units_kernel(n, x_ref, tissue_ref, after_ref, unit0_ref, unit1_ref, tile_ref, sems):
    rows, cols, patch, width = x_ref.shape
    chosen = [(row, c) for row in range(rows) for c in range(cols)]
    copies = fetched([x_ref.at[row, c] for row, c in chosen], [tile_ref.at[i] for i in range(len(chosen))], sems)
    masks = [by_sublane(tissue_ref[row]).astype(bf16) for row in range(rows)]
    for i, (row, c) in enumerate(chosen):
        copies[i].wait()
        unit, _ = unit_and_mask(tile_ref[i])
        at = (GHOST + c) * patch
        (unit0_ref, unit1_ref)[row][at : at + patch, :] = unit * masks[row][:, c : c + 1]


def own_units(x, tissue, after):
    rows, cols, patch, width = x.shape
    n = cols + 2 * GHOST
    unit = sds((n * patch, width), bf16)
    return pl.pallas_call(
        functools.partial(units_kernel, n),
        in_specs=[HBM_SPEC, VMEM_SPEC, ANY_SPEC],
        out_specs=[VMEM_SPEC] * 2,
        out_shape=(unit, unit),
        scratch_shapes=[pltpu.VMEM((rows * cols, patch, width), bf16), pltpu.SemaphoreType.DMA((rows * cols,))],
        compiler_params=pltpu.CompilerParams(vmem_limit_bytes=VMEM_BYTES),
    )(*in_hbm(x), tissue, after)


def bands(ranges, patch, unit0_ref, unit1_ref, m_ref, degree, diagonal):
    both = 2 * patch
    shape = (both, 3 * both)
    patch_of = iota(shape, 0)
    own = iota(shape, 1) == jnp.where(patch_of < patch, patch_of + patch, patch_of + 3 * patch)
    lane = iota((both, 128), 1)

    def band(e, carry):
        degree, diagonal = carry
        around = slice((e - 1) * patch, (e + 2) * patch)
        here = slice(e * patch, (e + 1) * patch)
        left = jnp.concatenate([unit0_ref[here, :], unit1_ref[here, :]], axis=0)
        right = jnp.concatenate([unit0_ref[around, :], unit1_ref[around, :]], axis=0)
        weights = affinity_of(left, right)
        others = jnp.where(own, 0.0, weights)
        m_ref[e] = others.astype(bf16)
        itself = jnp.sum(weights - others, axis=1, keepdims=True)
        degree = at_lane(lane, e, jnp.sum(weights, axis=1, keepdims=True), degree)
        diagonal = at_lane(lane, e, itself, diagonal)
        return degree, diagonal

    carry = (degree, diagonal)
    for low, high in ranges:
        for e in range(low, high):
            carry = band(e, carry)
    return carry


def inside_kernel(n, unit0_ref, unit1_ref, m_ref, sum_ref):
    patch = m_ref.shape[1] // 2
    empty = jnp.zeros((2 * patch, 128), f32)
    sum_ref[0], sum_ref[1] = bands([(GHOST + 1, n - GHOST - 1)], patch, unit0_ref, unit1_ref, m_ref, empty, empty)


def inside_affinity(unit0, unit1, patch):
    n = unit0.shape[0] // patch
    both = 2 * patch
    return pl.pallas_call(
        functools.partial(inside_kernel, n),
        out_shape=(sds((n, both, 3 * both), bf16), sds((2, both, 128), f32)),
        compiler_params=pltpu.CompilerParams(vmem_limit_bytes=VMEM_BYTES),
    )(unit0, unit1)


def outside_kernel(
    n,
    start0_ref, start1_ref, some_ref, tissue_ref, sum_ref, xl_ref, p_ref, xr_ref, after_ref,
    unit0_ref, unit1_ref, m_ref, stat_ref, pay_ref, pl_ref, pr_ref,
):
    rows, count, patch, _ = xl_ref.shape
    width = unit0_ref.shape[1]
    cols = n - 2 * count
    both = rows * patch
    lane = iota((patch, 128), 1)

    masks = []
    for row, unit_ref in ((0, unit0_ref), (1, unit1_ref)):
        own_mask = by_sublane(tissue_ref[row])
        mask = jnp.zeros((patch, 128), f32)
        for e in range(n):
            if e < count:
                unit, column = unit_and_mask(xl_ref[row, e, :, :width])
            elif e < count + cols:
                unit, column = None, own_mask[:, e - count : e - count + 1]
            else:
                unit, column = unit_and_mask(xr_ref[row, e - count - cols, :, :width])
            mask = at_lane(lane, e, column, mask)
            if unit is not None:
                unit_ref[e * patch : (e + 1) * patch, :] = unit
        masks.append(mask)
    mask = jnp.concatenate(masks, axis=0)
    ranges = [(1, GHOST + 1), (n - GHOST - 1, n - 1)]
    degree, diagonal = bands(ranges, patch, unit0_ref, unit1_ref, m_ref, sum_ref[0], sum_ref[1])
    degree = degree - FLOOR * absent_near(mask, 3 * both)
    stat_ref[0] = degree
    stat_ref[1] = diagonal
    stat_ref[2] = mask
    half = patch // 2
    tail = (n - 2) * half
    for e in range(1, n - 1):
        pay_ref[(e - 1) * half : e * half, :] = packed(panel_at((xl_ref, p_ref, xr_ref), 0, e)).astype(bf16)
    pay_ref[tail : tail + patch, :], pay_ref[tail + patch :, :] = pair_of(degree[:patch])
    pl_ref[...] = xl_ref[:, :, :, width:]
    pr_ref[...] = xr_ref[:, :, :, width:]


def payload_rows(columns, patch):
    return columns * patch // 2 + 2 * patch


def outside_affinity(unit0, unit1, m, tissue, sums, panel, after):
    n, both, _ = m.shape
    payload = sds((payload_rows(n - 2, both // 2), 2 * RANK), bf16)
    side = sds(panel[0].shape[:3] + (2 * RANK,), bf16)
    unit = sds(unit0.shape, bf16)
    return pl.pallas_call(
        functools.partial(outside_kernel, n),
        in_specs=[VMEM_SPEC] * 8 + [ANY_SPEC],
        out_specs=[VMEM_SPEC] * 7,
        out_shape=(unit, unit, sds(m.shape, bf16), sds((3, both, 128), f32), payload, side, side),
        input_output_aliases={0: 0, 1: 1, 2: 2},
        compiler_params=pltpu.CompilerParams(vmem_limit_bytes=VMEM_BYTES),
    )(unit0, unit1, m, tissue, sums, *panel, after)


def cut_kernel(be_ref, after_ref, left_ref, right_ref):
    left_ref[...] = be_ref[:GHOST]
    right_ref[...] = be_ref[be_ref.shape[0] - GHOST :]


def cut(be, after):
    vmem = pl.BlockSpec(memory_space=pltpu.VMEM)
    side = sds((GHOST,) + be.shape[1:], be.dtype)
    return pl.pallas_call(
        cut_kernel,
        in_specs=[vmem, pl.BlockSpec(memory_space=pl.ANY)],
        out_specs=[vmem] * 2,
        out_shape=(side, side),
        compiler_params=pltpu.CompilerParams(vmem_limit_bytes=VMEM_BYTES),
    )(be, after)


def stages(n):
    middle = list(range(GHOST + EDGE, n - GHOST - EDGE))
    ends = [c for c in range(n) if c not in middle]
    arrived, seen, steps = set(), set(), []
    for tiles in (ends, middle):
        arrived |= set(tiles)
        columns = [e for e in range(1, n - 1) if {e - 1, e, e + 1} <= arrived and e not in seen]
        seen |= set(columns)
        steps.append((tiles, columns))
    return steps


def scale_of(stat_ref, sums):
    down_sum, _, mask = sums
    patch = mask.shape[0]
    degree = 1.0 + stat_ref[0, patch:] + down_sum - FLOOR * absent_near(mask, 3 * patch)
    return stat_ref[2, patch:] * lax.rsqrt(degree)


def pair_source(e, tiles):
    some = next(iter(tiles.values()))
    near = [tiles.get(c, jnp.zeros_like(some)) for c in range(e - 1, e + 3)]
    return jnp.concatenate(near, axis=0)


def pairs_of(columns):
    return sorted({e - (e + 1) % 2 for e in columns})


def pair_products(columns, block_ref, tiles):
    results = {}
    for e in pairs_of(columns):
        product = jnp.dot(block_ref[e // 2], pair_source(e, tiles), preferred_element_type=f32)
        patch = product.shape[0] // 2
        results[e], results[e + 1] = product[:patch], product[patch:]
    return results


def products(columns, up_ref, tiles, pay_ref, first):
    half = up_ref.shape[1] // 4
    results = pair_products(columns, up_ref, tiles)
    for e in columns:
        pay_ref[(e - first) * half : (e - first + 1) * half, :] = packed(results[e]).astype(bf16)


def cross_kernel(n, stage, *refs):
    steps = stages(n)
    tiles, columns = steps[stage]
    count = 3 if stage == 0 else 1
    pieces, (own_ref, stat_ref, pl_ref, p_ref, pr_ref) = refs[:count], refs[count : count + 5]
    refs = refs[count + 5 :]
    patch = pieces[0].shape[1]
    lane = iota((patch, 128), 1)
    if stage == 0:
        v_ref, w_ref, sum_ref, u0_ref, pay_ref, unit_ref = refs
        empty = jnp.zeros((patch, 128), f32)
        down_sum, up_sum, mask = empty, empty, empty
    else:
        before, (v_ref, w_ref, sum_ref, u0_ref, pay_ref, unit_ref) = refs[:6], refs[6:12]
        down_sum, up_sum, mask = (before[2][i] for i in range(3))
    sources = [(ref, i) for ref in pieces for i in range(ref.shape[0])]
    for c, (ref, i) in zip(tiles, sources):
        unit, column = unit_and_mask(ref[i])
        unit_ref[c * patch : (c + 1) * patch, :] = unit
        mask = at_lane(lane, c, column, mask)
    shape = (2 * patch, 4 * patch)
    apart = iota(shape, 1) // patch - iota(shape, 0) // patch
    beside = (apart >= 0) & (apart <= 2)
    for e in pairs_of(columns):
        around = slice((e - 1) * patch, (e + 3) * patch)
        here = slice(e * patch, (e + 2) * patch)
        down = jnp.where(beside, affinity_of(own_ref[here, :], unit_ref[around, :]), 0.0)
        up = jnp.where(beside, affinity_of(unit_ref[here, :], own_ref[around, :]), 0.0)
        v_ref[e // 2] = down.astype(bf16)
        w_ref[e // 2] = up.astype(bf16)
        down = jnp.sum(down, axis=1, keepdims=True)
        up = jnp.sum(up, axis=1, keepdims=True)
        for i in range(2):
            span = slice(i * patch, (i + 1) * patch)
            down_sum = at_lane(lane, e + i, down[span], down_sum)
            up_sum = at_lane(lane, e + i, up[span], up_sum)
    sums = (down_sum, up_sum, mask)
    scale = scale_of(stat_ref, sums)
    for e in columns:
        u0_ref[e] = (scale[:, e : e + 1] * panel_at((pl_ref, p_ref, pr_ref), 1, e)).astype(bf16)
    inner, known = [], []
    for last in (stage - 1, stage):
        known = [e for _, reached in steps[: last + 1] for e in reached]
        inner.append({e for e in range(2, n - 2) if {e - 1, e, e + 1} <= set(known)})
    fresh = sorted(inner[1] - inner[0])
    near = {c for e in fresh for c in (e - 1, e, e + 1)}
    products(fresh, w_ref, {e: u0_ref[e] for e in near}, pay_ref, 2)
    if stage < len(steps) - 1:
        for i in range(3):
            sum_ref[i] = sums[i]
        return
    shared = up_sum - FLOOR * absent_near(stat_ref[2, patch:], 3 * patch)
    sum_ref[0], sum_ref[1], sum_ref[2] = shared, mask, scale
    tail = (n - 4) * patch // 2
    pay_ref[tail : tail + patch, :], pay_ref[tail + patch :, :] = pair_of(shared)


def cross_affinity(stage, pieces, u1, stat, panel, before=()):
    patch, width = pieces[0].shape[1:]
    n = u1.shape[0] // patch
    given = len(pieces) + 5
    return pl.pallas_call(
        functools.partial(cross_kernel, n, stage),
        out_shape=(
            sds((n // 2 - 1, 2 * patch, 4 * patch), bf16),
            sds((n // 2 - 1, 2 * patch, 4 * patch), bf16),
            sds((3, patch, 128), f32),
            sds((n, patch, RANK), bf16),
            sds((payload_rows(n - 4, patch), 2 * RANK), bf16),
            sds((n * patch, width), bf16),
        ),
        input_output_aliases={given + i: i for i in range(len(before))},
        compiler_params=pltpu.CompilerParams(vmem_limit_bytes=VMEM_BYTES),
    )(*pieces, u1, stat, *panel, *before)


def before_first_kernel(n, got_ref, sum_ref, stat_ref, u0_ref, m_ref, v_ref, z_ref, t_ref, gain_ref, own_ref, u2_ref):
    patch = u0_ref.shape[1]
    half = patch // 2
    tail = (n - 2) * half
    partial = got_ref[tail : tail + patch, :].astype(f32) + got_ref[tail + patch :, :].astype(f32)
    below_scale = sum_ref[1] * lax.rsqrt(1.0 + partial + sum_ref[0])
    scale = sum_ref[2]
    gain = 1.0 + scale * scale * stat_ref[1, patch:]
    upper = stat_ref[1, :patch]
    for e in range(1, n - 1):
        theirs = unpacked(got_ref[(e - 1) * half : e * half, :].astype(f32))
        u2_ref[e] = (below_scale[:, e : e + 1] * theirs).astype(bf16)
    lower = pair_products(range(2, n - 2), v_ref, {e: u2_ref[e] for e in range(1, n - 1)})
    for e in range(2, n - 2):
        own = u0_ref[e - 1 : e + 2].reshape(3 * patch, RANK)
        total = jnp.dot(m_ref[e, :, 3 * patch :], own, preferred_element_type=f32)
        z_ref[e, :patch] = total[:patch]
        z_ref[e, patch:] = total[patch:] + lower[e]
        for ref, table in ((t_ref, scale), (gain_ref, gain), (own_ref, upper)):
            ref[e] = jnp.broadcast_to(table[:, e : e + 1], (patch, RANK))


def before_first(got, sums, stat, u0, m, v):
    n, patch, _ = u0.shape
    spread = sds((n, patch, RANK), f32)
    return kernel_call(
        functools.partial(before_first_kernel, n),
        (sds((n, 2 * patch, RANK), f32), spread, spread, spread),
        [pltpu.VMEM((n, patch, RANK), bf16)],
    )(got, sums, stat, u0, m, v)


def first_kernel(
    n,
    got_ref, stat_ref, t1_ref, gain1_ref, own_ref, z_ref, pl_ref, p_ref, pr_ref, m_ref, w_ref,
    y_ref, u_ref, t0_ref, gain0_ref, up_ref, down_ref,
    start_ref,
):
    panel = (pl_ref, p_ref, pr_ref)
    patch = t1_ref.shape[1]
    half = patch // 2
    tail = (n - 4) * half
    partial = got_ref[tail : tail + patch, :].astype(f32) + got_ref[tail + patch :, :].astype(f32)
    scale = stat_ref[2, :patch] * lax.rsqrt(1.0 + stat_ref[0, :patch] + partial)
    for e in range(1, n - 1):
        t = jnp.broadcast_to(scale[:, e : e + 1], (patch, RANK))
        t0_ref[e] = t
        start_ref[e] = (t * panel_at(panel, 0, e)).astype(bf16)
    for e in range(2, n - 2):
        own = start_ref[e - 1 : e + 2].reshape(3 * patch, RANK)
        total = z_ref[e] + jnp.dot(m_ref[e, :, : 3 * patch], own, preferred_element_type=f32)
        upper = total[:patch] + unpacked(got_ref[(e - 2) * half : (e - 1) * half, :].astype(f32))
        gain = 1.0 + t0_ref[e] * t0_ref[e] * own_ref[e]
        gain0_ref[e] = gain
        for row, piece, t, g in ((0, upper, t0_ref[e], gain), (1, total[patch:], t1_ref[e], gain1_ref[e])):
            image = panel_at(panel, row, e) * g + t * piece
            y_ref[row, e] = image
            scaled = t * image
            u_ref[row, e] = scaled.astype(bf16)
            if row == 0:
                up_ref[(e - 2) * half : (e - 1) * half, :] = packed(scaled).astype(bf16)
    products(range(3, n - 3), w_ref, {e: u_ref[1, e] for e in range(2, n - 2)}, down_ref, 3)


def first_iteration(got, stat, t1, gain1, own, z, panel, m, w):
    n, both, _ = z.shape
    patch = both // 2
    half = patch // 2
    spread = sds((n, patch, RANK), f32)
    return kernel_call(
        functools.partial(first_kernel, n),
        (
            sds((2, n, patch, RANK), f32),
            sds((2, n, patch, RANK), bf16),
            spread,
            spread,
            sds(((n - 4) * half, 2 * RANK), bf16),
            sds(((n - 6) * half, 2 * RANK), bf16),
        ),
        [pltpu.VMEM((n, patch, RANK), bf16)],
    )(got, stat, t1, gain1, own, z, *panel, m, w)


def local_kernel(low, high, m_ref, u_ref, z_ref):
    patch = u_ref.shape[2]
    for e in range(low, high):
        upper = u_ref[0, e - 1 : e + 2].reshape(3 * patch, RANK)
        lower = u_ref[1, e - 1 : e + 2].reshape(3 * patch, RANK)
        z_ref[e] = jnp.dot(m_ref[e], jnp.concatenate([upper, lower], axis=0), preferred_element_type=f32)


def local_products(low, high, m, u):
    n, both, _ = m.shape
    return kernel_call(
        functools.partial(local_kernel, low, high),
        sds((n, both, RANK), f32),
    )(m, u)


def joined(e, low, lower, z_ref, above_ref, y_ref, scales, gains):
    patch = y_ref.shape[2]
    half = patch // 2
    upper = unpacked(above_ref[(e - low) * half : (e - low + 1) * half, :].astype(f32))
    pieces = (z_ref[e, :patch] + upper, z_ref[e, patch:] + lower[e])
    return [y_ref[row, e] * gains[row][e] + scales[row][e] * pieces[row] for row in range(2)]


def halo(n, low, half, below_ref):
    return {
        e: unpacked(below_ref[(e - low + 1) * half : (e - low + 2) * half, :]) for e in range(low - 1, n - low + 1)
    }


def middle_step_kernel(
    n, low,
    below_ref, above_ref, z_ref, y_ref, t0_ref, t1_ref, gain0_ref, gain1_ref, v_ref, w_ref,
    new_ref, u_ref, up_ref, down_ref,
):
    patch = y_ref.shape[2]
    half = patch // 2
    scales, gains = (t0_ref, t1_ref), (gain0_ref, gain1_ref)
    lower = pair_products(range(low, n - low), v_ref, halo(n, low, half, below_ref))
    for e in range(low, n - low):
        images = joined(e, low, lower, z_ref, above_ref, y_ref, scales, gains)
        for row in range(2):
            new_ref[row, e] = images[row]
            scaled = scales[row][e] * images[row]
            u_ref[row, e] = scaled.astype(bf16)
            if row == 0:
                up_ref[(e - low) * half : (e - low + 1) * half, :] = packed(scaled).astype(bf16)
    products(
        range(low + 1, n - low - 1), w_ref, {e: u_ref[1, e] for e in range(low, n - low)}, down_ref, low + 1
    )


def middle_step(low, below, above, z, y, spread, v, w):
    _, n, patch, _ = y.shape
    half = patch // 2
    return kernel_call(
        functools.partial(middle_step_kernel, n, low),
        (
            sds((2, n, patch, RANK), f32),
            sds((2, n, patch, RANK), bf16),
            sds(((n - 2 * low) * half, 2 * RANK), bf16),
            sds(((n - 2 * low - 2) * half, 2 * RANK), bf16),
        ),
    )(below, above, z, y, *spread, v, w)


def last_step_kernel(
    n, low,
    below_ref, above_ref, z_ref, y_ref, t0_ref, t1_ref, gain0_ref, gain1_ref, v_ref,
    new_ref, gram_ref, side_ref,
):
    patch = y_ref.shape[2]
    scales, gains = (t0_ref, t1_ref), (gain0_ref, gain1_ref)
    lower = pair_products(range(low, n - low), v_ref, halo(n, low, patch // 2, below_ref))
    wide = 2 * RANK
    for e in range(low, n - low):
        images = joined(e, low, lower, z_ref, above_ref, y_ref, scales, gains)
        for row in range(2):
            new_ref[row, e - low] = images[row]
        span = slice((e - low) * patch, (e - low + 1) * patch)
        side_ref[span, :wide], side_ref[span, wide:] = pair_of(jnp.concatenate(images, axis=1))
    side = side_ref[...]
    gram = lax.dot_general(side, side, ATB, preferred_element_type=f32)
    gram = gram[:wide] + gram[wide:]
    gram = gram[:, :wide] + gram[:, wide:]
    gram_ref[...] = packed(gram[:RANK, :RANK] + gram[RANK:, RANK:])


def last_step(low, below, above, z, y, spread, v):
    _, n, patch, _ = y.shape
    cols = n - 2 * low
    return kernel_call(
        functools.partial(last_step_kernel, n, low),
        (sds((2, cols, patch, RANK), f32), sds((RANK // 2, 2 * RANK), f32)),
        [pltpu.VMEM((cols * patch, 4 * RANK), bf16)],
    )(below, above, z, y, *spread, v)


def inverse_factor(gram):
    size = gram.shape[0]
    step = 8
    row = iota((size, 2 * size), 0)
    lane = iota((size, 2 * size), 1)
    table = jnp.concatenate([gram, identity(size).astype(f32)], axis=1)
    for k in range(0, size, step):
        cols = [jnp.broadcast_to(table[:, k + i : k + i + 1], table.shape) for i in range(step)]
        lines = [table[k + i : k + i + 1, :] for i in range(step)]
        for i in range(step):
            inverse = 1.0 / cols[i][k + i : k + i + 1, :]
            for j in range(i + 1, step):
                lines[j] = lines[j] - lines[i] * (cols[i][k + j : k + j + 1, :] * inverse)
                cols[j] = cols[j] - cols[i] * (cols[j][k + i : k + i + 1, :] * inverse)
            table = table - jnp.where(row > k + i, cols[i], 0.0) * (lines[i] * inverse)
    pivots = jnp.sum(jnp.where(row == lane, table, 0.0), axis=1, keepdims=True)
    return table[:, size:] * lax.rsqrt(pivots)


def finish_kernel(factor, count, *refs):
    parts, y_ref, out_ref = refs[:count], refs[count], refs[count + 1]
    total = parts[0][...]
    for part in parts[1:]:
        total = total + part[...]
    inverse = factor * inverse_factor(unpacked(total))
    zero = jnp.zeros_like(inverse)
    both = jnp.concatenate(
        [jnp.concatenate([inverse, zero], axis=1), jnp.concatenate([zero, inverse], axis=1)], axis=0
    )
    wide = 2 * RANK
    tiles, width = y_ref.shape
    pieces = [y_ref[:, q * wide : (q + 1) * wide] for q in range(width // wide)]
    y_high, y_low = pair_of(jnp.concatenate(pieces, axis=0))
    t_high, t_low = pair_of(both)

    def times(a, b):
        return lax.dot_general(a, b, ABT, preferred_element_type=f32)

    out = times(y_high, t_high) + (times(y_low, t_high) + times(y_high, t_low))
    for q in range(width // wide):
        out_ref[:, q * wide : (q + 1) * wide] = out[q * tiles : (q + 1) * tiles]


def finish(factor, parts, y):
    return kernel_call(
        functools.partial(finish_kernel, factor, len(parts)),
        sds(y.shape, f32),
    )(*parts, y)


def exchange_stages():
    stages = []
    for axis in ("col", "row"):
        size = lax.axis_size(axis)
        bit = 1
        if axis == "col":
            stages.append((axis, size, [1]))
            bit = 2
        while bit < size:
            if 2 * bit < size:
                stages.append((axis, size, [bit, 2 * bit, 3 * bit]))
                bit *= 4
            else:
                stages.append((axis, size, [bit]))
                bit *= 2
    return stages


def summed_parts(gram):
    stages = exchange_stages()
    for place, (axis, size, partners) in enumerate(stages):
        parts = [gram] + [
            lax.ppermute(gram, axis, [(i, i ^ p) for i in range(size)]) for p in partners
        ]
        if place == len(stages) - 1:
            return parts
        gram = parts[0]
        for part in parts[1:]:
            gram = gram + part


def passed_along(shard, axis, by):
    count = lax.axis_size(axis)
    pairs = [(i, i + by) for i in range(count) if 0 <= i + by < count]
    return lax.ppermute(shard, axis, pairs)


def local(features, tissue, probe):
    tile_rows, tile_cols, patches, width = features.shape
    edges = mark_edges(features, tissue)
    below_edges = passed_along(edges, "row", -1)
    own_panel = probe.reshape(tile_rows, tile_cols, patches, RANK)
    left_end, right_end, middle = mark_rest(features, tissue, own_panel, edges)
    from_left = passed_along(right_end, "col", 1)
    from_right = passed_along(left_end, "col", -1)
    below_middle = passed_along(middle, "row", -1)
    unit0, unit1 = own_units(features, tissue, left_end)
    m, sums = inside_affinity(unit0, unit1, patches)
    below_left, below_right = cut(below_edges, sums)
    panel = (from_left, own_panel, from_right)
    _, u1, m, stat, payload, *sides = outside_affinity(unit0, unit1, m, tissue, sums, panel, below_left)
    panel = (sides[0], own_panel, sides[1])
    below_left, below_right = passed_along(below_right, "col", 1), passed_along(below_left, "col", -1)
    got_below = passed_along(payload, "row", -1)
    n = tile_cols + 2 * GHOST
    cross = cross_affinity(0, (below_left, below_edges, below_right), u1, stat, panel)
    v, w, sums, u0, payload, _ = cross_affinity(1, (below_middle,), u1, stat, panel, cross)
    got_above = passed_along(payload, "row", 1)
    z, t1, gain1, own = before_first(got_below, sums, stat, u0, m, v)
    y, u, t0, gain0, up, down = first_iteration(got_above, stat, t1, gain1, own, z, panel, m, w)
    spread = (t0, t1, gain0, gain1)
    below, above = passed_along(up, "row", -1), passed_along(down, "row", 1)
    z = local_products(3, n - 3, m, u)
    y, u, up, down = middle_step(3, below, above, z, y, spread, v, w)
    below, above = passed_along(up, "row", -1), passed_along(down, "row", 1)
    z = local_products(4, n - 4, m, u)
    y, gram = last_step(4, below, above, z, y, spread, v)

    parts = summed_parts(gram)
    flat = y.reshape(tile_rows * tile_cols, patches * RANK)
    total = tile_rows * lax.axis_size("row") * tile_cols * lax.axis_size("col") * patches
    out = finish(math.sqrt(float(total)), parts, flat)
    return out.reshape(tile_rows, tile_cols, patches * RANK)


def solution(mesh):
    placed = (P("row", "col", None, None), P("row", "col", None), P("row", "col", None))
    return jax.shard_map(
        local, mesh=mesh, in_specs=placed, out_specs=P("row", "col", None), check_vma=False
    )
```

```python
import functools
import math

import jax
import jax.numpy as jnp
from jax import lax
from jax.experimental import pallas as pl
from jax.experimental.pallas import tpu as pltpu
from jax.sharding import PartitionSpec as P

RANK = 64
ITERS = 3
AFFINITY_TEMP = 4.0

GHOST = ITERS + 1
EDGE = 4
TINY = 1e-30
VMEM_BYTES = 16 * 1024 * 1024
FLOOR = math.exp(-AFFINITY_TEMP)
ABT = (((1,), (1,)), ((), ()))
ATB = (((0,), (0,)), ((), ()))

f32 = jnp.float32
bf16 = jnp.bfloat16


def kernel_call(body, out_shape, scratch=()):
    return pl.pallas_call(
        body,
        out_shape=out_shape,
        scratch_shapes=list(scratch),
        compiler_params=pltpu.CompilerParams(vmem_limit_bytes=VMEM_BYTES),
    )


def sds(shape, dtype):
    return jax.ShapeDtypeStruct(shape, dtype)


def iota(shape, dim):
    return lax.broadcasted_iota(jnp.int32, shape, dim)


def identity(n):
    return iota((n, n), 0) == iota((n, n), 1)


def unit_and_mask(block):
    values = block.astype(f32)
    scaled = values * lax.rsqrt(jnp.sum(values * values, axis=-1, keepdims=True) + 1e-06)
    return scaled.astype(bf16), (values[:, :1] != 0.0).astype(f32)


def affinity_of(left, right):
    scores = lax.dot_general(left, right, ABT, preferred_element_type=f32)
    return jnp.exp(AFFINITY_TEMP * scores - AFFINITY_TEMP)


def at_lane(lane, e, column, table):
    return jnp.where(lane == e, column, table)


def absent_near(mask, width):
    count = jnp.sum(mask, axis=0, keepdims=True)
    return width - (pltpu.roll(count, 1, 1) + count + pltpu.roll(count, 127, 1))


def packed(block):
    half = block.shape[0] // 2
    return jnp.concatenate([block[:half], block[half:]], axis=1)


def unpacked(block):
    return jnp.concatenate([block[:, :RANK], block[:, RANK:]], axis=0)


def pair_of(values):
    high = values.astype(bf16)
    return high, (values - high.astype(f32)).astype(bf16)


def four_of(values):
    high, middle = pair_of(values)
    low = (values - high.astype(f32) - middle.astype(f32)).astype(bf16)
    return jnp.concatenate([high, middle, low, jnp.zeros_like(low)], axis=1)


def whole_of(parts):
    parts = parts.astype(f32)
    return parts[:, :RANK] + parts[:, RANK : 2 * RANK] + parts[:, 2 * RANK : 3 * RANK]


def by_sublane(tissue):
    mask = (tissue != 0).astype(bf16)
    return lax.dot_general(mask, identity(mask.shape[0]).astype(bf16), ATB, preferred_element_type=f32)


def marked(tile, column):
    zero = (iota(tile.shape, 1) == 0) & (tile == 0)
    return jnp.where(zero, jnp.asarray(TINY, bf16), tile) * column.astype(bf16)


def fetched(sources, slots, sems):
    copies = [pltpu.make_async_copy(source, slot, sems.at[i]) for i, (source, slot) in enumerate(zip(sources, slots))]
    for copy in copies:
        copy.start()
    return copies


def in_hbm(*arrays):
    return tuple(pltpu.with_memory_space_constraint(array, pltpu.HBM) for array in arrays)


VMEM_SPEC = pl.BlockSpec(memory_space=pltpu.VMEM)
HBM_SPEC = pl.BlockSpec(memory_space=pltpu.HBM)
ANY_SPEC = pl.BlockSpec(memory_space=pl.ANY)


def folded_gram(side):
    wide = 2 * RANK
    gram = lax.dot_general(side, side, ATB, preferred_element_type=f32)
    gram = gram[:wide] + gram[wide:]
    gram = gram[:, :wide] + gram[:, wide:]
    return packed(gram[:RANK, :RANK] + gram[RANK:, RANK:])


def start_gram_kernel(probe_ref, gram_ref, flat_ref, sems):
    rows, cols, width = probe_ref.shape
    (copy,) = fetched([probe_ref], [flat_ref], sems)
    copy.wait()
    wide = 2 * RANK
    spans = [slice(q * wide, (q + 1) * wide) for q in range(width // wide)]
    side = jnp.concatenate([flat_ref[row, :, span] for row in range(rows) for span in spans], axis=0)
    gram_ref[...] = folded_gram(jnp.concatenate(pair_of(side), axis=1))


def start_gram(probe):
    return pl.pallas_call(
        start_gram_kernel,
        in_specs=[HBM_SPEC],
        out_specs=VMEM_SPEC,
        out_shape=sds((RANK // 2, 2 * RANK), f32),
        scratch_shapes=[pltpu.VMEM(probe.shape, f32), pltpu.SemaphoreType.DMA((1,))],
        compiler_params=pltpu.CompilerParams(vmem_limit_bytes=VMEM_BYTES),
    )(*in_hbm(probe))


def mark_edges_kernel(x_ref, tissue_ref, edge_ref, tile_ref, mask_ref, sems):
    cols = x_ref.shape[1]
    sources = [tissue_ref.at[0], x_ref.at[0, :EDGE], x_ref.at[0, cols - EDGE :]]
    copies = fetched(sources, [mask_ref, tile_ref.at[:EDGE], tile_ref.at[EDGE:]], sems)
    copies[0].wait()
    mask = by_sublane(mask_ref[...])
    for side, first in ((0, 0), (1, cols - EDGE)):
        copies[1 + side].wait()
        for i in range(EDGE):
            at = side * EDGE + i
            edge_ref[at] = marked(tile_ref[at], mask[:, first + i : first + i + 1])


def mark_edges(x, tissue):
    rows, cols, patch, width = x.shape
    shape = (2 * EDGE, patch, width)
    return pl.pallas_call(
        mark_edges_kernel,
        in_specs=[HBM_SPEC, HBM_SPEC],
        out_specs=VMEM_SPEC,
        out_shape=sds(shape, bf16),
        scratch_shapes=[
            pltpu.VMEM(shape, bf16),
            pltpu.VMEM((cols, patch), jnp.int32),
            pltpu.SemaphoreType.DMA((3,)),
        ],
        compiler_params=pltpu.CompilerParams(vmem_limit_bytes=VMEM_BYTES),
    )(*in_hbm(x, tissue))


def gate_kernel(count, *refs):
    for x_ref, out_ref in zip(refs[:count], refs[len(refs) - count :]):
        out_ref[...] = x_ref[...]


def gate(arrays, after):
    count = len(arrays)
    return pl.pallas_call(
        functools.partial(gate_kernel, count),
        in_specs=[VMEM_SPEC] * count + [ANY_SPEC] * len(after),
        out_specs=[VMEM_SPEC] * count,
        out_shape=tuple(sds(x.shape, x.dtype) for x in arrays),
        input_output_aliases={i: i for i in range(count)},
        compiler_params=pltpu.CompilerParams(vmem_limit_bytes=VMEM_BYTES),
    )(*arrays, *after)


def units_kernel(
    x_ref, tissue_ref, probe_ref, after_ref,
    left_ref, right_ref, middle_ref, unit0_ref, unit1_ref,
    tile_ref, sems,
):
    rows, cols, patch, width = x_ref.shape
    run = GHOST
    order = [(row, c) for row in range(rows) for c in (0, cols - run)]
    order += [(row, c) for row in range(rows) for c in range(run, cols - run, run)]
    copies = fetched([x_ref.at[row, c : c + run] for row, c in order], [tile_ref.at[i] for i in range(len(order))], sems)
    masks = [by_sublane(tissue_ref[row]) for row in range(rows)]
    for i, (row, first) in enumerate(order):
        copies[i].wait()
        for k in range(run):
            c = first + k
            tile, column = tile_ref[i, k], masks[row][:, c : c + 1]
            unit, _ = unit_and_mask(tile)
            at = (GHOST + c) * patch
            (unit0_ref, unit1_ref)[row][at : at + patch, :] = unit * column.astype(bf16)
            if first == 0 or first == cols - run:
                side_ref = left_ref if first == 0 else right_ref
                side_ref[row, k, :, :width] = marked(tile, column)
                side_ref[row, k, :, width:] = four_of(probe_ref[row, c])
            if row == 0 and EDGE <= c < cols - EDGE:
                middle_ref[c - EDGE] = marked(tile, column)


def own_units(x, tissue, probe, after):
    rows, cols, patch, width = x.shape
    n = cols + 2 * GHOST
    side = sds((rows, GHOST, patch, width + 4 * RANK), bf16)
    unit = sds((n * patch, width), bf16)
    return pl.pallas_call(
        units_kernel,
        in_specs=[HBM_SPEC, VMEM_SPEC, VMEM_SPEC, ANY_SPEC],
        out_specs=[VMEM_SPEC] * 5,
        out_shape=(side, side, sds((cols - 2 * EDGE, patch, width), bf16), unit, unit),
        scratch_shapes=[
            pltpu.VMEM((rows * cols // GHOST, GHOST, patch, width), bf16),
            pltpu.SemaphoreType.DMA((rows * cols // GHOST,)),
        ],
        compiler_params=pltpu.CompilerParams(vmem_limit_bytes=VMEM_BYTES),
    )(*in_hbm(x), tissue, probe, after)


def bands(ranges, patch, unit0_ref, unit1_ref, m_ref, degree, diagonal):
    both = 2 * patch
    shape = (both, 3 * both)
    patch_of = iota(shape, 0)
    own = iota(shape, 1) == jnp.where(patch_of < patch, patch_of + patch, patch_of + 3 * patch)
    lane = iota((both, 128), 1)

    def band(e, carry):
        degree, diagonal = carry
        around = slice((e - 1) * patch, (e + 2) * patch)
        here = slice(e * patch, (e + 1) * patch)
        left = jnp.concatenate([unit0_ref[here, :], unit1_ref[here, :]], axis=0)
        right = jnp.concatenate([unit0_ref[around, :], unit1_ref[around, :]], axis=0)
        weights = affinity_of(left, right)
        others = jnp.where(own, 0.0, weights)
        m_ref[e] = others.astype(bf16)
        itself = jnp.sum(weights - others, axis=1, keepdims=True)
        degree = at_lane(lane, e, jnp.sum(weights, axis=1, keepdims=True), degree)
        diagonal = at_lane(lane, e, itself, diagonal)
        return degree, diagonal

    carry = (degree, diagonal)
    for low, high in ranges:
        for e in range(low, high):
            carry = band(e, carry)
    return carry


def inside_kernel(n, unit0_ref, unit1_ref, m_ref, sum_ref):
    patch = m_ref.shape[1] // 2
    empty = jnp.zeros((2 * patch, 128), f32)
    sum_ref[0], sum_ref[1] = bands([(GHOST + 1, n - GHOST - 1)], patch, unit0_ref, unit1_ref, m_ref, empty, empty)


def inside_affinity(unit0, unit1, patch):
    n = unit0.shape[0] // patch
    both = 2 * patch
    return pl.pallas_call(
        functools.partial(inside_kernel, n),
        out_shape=(sds((n, both, 3 * both), bf16), sds((2, both, 128), f32)),
        compiler_params=pltpu.CompilerParams(vmem_limit_bytes=VMEM_BYTES),
    )(unit0, unit1)


def outside_kernel(
    n,
    start0_ref, start1_ref, some_ref, tissue_ref, sum_ref, xl_ref, xr_ref, after_ref,
    unit0_ref, unit1_ref, m_ref, stat_ref,
):
    rows, count, patch, _ = xl_ref.shape
    width = unit0_ref.shape[1]
    cols = n - 2 * count
    both = rows * patch
    lane = iota((patch, 128), 1)

    kept = slice(count * patch, (count + cols) * patch)
    unit0_ref[kept, :] = start0_ref[kept, :]
    unit1_ref[kept, :] = start1_ref[kept, :]
    for e in range(count + 1, n - count - 1):
        m_ref[e] = some_ref[e]
    masks = []
    for row, unit_ref in ((0, unit0_ref), (1, unit1_ref)):
        own_mask = by_sublane(tissue_ref[row])
        mask = jnp.zeros((patch, 128), f32)
        for e in range(n):
            if e < count:
                unit, column = unit_and_mask(xl_ref[row, e, :, :width])
            elif e < count + cols:
                unit, column = None, own_mask[:, e - count : e - count + 1]
            else:
                unit, column = unit_and_mask(xr_ref[row, e - count - cols, :, :width])
            mask = at_lane(lane, e, column, mask)
            if unit is not None:
                unit_ref[e * patch : (e + 1) * patch, :] = unit
        masks.append(mask)
    mask = jnp.concatenate(masks, axis=0)
    ranges = [(1, GHOST + 1), (n - GHOST - 1, n - 1)]
    degree, diagonal = bands(ranges, patch, unit0_ref, unit1_ref, m_ref, sum_ref[0], sum_ref[1])
    degree = degree - FLOOR * absent_near(mask, 3 * both)
    stat_ref[0] = degree
    stat_ref[1] = diagonal
    stat_ref[2] = mask

def payload_rows(columns, patch):
    return columns * patch // 2 + 2 * patch


def outside_affinity(unit0, unit1, m, tissue, sums, xl, xr, after):
    n, both, _ = m.shape
    unit = sds(unit0.shape, bf16)
    return pl.pallas_call(
        functools.partial(outside_kernel, n),
        in_specs=[VMEM_SPEC] * 7 + [ANY_SPEC],
        out_specs=[VMEM_SPEC] * 4,
        out_shape=(unit, unit, sds(m.shape, bf16), sds((3, both, 128), f32)),
        input_output_aliases={0: 0, 1: 1, 2: 2},
        compiler_params=pltpu.CompilerParams(vmem_limit_bytes=VMEM_BYTES),
    )(unit0, unit1, m, tissue, sums, xl, xr, after)


def start_kernel(factor, count, *refs):
    parts, (stat_ref, xl_ref, p_ref, xr_ref, panel_ref, pay_ref) = refs[:count], refs[count:]
    rows, cols, patch, _ = p_ref.shape
    n = cols + 2 * GHOST
    half = patch // 2
    width = xl_ref.shape[3] - 4 * RANK
    inverse = factor * inverse_factor(unpacked(balanced([part[...] for part in parts])), True)
    for row in range(rows):
        tiles = [whole_of(xl_ref[row, c, :, width:]) for c in range(GHOST)]
        tiles += [p_ref[row, c] for c in range(cols)]
        tiles += [whole_of(xr_ref[row, c, :, width:]) for c in range(GHOST)]
        turned = lax.dot_general(
            jnp.concatenate(tiles, axis=0), inverse, ABT, precision=lax.Precision.HIGHEST, preferred_element_type=f32
        )
        for e in range(n):
            tile = turned[e * patch : (e + 1) * patch]
            panel_ref[row, e] = tile
            if row == 0 and 0 < e < n - 1:
                pay_ref[(e - 1) * half : e * half, :] = packed(tile).astype(bf16)
    tail = (n - 2) * half
    pay_ref[tail : tail + patch, :], pay_ref[tail + patch :, :] = pair_of(stat_ref[0, :patch])


def start_panel(factor, parts, stat, xl, own_panel, xr):
    rows, cols, patch, _ = own_panel.shape
    n = cols + 2 * GHOST
    return kernel_call(
        functools.partial(start_kernel, factor, len(parts)),
        (sds((rows, n, patch, RANK), f32), sds((payload_rows(n - 2, patch), 2 * RANK), bf16)),
    )(*parts, stat, xl, own_panel, xr)


def cut_kernel(be_ref, after_ref, left_ref, right_ref):
    left_ref[...] = be_ref[:GHOST]
    right_ref[...] = be_ref[be_ref.shape[0] - GHOST :]


def cut(be, after):
    vmem = pl.BlockSpec(memory_space=pltpu.VMEM)
    side = sds((GHOST,) + be.shape[1:], be.dtype)
    return pl.pallas_call(
        cut_kernel,
        in_specs=[vmem, pl.BlockSpec(memory_space=pl.ANY)],
        out_specs=[vmem] * 2,
        out_shape=(side, side),
        compiler_params=pltpu.CompilerParams(vmem_limit_bytes=VMEM_BYTES),
    )(be, after)


def stages(n):
    middle = list(range(GHOST + EDGE, n - GHOST - EDGE))
    ends = [c for c in range(n) if c not in middle]
    arrived, seen, steps = set(), set(), []
    for tiles in (ends, middle):
        arrived |= set(tiles)
        columns = [e for e in range(1, n - 1) if {e - 1, e, e + 1} <= arrived and e not in seen]
        seen |= set(columns)
        steps.append((tiles, columns))
    return steps


def scale_of(stat_ref, sums):
    down_sum, _, mask = sums
    patch = mask.shape[0]
    degree = 1.0 + stat_ref[0, patch:] + down_sum - FLOOR * absent_near(mask, 3 * patch)
    return stat_ref[2, patch:] * lax.rsqrt(degree)


def pair_source(e, tiles):
    some = next(iter(tiles.values()))
    near = [tiles.get(c, jnp.zeros_like(some)) for c in range(e - 1, e + 3)]
    return jnp.concatenate(near, axis=0)


def pairs_of(columns):
    return sorted({e - (e + 1) % 2 for e in columns})


def pair_products(columns, block_ref, tiles):
    results = {}
    for e in pairs_of(columns):
        product = jnp.dot(block_ref[e // 2], pair_source(e, tiles), preferred_element_type=f32)
        patch = product.shape[0] // 2
        results[e], results[e + 1] = product[:patch], product[patch:]
    return results


def products(columns, up_ref, tiles, pay_ref, first):
    half = up_ref.shape[1] // 4
    results = pair_products(columns, up_ref, tiles)
    for e in columns:
        pay_ref[(e - first) * half : (e - first + 1) * half, :] = packed(results[e]).astype(bf16)


def cross_kernel(n, stage, *refs):
    steps = stages(n)
    tiles, columns = steps[stage]
    count = 3 if stage == 0 else 1
    pieces, (own_ref, stat_ref, p_ref) = refs[:count], refs[count : count + 3]
    refs = refs[count + 3 :]
    patch = pieces[0].shape[1]
    lane = iota((patch, 128), 1)
    if stage == 0:
        v_ref, w_ref, sum_ref, u0_ref, pay_ref, unit_ref = refs
        empty = jnp.zeros((patch, 128), f32)
        down_sum, up_sum, mask = empty, empty, empty
    else:
        before, (v_ref, w_ref, sum_ref, u0_ref, pay_ref, unit_ref) = refs[:6], refs[6:12]
        down_sum, up_sum, mask = (before[2][i] for i in range(3))
        earlier = {e for _, reached in steps[:stage] for e in reached}
        for e in pairs_of(earlier):
            v_ref[e // 2] = before[0][e // 2]
            w_ref[e // 2] = before[1][e // 2]
        for e in sorted(earlier):
            u0_ref[e] = before[3][e]
        for e in sorted(e for e in earlier if e - 1 in earlier and e + 1 in earlier):
            span = slice((e - 2) * patch // 2, (e - 1) * patch // 2)
            pay_ref[span, :] = before[4][span, :]
        for c in sorted({c for e in columns for c in (e - 1, e, e + 1)} - set(tiles)):
            span = slice(c * patch, (c + 1) * patch)
            unit_ref[span, :] = before[5][span, :]
    sources = [(ref, i) for ref in pieces for i in range(ref.shape[0])]
    for c, (ref, i) in zip(tiles, sources):
        unit, column = unit_and_mask(ref[i])
        unit_ref[c * patch : (c + 1) * patch, :] = unit
        mask = at_lane(lane, c, column, mask)
    shape = (2 * patch, 4 * patch)
    apart = iota(shape, 1) // patch - iota(shape, 0) // patch
    beside = (apart >= 0) & (apart <= 2)
    for e in pairs_of(columns):
        around = slice((e - 1) * patch, (e + 3) * patch)
        here = slice(e * patch, (e + 2) * patch)
        down = jnp.where(beside, affinity_of(own_ref[here, :], unit_ref[around, :]), 0.0)
        up = jnp.where(beside, affinity_of(unit_ref[here, :], own_ref[around, :]), 0.0)
        v_ref[e // 2] = down.astype(bf16)
        w_ref[e // 2] = up.astype(bf16)
        down = jnp.sum(down, axis=1, keepdims=True)
        up = jnp.sum(up, axis=1, keepdims=True)
        for i in range(2):
            span = slice(i * patch, (i + 1) * patch)
            down_sum = at_lane(lane, e + i, down[span], down_sum)
            up_sum = at_lane(lane, e + i, up[span], up_sum)
    sums = (down_sum, up_sum, mask)
    scale = scale_of(stat_ref, sums)
    for e in columns:
        u0_ref[e] = (scale[:, e : e + 1] * p_ref[1, e]).astype(bf16)
    inner, known = [], []
    for last in (stage - 1, stage):
        known = [e for _, reached in steps[: last + 1] for e in reached]
        inner.append({e for e in range(2, n - 2) if {e - 1, e, e + 1} <= set(known)})
    fresh = sorted(inner[1] - inner[0])
    near = {c for e in fresh for c in (e - 1, e, e + 1)}
    products(fresh, w_ref, {e: u0_ref[e] for e in near}, pay_ref, 2)
    if stage < len(steps) - 1:
        for i in range(3):
            sum_ref[i] = sums[i]
        return
    shared = up_sum - FLOOR * absent_near(stat_ref[2, patch:], 3 * patch)
    sum_ref[0], sum_ref[1], sum_ref[2] = shared, mask, scale
    tail = (n - 4) * patch // 2
    pay_ref[tail : tail + patch, :], pay_ref[tail + patch :, :] = pair_of(shared)


def cross_affinity(stage, pieces, u1, stat, panel, before=()):
    patch, width = pieces[0].shape[1:]
    n = u1.shape[0] // patch
    given = len(pieces) + 3
    return pl.pallas_call(
        functools.partial(cross_kernel, n, stage),
        out_shape=(
            sds((n // 2 - 1, 2 * patch, 4 * patch), bf16),
            sds((n // 2 - 1, 2 * patch, 4 * patch), bf16),
            sds((3, patch, 128), f32),
            sds((n, patch, RANK), bf16),
            sds((payload_rows(n - 4, patch), 2 * RANK), bf16),
            sds((n * patch, width), bf16),
        ),
        input_output_aliases={given + i: i for i in range(len(before))},
        compiler_params=pltpu.CompilerParams(vmem_limit_bytes=VMEM_BYTES),
    )(*pieces, u1, stat, panel, *before)


def before_first_kernel(n, got_ref, sum_ref, stat_ref, u0_ref, m_ref, v_ref, z_ref, t_ref, gain_ref, own_ref, u2_ref):
    patch = u0_ref.shape[1]
    half = patch // 2
    tail = (n - 2) * half
    partial = got_ref[tail : tail + patch, :].astype(f32) + got_ref[tail + patch :, :].astype(f32)
    below_scale = sum_ref[1] * lax.rsqrt(1.0 + partial + sum_ref[0])
    scale = sum_ref[2]
    gain = 1.0 + scale * scale * stat_ref[1, patch:]
    upper = stat_ref[1, :patch]
    for e in range(1, n - 1):
        theirs = unpacked(got_ref[(e - 1) * half : e * half, :].astype(f32))
        u2_ref[e] = (below_scale[:, e : e + 1] * theirs).astype(bf16)
    lower = pair_products(range(2, n - 2), v_ref, {e: u2_ref[e] for e in range(1, n - 1)})
    for e in range(2, n - 2):
        own = u0_ref[e - 1 : e + 2].reshape(3 * patch, RANK)
        total = jnp.dot(m_ref[e, :, 3 * patch :], own, preferred_element_type=f32)
        z_ref[e, :patch] = total[:patch]
        z_ref[e, patch:] = total[patch:] + lower[e]
        for ref, table in ((t_ref, scale), (gain_ref, gain), (own_ref, upper)):
            ref[e] = jnp.broadcast_to(table[:, e : e + 1], (patch, RANK))


def before_first(got, sums, stat, u0, m, v):
    n, patch, _ = u0.shape
    spread = sds((n, patch, RANK), f32)
    return kernel_call(
        functools.partial(before_first_kernel, n),
        (sds((n, 2 * patch, RANK), f32), spread, spread, spread),
        [pltpu.VMEM((n, patch, RANK), bf16)],
    )(got, sums, stat, u0, m, v)


def first_kernel(
    n,
    got_ref, stat_ref, t1_ref, gain1_ref, own_ref, z_ref, p_ref, m_ref, w_ref,
    y_ref, u_ref, t0_ref, gain0_ref, up_ref, down_ref,
    start_ref,
):
    patch = t1_ref.shape[1]
    half = patch // 2
    tail = (n - 4) * half
    partial = got_ref[tail : tail + patch, :].astype(f32) + got_ref[tail + patch :, :].astype(f32)
    scale = stat_ref[2, :patch] * lax.rsqrt(1.0 + stat_ref[0, :patch] + partial)
    for e in range(1, n - 1):
        t = jnp.broadcast_to(scale[:, e : e + 1], (patch, RANK))
        t0_ref[e] = t
        start_ref[e] = (t * p_ref[0, e]).astype(bf16)
    for e in range(2, n - 2):
        own = start_ref[e - 1 : e + 2].reshape(3 * patch, RANK)
        total = z_ref[e] + jnp.dot(m_ref[e, :, : 3 * patch], own, preferred_element_type=f32)
        upper = total[:patch] + unpacked(got_ref[(e - 2) * half : (e - 1) * half, :].astype(f32))
        gain = 1.0 + t0_ref[e] * t0_ref[e] * own_ref[e]
        gain0_ref[e] = gain
        for row, piece, t, g in ((0, upper, t0_ref[e], gain), (1, total[patch:], t1_ref[e], gain1_ref[e])):
            image = p_ref[row, e] * g + t * piece
            y_ref[row, e] = image
            scaled = t * image
            u_ref[row, e] = scaled.astype(bf16)
            if row == 0:
                up_ref[(e - 2) * half : (e - 1) * half, :] = packed(scaled).astype(bf16)
    products(range(3, n - 3), w_ref, {e: u_ref[1, e] for e in range(2, n - 2)}, down_ref, 3)


def first_iteration(got, stat, t1, gain1, own, z, panel, m, w):
    n, both, _ = z.shape
    patch = both // 2
    half = patch // 2
    spread = sds((n, patch, RANK), f32)
    return kernel_call(
        functools.partial(first_kernel, n),
        (
            sds((2, n, patch, RANK), f32),
            sds((2, n, patch, RANK), bf16),
            spread,
            spread,
            sds(((n - 4) * half, 2 * RANK), bf16),
            sds(((n - 6) * half, 2 * RANK), bf16),
        ),
        [pltpu.VMEM((n, patch, RANK), bf16)],
    )(got, stat, t1, gain1, own, z, panel, m, w)


def local_kernel(low, high, m_ref, u_ref, z_ref):
    patch = u_ref.shape[2]
    for e in range(low, high):
        upper = u_ref[0, e - 1 : e + 2].reshape(3 * patch, RANK)
        lower = u_ref[1, e - 1 : e + 2].reshape(3 * patch, RANK)
        z_ref[e] = jnp.dot(m_ref[e], jnp.concatenate([upper, lower], axis=0), preferred_element_type=f32)


def local_products(low, high, m, u):
    n, both, _ = m.shape
    return kernel_call(
        functools.partial(local_kernel, low, high),
        sds((n, both, RANK), f32),
    )(m, u)


def joined(e, low, lower, z_ref, above_ref, y_ref, scales, gains):
    patch = y_ref.shape[2]
    half = patch // 2
    upper = unpacked(above_ref[(e - low) * half : (e - low + 1) * half, :].astype(f32))
    pieces = (z_ref[e, :patch] + upper, z_ref[e, patch:] + lower[e])
    return [y_ref[row, e] * gains[row][e] + scales[row][e] * pieces[row] for row in range(2)]


def halo(n, low, half, below_ref):
    return {
        e: unpacked(below_ref[(e - low + 1) * half : (e - low + 2) * half, :]) for e in range(low - 1, n - low + 1)
    }


def middle_step_kernel(
    n, low,
    below_ref, above_ref, z_ref, y_ref, t0_ref, t1_ref, gain0_ref, gain1_ref, v_ref, w_ref,
    new_ref, u_ref, up_ref, down_ref,
):
    patch = y_ref.shape[2]
    half = patch // 2
    scales, gains = (t0_ref, t1_ref), (gain0_ref, gain1_ref)
    lower = pair_products(range(low, n - low), v_ref, halo(n, low, half, below_ref))
    for e in range(low, n - low):
        images = joined(e, low, lower, z_ref, above_ref, y_ref, scales, gains)
        for row in range(2):
            new_ref[row, e] = images[row]
            scaled = scales[row][e] * images[row]
            u_ref[row, e] = scaled.astype(bf16)
            if row == 0:
                up_ref[(e - low) * half : (e - low + 1) * half, :] = packed(scaled).astype(bf16)
    products(
        range(low + 1, n - low - 1), w_ref, {e: u_ref[1, e] for e in range(low, n - low)}, down_ref, low + 1
    )


def middle_step(low, below, above, z, y, spread, v, w):
    _, n, patch, _ = y.shape
    half = patch // 2
    return kernel_call(
        functools.partial(middle_step_kernel, n, low),
        (
            sds((2, n, patch, RANK), f32),
            sds((2, n, patch, RANK), bf16),
            sds(((n - 2 * low) * half, 2 * RANK), bf16),
            sds(((n - 2 * low - 2) * half, 2 * RANK), bf16),
        ),
    )(below, above, z, y, *spread, v, w)


def last_step_kernel(
    n, low,
    below_ref, above_ref, z_ref, y_ref, t0_ref, t1_ref, gain0_ref, gain1_ref, v_ref,
    new_ref, gram_ref, side_ref,
):
    patch = y_ref.shape[2]
    scales, gains = (t0_ref, t1_ref), (gain0_ref, gain1_ref)
    lower = pair_products(range(low, n - low), v_ref, halo(n, low, patch // 2, below_ref))
    wide = 2 * RANK
    for e in range(low, n - low):
        images = joined(e, low, lower, z_ref, above_ref, y_ref, scales, gains)
        for row in range(2):
            new_ref[row, e - low] = images[row]
        span = slice((e - low) * patch, (e - low + 1) * patch)
        side_ref[span, :wide], side_ref[span, wide:] = pair_of(jnp.concatenate(images, axis=1))
    gram_ref[...] = folded_gram(side_ref[...])


def last_step(low, below, above, z, y, spread, v):
    _, n, patch, _ = y.shape
    cols = n - 2 * low
    return kernel_call(
        functools.partial(last_step_kernel, n, low),
        (sds((2, cols, patch, RANK), f32), sds((RANK // 2, 2 * RANK), f32)),
        [pltpu.VMEM((cols * patch, 4 * RANK), bf16)],
    )(below, above, z, y, *spread, v)


def inverse_factor(gram, bounded=False):
    size = gram.shape[0]
    least = 0.0
    if bounded:
        least = 1e-6 * jnp.sum(jnp.where(identity(size), gram, 0.0), axis=1, keepdims=True) + 1e-30
    step = 8
    row = iota((size, 2 * size), 0)
    lane = iota((size, 2 * size), 1)
    table = jnp.concatenate([gram, identity(size).astype(f32)], axis=1)
    for k in range(0, size, step):
        cols = [jnp.broadcast_to(table[:, k + i : k + i + 1], table.shape) for i in range(step)]
        lines = [table[k + i : k + i + 1, :] for i in range(step)]
        for i in range(step):
            pivot = cols[i][k + i : k + i + 1, :]
            inverse = 1.0 / (jnp.maximum(pivot, least[k + i : k + i + 1, :]) if bounded else pivot)
            for j in range(i + 1, step):
                lines[j] = lines[j] - lines[i] * (cols[i][k + j : k + j + 1, :] * inverse)
                cols[j] = cols[j] - cols[i] * (cols[j][k + i : k + i + 1, :] * inverse)
            table = table - jnp.where(row > k + i, cols[i], 0.0) * (lines[i] * inverse)
    pivots = jnp.sum(jnp.where(row == lane, table, 0.0), axis=1, keepdims=True)
    return table[:, size:] * lax.rsqrt(jnp.maximum(pivots, least) if bounded else pivots)


def balanced(parts):
    while len(parts) > 1:
        parts = [a + b for a, b in zip(parts[::2], parts[1::2])]
    return parts[0]


def finish_kernel(factor, count, *refs):
    parts, y_ref, out_ref = refs[:count], refs[count], refs[count + 1]
    inverse = factor * inverse_factor(unpacked(balanced([part[...] for part in parts])))
    zero = jnp.zeros_like(inverse)
    both = jnp.concatenate(
        [jnp.concatenate([inverse, zero], axis=1), jnp.concatenate([zero, inverse], axis=1)], axis=0
    )
    wide = 2 * RANK
    tiles, width = y_ref.shape
    pieces = [y_ref[:, q * wide : (q + 1) * wide] for q in range(width // wide)]
    y_high, y_low = pair_of(jnp.concatenate(pieces, axis=0))
    t_high, t_low = pair_of(both)

    def times(a, b):
        return lax.dot_general(a, b, ABT, preferred_element_type=f32)

    out = times(y_high, t_high) + (times(y_low, t_high) + times(y_high, t_low))
    for q in range(width // wide):
        out_ref[:, q * wide : (q + 1) * wide] = out[q * tiles : (q + 1) * tiles]


def finish(factor, parts, y):
    return kernel_call(
        functools.partial(finish_kernel, factor, len(parts)),
        sds(y.shape, f32),
    )(*parts, y)


def exchange_stages(axis):
    size = lax.axis_size(axis)
    stages, bit = [], 1
    if axis == "col":
        stages.append([1])
        bit = 2
    while bit < size:
        if 2 * bit < size:
            stages.append([bit, 2 * bit, 3 * bit])
            bit *= 4
        else:
            stages.append([bit])
            bit *= 2
    return stages


def summed_parts(gram, axis):
    size = lax.axis_size(axis)
    parts = [gram]
    for partners in exchange_stages(axis):
        gram = balanced(parts)
        parts = [gram] + [lax.ppermute(gram, axis, [(i, i ^ p) for i in range(size)]) for p in partners]
    return parts


def passed_along(shard, axis, by):
    count = lax.axis_size(axis)
    pairs = [(i, i + by) for i in range(count) if 0 <= i + by < count]
    return lax.ppermute(shard, axis, pairs)


def local(features, tissue, probe):
    tile_rows, tile_cols, patches, width = features.shape
    total = tile_rows * lax.axis_size("row") * tile_cols * lax.axis_size("col") * patches
    factor = math.sqrt(float(total))
    parts = summed_parts(start_gram(probe), "row")
    (edges,) = gate((mark_edges(features, tissue),), parts[1:])
    below_edges = passed_along(edges, "row", -1)
    parts = summed_parts(balanced(parts), "col")
    own_panel = probe.reshape(tile_rows, tile_cols, patches, RANK)
    left_end, right_end, middle, unit0, unit1 = own_units(features, tissue, own_panel, edges)
    left_end, right_end = gate((left_end, right_end), parts)
    from_left = passed_along(right_end, "col", 1)
    from_right = passed_along(left_end, "col", -1)
    below_middle = passed_along(middle, "row", -1)
    m, sums = inside_affinity(unit0, unit1, patches)
    below_left, below_right = cut(below_edges, sums)
    _, u1, m, stat = outside_affinity(unit0, unit1, m, tissue, sums, from_left, from_right, below_left)
    panel, payload = start_panel(factor, parts, stat, from_left, own_panel, from_right)
    below_left, below_right = passed_along(below_right, "col", 1), passed_along(below_left, "col", -1)
    got_below = passed_along(payload, "row", -1)
    n = tile_cols + 2 * GHOST
    cross = cross_affinity(0, (below_left, below_edges, below_right), u1, stat, panel)
    v, w, sums, u0, payload, _ = cross_affinity(1, (below_middle,), u1, stat, panel, cross)
    got_above = passed_along(payload, "row", 1)
    z, t1, gain1, own = before_first(got_below, sums, stat, u0, m, v)
    y, u, t0, gain0, up, down = first_iteration(got_above, stat, t1, gain1, own, z, panel, m, w)
    spread = (t0, t1, gain0, gain1)
    below, above = passed_along(up, "row", -1), passed_along(down, "row", 1)
    z = local_products(3, n - 3, m, u)
    y, u, up, down = middle_step(3, below, above, z, y, spread, v, w)
    below, above = passed_along(up, "row", -1), passed_along(down, "row", 1)
    z = local_products(4, n - 4, m, u)
    y, gram = last_step(4, below, above, z, y, spread, v)

    parts = summed_parts(balanced(summed_parts(gram, "col")), "row")
    flat = y.reshape(tile_rows * tile_cols, patches * RANK)
    out = finish(factor, parts, flat)
    return out.reshape(tile_rows, tile_cols, patches * RANK)


def solution(mesh):
    placed = (P("row", "col", None, None), P("row", "col", None), P("row", "col", None))
    return jax.shard_map(
        local, mesh=mesh, in_specs=placed, out_specs=P("row", "col", None), check_vma=False
    )
```

```python
import functools
import math

import jax
import jax.numpy as jnp
from jax import lax
from jax.experimental import pallas as pl
from jax.experimental.pallas import tpu as pltpu
from jax.sharding import PartitionSpec as P

RANK = 64
ITERS = 3
AFFINITY_TEMP = 4.0

GHOST = ITERS + 1
EDGE = 4
TINY = 1e-30
VMEM_BYTES = 16 * 1024 * 1024
FLOOR = math.exp(-AFFINITY_TEMP)
ABT = (((1,), (1,)), ((), ()))
ATB = (((0,), (0,)), ((), ()))

f32 = jnp.float32
bf16 = jnp.bfloat16


def kernel_call(body, out_shape, scratch=()):
    return pl.pallas_call(
        body,
        out_shape=out_shape,
        scratch_shapes=list(scratch),
        compiler_params=pltpu.CompilerParams(vmem_limit_bytes=VMEM_BYTES),
    )


def sds(shape, dtype):
    return jax.ShapeDtypeStruct(shape, dtype)


def iota(shape, dim):
    return lax.broadcasted_iota(jnp.int32, shape, dim)


def identity(n):
    return iota((n, n), 0) == iota((n, n), 1)


def unit_and_mask(block):
    values = block.astype(f32)
    scaled = values * lax.rsqrt(jnp.sum(values * values, axis=-1, keepdims=True) + 1e-06)
    return scaled.astype(bf16), (values[:, :1] != 0.0).astype(f32)


def affinity_of(left, right):
    scores = lax.dot_general(left, right, ABT, preferred_element_type=f32)
    return jnp.exp(AFFINITY_TEMP * scores - AFFINITY_TEMP)


def at_lane(lane, e, column, table):
    return jnp.where(lane == e, column, table)


def absent_near(mask, width):
    count = jnp.sum(mask, axis=0, keepdims=True)
    return width - (pltpu.roll(count, 1, 1) + count + pltpu.roll(count, 127, 1))


def packed(block):
    half = block.shape[0] // 2
    return jnp.concatenate([block[:half], block[half:]], axis=1)


def unpacked(block):
    return jnp.concatenate([block[:, :RANK], block[:, RANK:]], axis=0)


def pair_of(values):
    high = values.astype(bf16)
    return high, (values - high.astype(f32)).astype(bf16)


def four_of(values):
    high, middle = pair_of(values)
    low = (values - high.astype(f32) - middle.astype(f32)).astype(bf16)
    return jnp.concatenate([high, middle, low, jnp.zeros_like(low)], axis=1)


def basis_rows(table):
    parts = four_of(table)
    return jnp.concatenate([parts[:, : 2 * RANK], packed(parts[:, 2 * RANK : 3 * RANK])], axis=0)


def basis_of(rows):
    rows = rows.astype(f32)
    return rows[:RANK, :RANK] + rows[:RANK, RANK:] + unpacked(rows[RANK:])


def turn_of(theirs, inverse):
    return lax.dot_general(
        theirs, inverse, ABT, precision=lax.Precision.HIGHEST, preferred_element_type=f32
    )


def turned(tiles, turn):
    patch = tiles[0].shape[0]
    stack = jnp.concatenate(tiles, axis=0).astype(bf16)
    high, low = turn
    result = jnp.dot(stack, high, preferred_element_type=f32) + jnp.dot(stack, low, preferred_element_type=f32)
    return [result[i * patch : (i + 1) * patch] for i in range(len(tiles))]


def whole_of(parts):
    parts = parts.astype(f32)
    return parts[:, :RANK] + parts[:, RANK : 2 * RANK] + parts[:, 2 * RANK : 3 * RANK]


def by_sublane(tissue):
    mask = (tissue != 0).astype(bf16)
    return lax.dot_general(mask, identity(mask.shape[0]).astype(bf16), ATB, preferred_element_type=f32)


def marked(tile, column):
    zero = (iota(tile.shape, 1) == 0) & (tile == 0)
    return jnp.where(zero, jnp.asarray(TINY, bf16), tile) * column.astype(bf16)


def fetched(sources, slots, sems):
    copies = [pltpu.make_async_copy(source, slot, sems.at[i]) for i, (source, slot) in enumerate(zip(sources, slots))]
    for copy in copies:
        copy.start()
    return copies


def in_hbm(*arrays):
    return tuple(pltpu.with_memory_space_constraint(array, pltpu.HBM) for array in arrays)


VMEM_SPEC = pl.BlockSpec(memory_space=pltpu.VMEM)
HBM_SPEC = pl.BlockSpec(memory_space=pltpu.HBM)
ANY_SPEC = pl.BlockSpec(memory_space=pl.ANY)


def folded_gram(side):
    wide = 2 * RANK
    gram = lax.dot_general(side, side, ATB, preferred_element_type=f32)
    gram = gram[:wide] + gram[wide:]
    gram = gram[:, :wide] + gram[:, wide:]
    return packed(gram[:RANK, :RANK] + gram[RANK:, RANK:])


def start_gram_kernel(probe_ref, gram_ref, flat_ref, sems):
    rows, cols, width = probe_ref.shape
    (copy,) = fetched([probe_ref], [flat_ref], sems)
    copy.wait()
    wide = 2 * RANK
    spans = [slice(q * wide, (q + 1) * wide) for q in range(width // wide)]
    side = jnp.concatenate([flat_ref[row, :, span] for row in range(rows) for span in spans], axis=0)
    gram_ref[...] = folded_gram(jnp.concatenate(pair_of(side), axis=1))


def start_gram(probe):
    return pl.pallas_call(
        start_gram_kernel,
        in_specs=[HBM_SPEC],
        out_specs=VMEM_SPEC,
        out_shape=sds((RANK // 2, 2 * RANK), f32),
        scratch_shapes=[pltpu.VMEM(probe.shape, f32), pltpu.SemaphoreType.DMA((1,))],
        compiler_params=pltpu.CompilerParams(vmem_limit_bytes=VMEM_BYTES),
    )(*in_hbm(probe))


def mark_edges_kernel(x_ref, tissue_ref, edge_ref, tile_ref, mask_ref, sems):
    cols = x_ref.shape[1]
    sources = [tissue_ref.at[0], x_ref.at[0, :EDGE], x_ref.at[0, cols - EDGE :]]
    copies = fetched(sources, [mask_ref, tile_ref.at[:EDGE], tile_ref.at[EDGE:]], sems)
    copies[0].wait()
    mask = by_sublane(mask_ref[...])
    for side, first in ((0, 0), (1, cols - EDGE)):
        copies[1 + side].wait()
        for i in range(EDGE):
            at = side * EDGE + i
            edge_ref[at] = marked(tile_ref[at], mask[:, first + i : first + i + 1])


def mark_edges(x, tissue):
    rows, cols, patch, width = x.shape
    shape = (2 * EDGE, patch, width)
    return pl.pallas_call(
        mark_edges_kernel,
        in_specs=[HBM_SPEC, HBM_SPEC],
        out_specs=VMEM_SPEC,
        out_shape=sds(shape, bf16),
        scratch_shapes=[
            pltpu.VMEM(shape, bf16),
            pltpu.VMEM((cols, patch), jnp.int32),
            pltpu.SemaphoreType.DMA((3,)),
        ],
        compiler_params=pltpu.CompilerParams(vmem_limit_bytes=VMEM_BYTES),
    )(*in_hbm(x, tissue))


def gate_kernel(count, *refs):
    for x_ref, out_ref in zip(refs[:count], refs[len(refs) - count :]):
        out_ref[...] = x_ref[...]


def gate(arrays, after):
    count = len(arrays)
    return pl.pallas_call(
        functools.partial(gate_kernel, count),
        in_specs=[VMEM_SPEC] * count + [ANY_SPEC] * len(after),
        out_specs=[VMEM_SPEC] * count,
        out_shape=tuple(sds(x.shape, x.dtype) for x in arrays),
        input_output_aliases={i: i for i in range(count)},
        compiler_params=pltpu.CompilerParams(vmem_limit_bytes=VMEM_BYTES),
    )(*arrays, *after)


def units_kernel(
    x_ref, tissue_ref, probe_ref, after_ref,
    left_ref, right_ref, middle_ref, unit0_ref, unit1_ref,
    tile_ref, sems,
):
    rows, cols, patch, width = x_ref.shape
    run = GHOST
    order = [(row, c) for row in range(rows) for c in (0, cols - run)]
    order += [(row, c) for row in range(rows) for c in range(run, cols - run, run)]
    copies = fetched([x_ref.at[row, c : c + run] for row, c in order], [tile_ref.at[i] for i in range(len(order))], sems)
    masks = [by_sublane(tissue_ref[row]) for row in range(rows)]
    for i, (row, first) in enumerate(order):
        copies[i].wait()
        for k in range(run):
            c = first + k
            tile, column = tile_ref[i, k], masks[row][:, c : c + 1]
            unit, _ = unit_and_mask(tile)
            at = (GHOST + c) * patch
            (unit0_ref, unit1_ref)[row][at : at + patch, :] = unit * column.astype(bf16)
            if first == 0 or first == cols - run:
                side_ref = left_ref if first == 0 else right_ref
                side_ref[row, k, :, :width] = marked(tile, column)
                side_ref[row, k, :, width:] = four_of(probe_ref[row, c])
            if row == 0 and EDGE <= c < cols - EDGE:
                middle_ref[c - EDGE] = marked(tile, column)


def own_units(x, tissue, probe, after):
    rows, cols, patch, width = x.shape
    n = cols + 2 * GHOST
    side = sds((rows, GHOST, patch, width + 4 * RANK), bf16)
    unit = sds((n * patch, width), bf16)
    return pl.pallas_call(
        units_kernel,
        in_specs=[HBM_SPEC, VMEM_SPEC, VMEM_SPEC, ANY_SPEC],
        out_specs=[VMEM_SPEC] * 5,
        out_shape=(side, side, sds((cols - 2 * EDGE, patch, width), bf16), unit, unit),
        scratch_shapes=[
            pltpu.VMEM((rows * cols // GHOST, GHOST, patch, width), bf16),
            pltpu.SemaphoreType.DMA((rows * cols // GHOST,)),
        ],
        compiler_params=pltpu.CompilerParams(vmem_limit_bytes=VMEM_BYTES),
    )(*in_hbm(x), tissue, probe, after)


def bands(ranges, patch, unit0_ref, unit1_ref, m_ref, degree, diagonal):
    both = 2 * patch
    shape = (both, 3 * both)
    patch_of = iota(shape, 0)
    own = iota(shape, 1) == jnp.where(patch_of < patch, patch_of + patch, patch_of + 3 * patch)
    lane = iota((both, 128), 1)

    def band(e, carry):
        degree, diagonal = carry
        around = slice((e - 1) * patch, (e + 2) * patch)
        here = slice(e * patch, (e + 1) * patch)
        left = jnp.concatenate([unit0_ref[here, :], unit1_ref[here, :]], axis=0)
        right = jnp.concatenate([unit0_ref[around, :], unit1_ref[around, :]], axis=0)
        weights = affinity_of(left, right)
        others = jnp.where(own, 0.0, weights)
        m_ref[e] = others.astype(bf16)
        itself = jnp.sum(weights - others, axis=1, keepdims=True)
        degree = at_lane(lane, e, jnp.sum(weights, axis=1, keepdims=True), degree)
        diagonal = at_lane(lane, e, itself, diagonal)
        return degree, diagonal

    carry = (degree, diagonal)
    for low, high in ranges:
        for e in range(low, high):
            carry = band(e, carry)
    return carry


def inside_kernel(n, unit0_ref, unit1_ref, m_ref, sum_ref):
    patch = m_ref.shape[1] // 2
    empty = jnp.zeros((2 * patch, 128), f32)
    sum_ref[0], sum_ref[1] = bands([(GHOST + 1, n - GHOST - 1)], patch, unit0_ref, unit1_ref, m_ref, empty, empty)


def inside_affinity(unit0, unit1, patch):
    n = unit0.shape[0] // patch
    both = 2 * patch
    return pl.pallas_call(
        functools.partial(inside_kernel, n),
        out_shape=(sds((n, both, 3 * both), bf16), sds((2, both, 128), f32)),
        compiler_params=pltpu.CompilerParams(vmem_limit_bytes=VMEM_BYTES),
    )(unit0, unit1)


def outside_kernel(
    n,
    start0_ref, start1_ref, some_ref, tissue_ref, sum_ref, xl_ref, xr_ref, after_ref,
    unit0_ref, unit1_ref, m_ref, stat_ref,
):
    rows, count, patch, _ = xl_ref.shape
    width = unit0_ref.shape[1]
    cols = n - 2 * count
    both = rows * patch
    lane = iota((patch, 128), 1)

    kept = slice(count * patch, (count + cols) * patch)
    unit0_ref[kept, :] = start0_ref[kept, :]
    unit1_ref[kept, :] = start1_ref[kept, :]
    for e in range(count + 1, n - count - 1):
        m_ref[e] = some_ref[e]
    masks = []
    for row, unit_ref in ((0, unit0_ref), (1, unit1_ref)):
        own_mask = by_sublane(tissue_ref[row])
        mask = jnp.zeros((patch, 128), f32)
        for e in range(n):
            if e < count:
                unit, column = unit_and_mask(xl_ref[row, e, :, :width])
            elif e < count + cols:
                unit, column = None, own_mask[:, e - count : e - count + 1]
            else:
                unit, column = unit_and_mask(xr_ref[row, e - count - cols, :, :width])
            mask = at_lane(lane, e, column, mask)
            if unit is not None:
                unit_ref[e * patch : (e + 1) * patch, :] = unit
        masks.append(mask)
    mask = jnp.concatenate(masks, axis=0)
    ranges = [(1, GHOST + 1), (n - GHOST - 1, n - 1)]
    degree, diagonal = bands(ranges, patch, unit0_ref, unit1_ref, m_ref, sum_ref[0], sum_ref[1])
    degree = degree - FLOOR * absent_near(mask, 3 * both)
    stat_ref[0] = degree
    stat_ref[1] = diagonal
    stat_ref[2] = mask

def payload_rows(columns, patch):
    return columns * patch // 2 + patch // 2 + RANK * 3 // 2


def outside_affinity(unit0, unit1, m, tissue, sums, xl, xr, after):
    n, both, _ = m.shape
    unit = sds(unit0.shape, bf16)
    return pl.pallas_call(
        functools.partial(outside_kernel, n),
        in_specs=[VMEM_SPEC] * 7 + [ANY_SPEC],
        out_specs=[VMEM_SPEC] * 4,
        out_shape=(unit, unit, sds(m.shape, bf16), sds((3, both, 128), f32)),
        input_output_aliases={0: 0, 1: 1, 2: 2},
        compiler_params=pltpu.CompilerParams(vmem_limit_bytes=VMEM_BYTES),
    )(unit0, unit1, m, tissue, sums, xl, xr, after)


def start_kernel(factor, count, *refs):
    parts, (stat_ref, xl_ref, p_ref, xr_ref, panel_ref, pay_ref, base_ref) = refs[:count], refs[count:]
    rows, cols, patch, _ = p_ref.shape
    n = cols + 2 * GHOST
    half = patch // 2
    width = xl_ref.shape[3] - 4 * RANK
    inverse, root = inverse_factor(unpacked(balanced([part[...] for part in parts])), True)
    inverse, root = factor * inverse, root / factor
    base_ref[0], base_ref[1] = inverse, root
    for row in range(rows):
        tiles = [whole_of(xl_ref[row, c, :, width:]) for c in range(GHOST)]
        tiles += [p_ref[row, c] for c in range(cols)]
        tiles += [whole_of(xr_ref[row, c, :, width:]) for c in range(GHOST)]
        turned = lax.dot_general(
            jnp.concatenate(tiles, axis=0), inverse, ABT, precision=lax.Precision.HIGHEST, preferred_element_type=f32
        )
        for e in range(n):
            tile = turned[e * patch : (e + 1) * patch]
            panel_ref[row, e] = tile
            if row == 0 and 0 < e < n - 1:
                pay_ref[(e - 1) * half : e * half, :] = packed(tile).astype(bf16)
    tail = (n - 2) * half
    put_tail(pay_ref, tail, stat_ref[0, :patch], root)


def put_tail(pay_ref, tail, table, root):
    half = table.shape[0] // 2
    high, low = pair_of(jnp.where(iota(table.shape, 1) < 32, table, 0.0))
    both = high.astype(f32) + pltpu.roll(low.astype(f32), 32, 1)
    pay_ref[tail : tail + half, :] = (both[:half] + pltpu.roll(both[half:], 64, 1)).astype(bf16)
    pay_ref[tail + half :, :] = basis_rows(root)


def got_tail(got_ref, tail, patch):
    half = patch // 2
    both = got_ref[tail : tail + half, :].astype(f32)
    upper = both + pltpu.roll(both, 96, 1)
    lower = pltpu.roll(both, 64, 1) + pltpu.roll(both, 32, 1)
    return jnp.concatenate([upper, lower], axis=0), basis_of(got_ref[tail + half :, :])


def start_panel(factor, parts, stat, xl, own_panel, xr):
    rows, cols, patch, _ = own_panel.shape
    n = cols + 2 * GHOST
    return kernel_call(
        functools.partial(start_kernel, factor, len(parts)),
        (
            sds((rows, n, patch, RANK), f32),
            sds((payload_rows(n - 2, patch), 2 * RANK), bf16),
            sds((2, RANK, RANK), f32),
        ),
    )(*parts, stat, xl, own_panel, xr)


def cut_kernel(be_ref, after_ref, left_ref, right_ref):
    left_ref[...] = be_ref[:GHOST]
    right_ref[...] = be_ref[be_ref.shape[0] - GHOST :]


def cut(be, after):
    vmem = pl.BlockSpec(memory_space=pltpu.VMEM)
    side = sds((GHOST,) + be.shape[1:], be.dtype)
    return pl.pallas_call(
        cut_kernel,
        in_specs=[vmem, pl.BlockSpec(memory_space=pl.ANY)],
        out_specs=[vmem] * 2,
        out_shape=(side, side),
        compiler_params=pltpu.CompilerParams(vmem_limit_bytes=VMEM_BYTES),
    )(be, after)


def stages(n):
    middle = list(range(GHOST + EDGE, n - GHOST - EDGE))
    ends = [c for c in range(n) if c not in middle]
    arrived, seen, steps = set(), set(), []
    for tiles in (ends, middle):
        arrived |= set(tiles)
        columns = [e for e in range(1, n - 1) if {e - 1, e, e + 1} <= arrived and e not in seen]
        seen |= set(columns)
        steps.append((tiles, columns))
    return steps


def scale_of(stat_ref, sums):
    down_sum, _, mask = sums
    patch = mask.shape[0]
    degree = 1.0 + stat_ref[0, patch:] + down_sum - FLOOR * absent_near(mask, 3 * patch)
    return stat_ref[2, patch:] * lax.rsqrt(degree)


def pair_source(e, tiles):
    some = next(iter(tiles.values()))
    near = [tiles.get(c, jnp.zeros_like(some)) for c in range(e - 1, e + 3)]
    return jnp.concatenate(near, axis=0)


def pairs_of(columns):
    return sorted({e - (e + 1) % 2 for e in columns})


def pair_products(columns, block_ref, tiles):
    results = {}
    for e in pairs_of(columns):
        product = jnp.dot(block_ref[e // 2], pair_source(e, tiles), preferred_element_type=f32)
        patch = product.shape[0] // 2
        results[e], results[e + 1] = product[:patch], product[patch:]
    return results


def products(columns, up_ref, tiles, pay_ref, first):
    half = up_ref.shape[1] // 4
    results = pair_products(columns, up_ref, tiles)
    for e in columns:
        pay_ref[(e - first) * half : (e - first + 1) * half, :] = packed(results[e]).astype(bf16)


def cross_kernel(n, stage, *refs):
    steps = stages(n)
    tiles, columns = steps[stage]
    count = 3 if stage == 0 else 1
    pieces, (own_ref, stat_ref, p_ref, base_ref) = refs[:count], refs[count : count + 4]
    refs = refs[count + 4 :]
    patch = pieces[0].shape[1]
    lane = iota((patch, 128), 1)
    if stage == 0:
        v_ref, w_ref, sum_ref, u0_ref, pay_ref, unit_ref = refs
        empty = jnp.zeros((patch, 128), f32)
        down_sum, up_sum, mask = empty, empty, empty
    else:
        before, (v_ref, w_ref, sum_ref, u0_ref, pay_ref, unit_ref) = refs[:6], refs[6:12]
        down_sum, up_sum, mask = (before[2][i] for i in range(3))
        earlier = {e for _, reached in steps[:stage] for e in reached}
        for e in pairs_of(earlier):
            v_ref[e // 2] = before[0][e // 2]
            w_ref[e // 2] = before[1][e // 2]
        for e in sorted(earlier):
            u0_ref[e] = before[3][e]
        for e in sorted(e for e in earlier if e - 1 in earlier and e + 1 in earlier):
            span = slice((e - 2) * patch // 2, (e - 1) * patch // 2)
            pay_ref[span, :] = before[4][span, :]
        for c in sorted({c for e in columns for c in (e - 1, e, e + 1)} - set(tiles)):
            span = slice(c * patch, (c + 1) * patch)
            unit_ref[span, :] = before[5][span, :]
    sources = [(ref, i) for ref in pieces for i in range(ref.shape[0])]
    for c, (ref, i) in zip(tiles, sources):
        unit, column = unit_and_mask(ref[i])
        unit_ref[c * patch : (c + 1) * patch, :] = unit
        mask = at_lane(lane, c, column, mask)
    shape = (2 * patch, 4 * patch)
    apart = iota(shape, 1) // patch - iota(shape, 0) // patch
    beside = (apart >= 0) & (apart <= 2)
    for e in pairs_of(columns):
        around = slice((e - 1) * patch, (e + 3) * patch)
        here = slice(e * patch, (e + 2) * patch)
        down = jnp.where(beside, affinity_of(own_ref[here, :], unit_ref[around, :]), 0.0)
        up = jnp.where(beside, affinity_of(unit_ref[here, :], own_ref[around, :]), 0.0)
        v_ref[e // 2] = down.astype(bf16)
        w_ref[e // 2] = up.astype(bf16)
        down = jnp.sum(down, axis=1, keepdims=True)
        up = jnp.sum(up, axis=1, keepdims=True)
        for i in range(2):
            span = slice(i * patch, (i + 1) * patch)
            down_sum = at_lane(lane, e + i, down[span], down_sum)
            up_sum = at_lane(lane, e + i, up[span], up_sum)
    sums = (down_sum, up_sum, mask)
    scale = scale_of(stat_ref, sums)
    for e in columns:
        u0_ref[e] = (scale[:, e : e + 1] * p_ref[1, e]).astype(bf16)
    inner, known = [], []
    for last in (stage - 1, stage):
        known = [e for _, reached in steps[: last + 1] for e in reached]
        inner.append({e for e in range(2, n - 2) if {e - 1, e, e + 1} <= set(known)})
    fresh = sorted(inner[1] - inner[0])
    near = {c for e in fresh for c in (e - 1, e, e + 1)}
    products(fresh, w_ref, {e: u0_ref[e] for e in near}, pay_ref, 2)
    if stage < len(steps) - 1:
        for i in range(3):
            sum_ref[i] = sums[i]
        return
    shared = up_sum - FLOOR * absent_near(stat_ref[2, patch:], 3 * patch)
    sum_ref[0], sum_ref[1], sum_ref[2] = shared, mask, scale
    tail = (n - 4) * patch // 2
    put_tail(pay_ref, tail, shared, base_ref[1])


def cross_affinity(stage, pieces, u1, stat, panel, base, before=()):
    patch, width = pieces[0].shape[1:]
    n = u1.shape[0] // patch
    given = len(pieces) + 4
    return pl.pallas_call(
        functools.partial(cross_kernel, n, stage),
        out_shape=(
            sds((n // 2 - 1, 2 * patch, 4 * patch), bf16),
            sds((n // 2 - 1, 2 * patch, 4 * patch), bf16),
            sds((3, patch, 128), f32),
            sds((n, patch, RANK), bf16),
            sds((payload_rows(n - 4, patch), 2 * RANK), bf16),
            sds((n * patch, width), bf16),
        ),
        input_output_aliases={given + i: i for i in range(len(before))},
        compiler_params=pltpu.CompilerParams(vmem_limit_bytes=VMEM_BYTES),
    )(*pieces, u1, stat, panel, base, *before)


def before_first_kernel(
    n,
    got_ref, sum_ref, stat_ref, u0_ref, m_ref, v_ref, base_ref,
    z_ref, t_ref, gain_ref, own_ref, turn_ref,
):
    patch = u0_ref.shape[1]
    half = patch // 2
    tail = (n - 2) * half
    partial, theirs = got_tail(got_ref, tail, patch)
    below_scale = sum_ref[1] * lax.rsqrt(1.0 + partial + sum_ref[0])
    scale = sum_ref[2]
    gain = 1.0 + scale * scale * stat_ref[1, patch:]
    upper = stat_ref[1, :patch]
    turn = pair_of(turn_of(theirs, base_ref[0]))
    turn_ref[0], turn_ref[1] = turn
    tiles = [unpacked(got_ref[(e - 1) * half : e * half, :].astype(f32)) for e in range(1, n - 1)]
    tiles = turned([below_scale[:, e : e + 1] * tile for e, tile in zip(range(1, n - 1), tiles)], turn)
    lower = pair_products(range(2, n - 2), v_ref, {e: tile.astype(bf16) for e, tile in zip(range(1, n - 1), tiles)})
    for e in range(2, n - 2):
        own = u0_ref[e - 1 : e + 2].reshape(3 * patch, RANK)
        total = jnp.dot(m_ref[e, :, 3 * patch :], own, preferred_element_type=f32)
        z_ref[e, :patch] = total[:patch]
        z_ref[e, patch:] = total[patch:] + lower[e]
        for ref, table in ((t_ref, scale), (gain_ref, gain), (own_ref, upper)):
            ref[e] = jnp.broadcast_to(table[:, e : e + 1], (patch, RANK))


def before_first(got, sums, stat, u0, m, v, base):
    n, patch, _ = u0.shape
    spread = sds((n, patch, RANK), f32)
    return kernel_call(
        functools.partial(before_first_kernel, n),
        (sds((n, 2 * patch, RANK), f32), spread, spread, spread, sds((2, RANK, RANK), bf16)),
    )(got, sums, stat, u0, m, v, base)


def first_kernel(
    n,
    got_ref, stat_ref, t1_ref, gain1_ref, own_ref, z_ref, p_ref, m_ref, w_ref, base_ref,
    y_ref, u_ref, t0_ref, gain0_ref, up_ref, down_ref, turn_ref,
    start_ref,
):
    patch = t1_ref.shape[1]
    half = patch // 2
    tail = (n - 4) * half
    partial, theirs = got_tail(got_ref, tail, patch)
    turn = pair_of(turn_of(theirs, base_ref[0]))
    turn_ref[0], turn_ref[1] = turn
    above = turned([unpacked(got_ref[(e - 2) * half : (e - 1) * half, :]) for e in range(2, n - 2)], turn)
    scale = stat_ref[2, :patch] * lax.rsqrt(1.0 + stat_ref[0, :patch] + partial)
    for e in range(1, n - 1):
        t = jnp.broadcast_to(scale[:, e : e + 1], (patch, RANK))
        t0_ref[e] = t
        start_ref[e] = (t * p_ref[0, e]).astype(bf16)
    for e in range(2, n - 2):
        own = start_ref[e - 1 : e + 2].reshape(3 * patch, RANK)
        total = z_ref[e] + jnp.dot(m_ref[e, :, : 3 * patch], own, preferred_element_type=f32)
        upper = total[:patch] + above[e - 2]
        gain = 1.0 + t0_ref[e] * t0_ref[e] * own_ref[e]
        gain0_ref[e] = gain
        for row, piece, t, g in ((0, upper, t0_ref[e], gain), (1, total[patch:], t1_ref[e], gain1_ref[e])):
            image = p_ref[row, e] * g + t * piece
            y_ref[row, e] = image
            scaled = t * image
            u_ref[row, e] = scaled.astype(bf16)
            if row == 0:
                up_ref[(e - 2) * half : (e - 1) * half, :] = packed(scaled).astype(bf16)
    products(range(3, n - 3), w_ref, {e: u_ref[1, e] for e in range(2, n - 2)}, down_ref, 3)


def first_iteration(got, stat, t1, gain1, own, z, panel, m, w, base):
    n, both, _ = z.shape
    patch = both // 2
    half = patch // 2
    spread = sds((n, patch, RANK), f32)
    return kernel_call(
        functools.partial(first_kernel, n),
        (
            sds((2, n, patch, RANK), f32),
            sds((2, n, patch, RANK), bf16),
            spread,
            spread,
            sds(((n - 4) * half, 2 * RANK), bf16),
            sds(((n - 6) * half, 2 * RANK), bf16),
            sds((2, RANK, RANK), bf16),
        ),
        [pltpu.VMEM((n, patch, RANK), bf16)],
    )(got, stat, t1, gain1, own, z, panel, m, w, base)


def local_kernel(low, high, m_ref, u_ref, z_ref):
    patch = u_ref.shape[2]
    for e in range(low, high):
        upper = u_ref[0, e - 1 : e + 2].reshape(3 * patch, RANK)
        lower = u_ref[1, e - 1 : e + 2].reshape(3 * patch, RANK)
        z_ref[e] = jnp.dot(m_ref[e], jnp.concatenate([upper, lower], axis=0), preferred_element_type=f32)


def local_products(low, high, m, u):
    n, both, _ = m.shape
    return kernel_call(
        functools.partial(local_kernel, low, high),
        sds((n, both, RANK), f32),
    )(m, u)


def images_of(n, low, below_ref, above_ref, z_ref, y_ref, scales, gains, turns, v_ref):
    patch = y_ref.shape[2]
    half = patch // 2
    count = n - 2 * low
    down, up = ((ref[0], ref[1]) for ref in turns)
    near = turned([unpacked(below_ref[i * half : (i + 1) * half, :]) for i in range(count + 2)], down)
    near = {low - 1 + i: tile.astype(bf16) for i, tile in enumerate(near)}
    lower = pair_products(range(low, n - low), v_ref, near)
    upper = turned([unpacked(above_ref[i * half : (i + 1) * half, :]) for i in range(count)], up)
    for e in range(low, n - low):
        pieces = (z_ref[e, :patch] + upper[e - low], z_ref[e, patch:] + lower[e])
        yield e, [y_ref[row, e] * gains[row][e] + scales[row][e] * pieces[row] for row in range(2)]


def middle_step_kernel(
    n, low,
    below_ref, above_ref, z_ref, y_ref, t0_ref, t1_ref, gain0_ref, gain1_ref, turn0_ref, turn1_ref, v_ref, w_ref,
    new_ref, u_ref, up_ref, down_ref,
):
    patch = y_ref.shape[2]
    half = patch // 2
    scales, gains = (t0_ref, t1_ref), (gain0_ref, gain1_ref)
    turns = (turn0_ref, turn1_ref)
    for e, images in images_of(n, low, below_ref, above_ref, z_ref, y_ref, scales, gains, turns, v_ref):
        for row in range(2):
            new_ref[row, e] = images[row]
            scaled = scales[row][e] * images[row]
            u_ref[row, e] = scaled.astype(bf16)
            if row == 0:
                up_ref[(e - low) * half : (e - low + 1) * half, :] = packed(scaled).astype(bf16)
    products(
        range(low + 1, n - low - 1), w_ref, {e: u_ref[1, e] for e in range(low, n - low)}, down_ref, low + 1
    )


def middle_step(low, below, above, z, y, spread, v, w):
    _, n, patch, _ = y.shape
    half = patch // 2
    return kernel_call(
        functools.partial(middle_step_kernel, n, low),
        (
            sds((2, n, patch, RANK), f32),
            sds((2, n, patch, RANK), bf16),
            sds(((n - 2 * low) * half, 2 * RANK), bf16),
            sds(((n - 2 * low - 2) * half, 2 * RANK), bf16),
        ),
    )(below, above, z, y, *spread, v, w)


def last_step_kernel(
    n, low,
    below_ref, above_ref, z_ref, y_ref, t0_ref, t1_ref, gain0_ref, gain1_ref, turn0_ref, turn1_ref, v_ref,
    new_ref, gram_ref, side_ref,
):
    patch = y_ref.shape[2]
    scales, gains = (t0_ref, t1_ref), (gain0_ref, gain1_ref)
    wide = 2 * RANK
    turns = (turn0_ref, turn1_ref)
    for e, images in images_of(n, low, below_ref, above_ref, z_ref, y_ref, scales, gains, turns, v_ref):
        for row in range(2):
            new_ref[row, e - low] = images[row]
        span = slice((e - low) * patch, (e - low + 1) * patch)
        side_ref[span, :wide], side_ref[span, wide:] = pair_of(jnp.concatenate(images, axis=1))
    gram_ref[...] = folded_gram(side_ref[...])


def last_step(low, below, above, z, y, spread, v):
    _, n, patch, _ = y.shape
    cols = n - 2 * low
    return kernel_call(
        functools.partial(last_step_kernel, n, low),
        (sds((2, cols, patch, RANK), f32), sds((RANK // 2, 2 * RANK), f32)),
        [pltpu.VMEM((cols * patch, 4 * RANK), bf16)],
    )(below, above, z, y, *spread, v)


def inverse_factor(gram, bounded=False):
    size = gram.shape[0]
    least = 0.0
    if bounded:
        least = 1e-6 * jnp.sum(jnp.where(identity(size), gram, 0.0), axis=1, keepdims=True) + 1e-16
    step = 8
    row = iota((size, 2 * size), 0)
    lane = iota((size, 2 * size), 1)
    table = jnp.concatenate([gram, identity(size).astype(f32)], axis=1)
    for k in range(0, size, step):
        cols = [jnp.broadcast_to(table[:, k + i : k + i + 1], table.shape) for i in range(step)]
        lines = [table[k + i : k + i + 1, :] for i in range(step)]
        for i in range(step):
            pivot = cols[i][k + i : k + i + 1, :]
            inverse = 1.0 / (jnp.maximum(pivot, least[k + i : k + i + 1, :]) if bounded else pivot)
            for j in range(i + 1, step):
                lines[j] = lines[j] - lines[i] * (cols[i][k + j : k + j + 1, :] * inverse)
                cols[j] = cols[j] - cols[i] * (cols[j][k + i : k + i + 1, :] * inverse)
            table = table - jnp.where(row > k + i, cols[i], 0.0) * (lines[i] * inverse)
    pivots = jnp.sum(jnp.where(row == lane, table, 0.0), axis=1, keepdims=True)
    if not bounded:
        return table[:, size:] * lax.rsqrt(pivots)
    pivots = jnp.maximum(pivots, least)
    row, lane = row[:, :size], lane[:, :size]
    upper = jnp.where(lane > row, table[:, :size], jnp.where(lane == row, pivots, 0.0))
    return table[:, size:] * lax.rsqrt(pivots), upper * lax.rsqrt(pivots)


def balanced(parts):
    while len(parts) > 1:
        parts = [a + b for a, b in zip(parts[::2], parts[1::2])]
    return parts[0]


def joint_gram(parts, base_ref):
    size = RANK // 2
    turns = turn_of(jnp.concatenate([unpacked(part[size:, :]) for part in parts[1:]], axis=0), base_ref[0])
    first = []
    for i, part in enumerate(parts[1:]):
        turn = turns[i * RANK : (i + 1) * RANK]
        first.append(
            jnp.dot(
                unpacked(part[:size, :]), turn, precision=lax.Precision.HIGHEST, preferred_element_type=f32
            )
        )
    others = lax.dot_general(
        turns, jnp.concatenate(first, axis=0), ATB, precision=lax.Precision.HIGHEST, preferred_element_type=f32
    )
    return unpacked(parts[0][:size, :]) + others


def joint_kernel(count, *refs):
    refs[-1][: RANK // 2, :] = packed(joint_gram(refs[:count], refs[count]))
    refs[-1][RANK // 2 :, :] = packed(refs[count][1])


def joint(parts, base):
    return kernel_call(functools.partial(joint_kernel, len(parts)), sds(parts[0].shape, f32))(*parts, base)


def finish_kernel(factor, count, *refs):
    parts, (base_ref, y_ref, out_ref) = refs[:count], refs[count:]
    inverse = factor * inverse_factor(joint_gram(parts, base_ref))
    zero = jnp.zeros_like(inverse)
    both = jnp.concatenate(
        [jnp.concatenate([inverse, zero], axis=1), jnp.concatenate([zero, inverse], axis=1)], axis=0
    )
    wide = 2 * RANK
    tiles, width = y_ref.shape
    pieces = [y_ref[:, q * wide : (q + 1) * wide] for q in range(width // wide)]
    y_high, y_low = pair_of(jnp.concatenate(pieces, axis=0))
    t_high, t_low = pair_of(both)

    def times(a, b):
        return lax.dot_general(a, b, ABT, preferred_element_type=f32)

    out = times(y_high, t_high) + (times(y_low, t_high) + times(y_high, t_low))
    for q in range(width // wide):
        out_ref[:, q * wide : (q + 1) * wide] = out[q * tiles : (q + 1) * tiles]


def finish(factor, parts, base, y):
    return kernel_call(
        functools.partial(finish_kernel, factor, len(parts)),
        sds(y.shape, f32),
    )(*parts, base, y)


def exchange_stages(axis):
    size = lax.axis_size(axis)
    stages, bit = [], 1
    if axis == "col":
        stages.append([1])
        bit = 2
    while bit < size:
        if 2 * bit < size:
            stages.append([bit, 2 * bit, 3 * bit])
            bit *= 4
        else:
            stages.append([bit])
            bit *= 2
    return stages


def summed_parts(gram, axis, combine):
    size = lax.axis_size(axis)
    parts = [gram]
    for partners in exchange_stages(axis):
        gram = combine(parts) if len(parts) > 1 else gram
        parts = [gram] + [lax.ppermute(gram, axis, [(i, i ^ p) for i in range(size)]) for p in partners]
    return parts


def passed_along(shard, axis, by):
    count = lax.axis_size(axis)
    pairs = [(i, i + by) for i in range(count) if 0 <= i + by < count]
    return lax.ppermute(shard, axis, pairs)


def local(features, tissue, probe):
    tile_rows, tile_cols, patches, width = features.shape
    total = tile_rows * lax.axis_size("row") * tile_cols * lax.axis_size("col") * patches
    factor = math.sqrt(float(total))
    edges = mark_edges(features, tissue)
    below_edges = passed_along(edges, "row", -1)
    parts = summed_parts(start_gram(probe), "col", balanced)
    own_panel = probe.reshape(tile_rows, tile_cols, patches, RANK)
    left_end, right_end, middle, unit0, unit1 = own_units(features, tissue, own_panel, edges)
    left_end, right_end = gate((left_end, right_end), parts)
    from_left = passed_along(right_end, "col", 1)
    from_right = passed_along(left_end, "col", -1)
    below_middle = passed_along(middle, "row", -1)
    m, sums = inside_affinity(unit0, unit1, patches)
    below_left, below_right = cut(below_edges, sums)
    _, u1, m, stat = outside_affinity(unit0, unit1, m, tissue, sums, from_left, from_right, below_left)
    panel, payload, base = start_panel(factor, parts, stat, from_left, own_panel, from_right)
    below_left, below_right = passed_along(below_right, "col", 1), passed_along(below_left, "col", -1)
    got_below = passed_along(payload, "row", -1)
    n = tile_cols + 2 * GHOST
    cross = cross_affinity(0, (below_left, below_edges, below_right), u1, stat, panel, base)
    v, w, sums, u0, payload, _ = cross_affinity(1, (below_middle,), u1, stat, panel, base, cross)
    got_above = passed_along(payload, "row", 1)
    z, t1, gain1, own, turn0 = before_first(got_below, sums, stat, u0, m, v, base)
    y, u, t0, gain0, up, down, turn1 = first_iteration(got_above, stat, t1, gain1, own, z, panel, m, w, base)
    spread = (t0, t1, gain0, gain1, turn0, turn1)
    below, above = passed_along(up, "row", -1), passed_along(down, "row", 1)
    z = local_products(3, n - 3, m, u)
    y, u, up, down = middle_step(3, below, above, z, y, spread, v, w)
    below, above = passed_along(up, "row", -1), passed_along(down, "row", 1)
    z = local_products(4, n - 4, m, u)
    y, gram = last_step(4, below, above, z, y, spread, v)

    gram = balanced(summed_parts(gram, "col", balanced))
    root = jnp.concatenate([base[1, : RANK // 2], base[1, RANK // 2 :]], axis=1)
    parts = summed_parts(jnp.concatenate([gram, root], axis=0), "row", lambda parts: joint(parts, base))
    flat = y.reshape(tile_rows * tile_cols, patches * RANK)
    out = finish(factor, parts, base, flat)
    return out.reshape(tile_rows, tile_cols, patches * RANK)


def solution(mesh):
    placed = (P("row", "col", None, None), P("row", "col", None), P("row", "col", None))
    return jax.shard_map(
        local, mesh=mesh, in_specs=placed, out_specs=P("row", "col", None), check_vma=False
    )
```

```python
import functools
import math

import jax
import jax.numpy as jnp
from jax import lax
from jax.experimental import pallas as pl
from jax.experimental.pallas import tpu as pltpu
from jax.sharding import PartitionSpec as P

RANK = 64
ITERS = 3
AFFINITY_TEMP = 4.0

GHOST = ITERS + 1
EDGE = 4
TINY = 1e-30
VMEM_BYTES = 16 * 1024 * 1024
FLOOR = math.exp(-AFFINITY_TEMP)
ABT = (((1,), (1,)), ((), ()))
ATB = (((0,), (0,)), ((), ()))

f32 = jnp.float32
bf16 = jnp.bfloat16


def kernel_call(body, out_shape, scratch=()):
    return pl.pallas_call(
        body,
        out_shape=out_shape,
        scratch_shapes=list(scratch),
        compiler_params=pltpu.CompilerParams(vmem_limit_bytes=VMEM_BYTES),
    )


def sds(shape, dtype):
    return jax.ShapeDtypeStruct(shape, dtype)


def iota(shape, dim):
    return lax.broadcasted_iota(jnp.int32, shape, dim)


def identity(n):
    return iota((n, n), 0) == iota((n, n), 1)


def unit_and_mask(block):
    values = block.astype(f32)
    scaled = values * lax.rsqrt(jnp.sum(values * values, axis=-1, keepdims=True) + 1e-06)
    return scaled.astype(bf16), (values[:, :1] != 0.0).astype(f32)


def affinity_of(left, right):
    scores = lax.dot_general(left, right, ABT, preferred_element_type=f32)
    return jnp.exp(AFFINITY_TEMP * scores - AFFINITY_TEMP)


def at_lane(lane, e, column, table):
    return jnp.where(lane == e, column, table)


def absent_near(mask, width):
    count = jnp.sum(mask, axis=0, keepdims=True)
    return width - (pltpu.roll(count, 1, 1) + count + pltpu.roll(count, 127, 1))


def packed(block):
    half = block.shape[0] // 2
    return jnp.concatenate([block[:half], block[half:]], axis=1)


def unpacked(block):
    return jnp.concatenate([block[:, :RANK], block[:, RANK:]], axis=0)


def pair_of(values):
    high = values.astype(bf16)
    return high, (values - high.astype(f32)).astype(bf16)


def four_of(values):
    high, middle = pair_of(values)
    low = (values - high.astype(f32) - middle.astype(f32)).astype(bf16)
    return jnp.concatenate([high, middle, low, jnp.zeros_like(low)], axis=1)


def basis_rows(table):
    parts = four_of(table)
    return jnp.concatenate([parts[:, : 2 * RANK], packed(parts[:, 2 * RANK : 3 * RANK])], axis=0)


def basis_of(rows):
    rows = rows.astype(f32)
    return rows[:RANK, :RANK] + rows[:RANK, RANK:] + unpacked(rows[RANK:])


def turn_of(theirs, inverse):
    return lax.dot_general(
        theirs, inverse, ABT, precision=lax.Precision.HIGHEST, preferred_element_type=f32
    )


def turned(tiles, turn):
    patch = tiles[0].shape[0]
    stack = jnp.concatenate(tiles, axis=0).astype(bf16)
    high, low = turn
    result = jnp.dot(stack, high, preferred_element_type=f32) + jnp.dot(stack, low, preferred_element_type=f32)
    return [result[i * patch : (i + 1) * patch] for i in range(len(tiles))]


def whole_of(parts):
    parts = parts.astype(f32)
    return parts[:, :RANK] + parts[:, RANK : 2 * RANK] + parts[:, 2 * RANK : 3 * RANK]


def by_sublane(tissue):
    mask = (tissue != 0).astype(bf16)
    return lax.dot_general(mask, identity(mask.shape[0]).astype(bf16), ATB, preferred_element_type=f32)


def marked(tile, column):
    zero = (iota(tile.shape, 1) == 0) & (tile == 0)
    return jnp.where(zero, jnp.asarray(TINY, bf16), tile) * column.astype(bf16)


def fetched(sources, slots, sems):
    copies = [pltpu.make_async_copy(source, slot, sems.at[i]) for i, (source, slot) in enumerate(zip(sources, slots))]
    for copy in copies:
        copy.start()
    return copies


def in_hbm(*arrays):
    return tuple(pltpu.with_memory_space_constraint(array, pltpu.HBM) for array in arrays)


VMEM_SPEC = pl.BlockSpec(memory_space=pltpu.VMEM)
HBM_SPEC = pl.BlockSpec(memory_space=pltpu.HBM)
ANY_SPEC = pl.BlockSpec(memory_space=pl.ANY)


def folded_gram(side):
    wide = 2 * RANK
    gram = lax.dot_general(side, side, ATB, preferred_element_type=f32)
    gram = gram[:wide] + gram[wide:]
    gram = gram[:, :wide] + gram[:, wide:]
    return packed(gram[:RANK, :RANK] + gram[RANK:, RANK:])


def start_gram_kernel(probe_ref, gram_ref, flat_ref, sems):
    rows, cols, width = probe_ref.shape
    (copy,) = fetched([probe_ref], [flat_ref], sems)
    copy.wait()
    wide = 2 * RANK
    spans = [slice(q * wide, (q + 1) * wide) for q in range(width // wide)]
    side = jnp.concatenate([flat_ref[row, :, span] for row in range(rows) for span in spans], axis=0)
    gram_ref[...] = folded_gram(jnp.concatenate(pair_of(side), axis=1))


def start_gram(probe):
    return pl.pallas_call(
        start_gram_kernel,
        in_specs=[HBM_SPEC],
        out_specs=VMEM_SPEC,
        out_shape=sds((RANK // 2, 2 * RANK), f32),
        scratch_shapes=[pltpu.VMEM(probe.shape, f32), pltpu.SemaphoreType.DMA((1,))],
        compiler_params=pltpu.CompilerParams(vmem_limit_bytes=VMEM_BYTES),
    )(*in_hbm(probe))


def mark_edges_kernel(x_ref, tissue_ref, edge_ref, tile_ref, mask_ref, sems):
    cols = x_ref.shape[1]
    sources = [tissue_ref.at[0], x_ref.at[0, :EDGE], x_ref.at[0, cols - EDGE :]]
    copies = fetched(sources, [mask_ref, tile_ref.at[:EDGE], tile_ref.at[EDGE:]], sems)
    copies[0].wait()
    mask = by_sublane(mask_ref[...])
    for side, first in ((0, 0), (1, cols - EDGE)):
        copies[1 + side].wait()
        for i in range(EDGE):
            at = side * EDGE + i
            edge_ref[at] = marked(tile_ref[at], mask[:, first + i : first + i + 1])


def mark_edges(x, tissue):
    rows, cols, patch, width = x.shape
    shape = (2 * EDGE, patch, width)
    return pl.pallas_call(
        mark_edges_kernel,
        in_specs=[HBM_SPEC, HBM_SPEC],
        out_specs=VMEM_SPEC,
        out_shape=sds(shape, bf16),
        scratch_shapes=[
            pltpu.VMEM(shape, bf16),
            pltpu.VMEM((cols, patch), jnp.int32),
            pltpu.SemaphoreType.DMA((3,)),
        ],
        compiler_params=pltpu.CompilerParams(vmem_limit_bytes=VMEM_BYTES),
    )(*in_hbm(x, tissue))


def gate_kernel(count, *refs):
    for x_ref, out_ref in zip(refs[:count], refs[len(refs) - count :]):
        out_ref[...] = x_ref[...]


def gate(arrays, after):
    count = len(arrays)
    return pl.pallas_call(
        functools.partial(gate_kernel, count),
        in_specs=[VMEM_SPEC] * count + [ANY_SPEC] * len(after),
        out_specs=[VMEM_SPEC] * count,
        out_shape=tuple(sds(x.shape, x.dtype) for x in arrays),
        input_output_aliases={i: i for i in range(count)},
        compiler_params=pltpu.CompilerParams(vmem_limit_bytes=VMEM_BYTES),
    )(*arrays, *after)


def units_kernel(
    x_ref, tissue_ref, probe_ref, after_ref,
    left_ref, right_ref, middle_ref, unit0_ref, unit1_ref,
    tile_ref, sems,
):
    rows, cols, patch, width = x_ref.shape
    run = GHOST
    order = [(row, c) for row in range(rows) for c in (0, cols - run)]
    order += [(row, c) for row in range(rows) for c in range(run, cols - run, run)]
    copies = fetched([x_ref.at[row, c : c + run] for row, c in order], [tile_ref.at[i] for i in range(len(order))], sems)
    masks = [by_sublane(tissue_ref[row]) for row in range(rows)]
    for i, (row, first) in enumerate(order):
        copies[i].wait()
        for k in range(run):
            c = first + k
            tile, column = tile_ref[i, k], masks[row][:, c : c + 1]
            unit, _ = unit_and_mask(tile)
            at = (GHOST + c) * patch
            (unit0_ref, unit1_ref)[row][at : at + patch, :] = unit * column.astype(bf16)
            if first == 0 or first == cols - run:
                side_ref = left_ref if first == 0 else right_ref
                side_ref[row, k, :, :width] = marked(tile, column)
                side_ref[row, k, :, width:] = four_of(probe_ref[row, c])
            if row == 0 and EDGE <= c < cols - EDGE:
                middle_ref[c - EDGE] = marked(tile, column)


def own_units(x, tissue, probe, after):
    rows, cols, patch, width = x.shape
    n = cols + 2 * GHOST
    side = sds((rows, GHOST, patch, width + 4 * RANK), bf16)
    unit = sds((n * patch, width), bf16)
    return pl.pallas_call(
        units_kernel,
        in_specs=[HBM_SPEC, VMEM_SPEC, VMEM_SPEC, ANY_SPEC],
        out_specs=[VMEM_SPEC] * 5,
        out_shape=(side, side, sds((cols - 2 * EDGE, patch, width), bf16), unit, unit),
        scratch_shapes=[
            pltpu.VMEM((rows * cols // GHOST, GHOST, patch, width), bf16),
            pltpu.SemaphoreType.DMA((rows * cols // GHOST,)),
        ],
        compiler_params=pltpu.CompilerParams(vmem_limit_bytes=VMEM_BYTES),
    )(*in_hbm(x), tissue, probe, after)


def bands(ranges, patch, unit0_ref, unit1_ref, m_ref, degree, diagonal):
    both = 2 * patch
    shape = (both, 3 * both)
    patch_of = iota(shape, 0)
    own = iota(shape, 1) == jnp.where(patch_of < patch, patch_of + patch, patch_of + 3 * patch)
    lane = iota((both, 128), 1)

    def band(e, carry):
        degree, diagonal = carry
        around = slice((e - 1) * patch, (e + 2) * patch)
        here = slice(e * patch, (e + 1) * patch)
        left = jnp.concatenate([unit0_ref[here, :], unit1_ref[here, :]], axis=0)
        right = jnp.concatenate([unit0_ref[around, :], unit1_ref[around, :]], axis=0)
        weights = affinity_of(left, right)
        others = jnp.where(own, 0.0, weights)
        m_ref[e] = others.astype(bf16)
        itself = jnp.sum(weights - others, axis=1, keepdims=True)
        degree = at_lane(lane, e, jnp.sum(weights, axis=1, keepdims=True), degree)
        diagonal = at_lane(lane, e, itself, diagonal)
        return degree, diagonal

    carry = (degree, diagonal)
    for low, high in ranges:
        for e in range(low, high):
            carry = band(e, carry)
    return carry


def inside_kernel(n, unit0_ref, unit1_ref, m_ref, sum_ref):
    patch = m_ref.shape[1] // 2
    empty = jnp.zeros((2 * patch, 128), f32)
    sum_ref[0], sum_ref[1] = bands([(GHOST + 1, n - GHOST - 1)], patch, unit0_ref, unit1_ref, m_ref, empty, empty)


def inside_affinity(unit0, unit1, patch):
    n = unit0.shape[0] // patch
    both = 2 * patch
    return pl.pallas_call(
        functools.partial(inside_kernel, n),
        out_shape=(sds((n, both, 3 * both), bf16), sds((2, both, 128), f32)),
        compiler_params=pltpu.CompilerParams(vmem_limit_bytes=VMEM_BYTES),
    )(unit0, unit1)


def outside_kernel(
    n,
    start0_ref, start1_ref, some_ref, tissue_ref, sum_ref, xl_ref, xr_ref, after_ref,
    unit0_ref, unit1_ref, m_ref, stat_ref,
):
    rows, count, patch, _ = xl_ref.shape
    width = unit0_ref.shape[1]
    cols = n - 2 * count
    both = rows * patch
    lane = iota((patch, 128), 1)

    kept = slice(count * patch, (count + cols) * patch)
    unit0_ref[kept, :] = start0_ref[kept, :]
    unit1_ref[kept, :] = start1_ref[kept, :]
    for e in range(count + 1, n - count - 1):
        m_ref[e] = some_ref[e]
    masks = []
    for row, unit_ref in ((0, unit0_ref), (1, unit1_ref)):
        own_mask = by_sublane(tissue_ref[row])
        mask = jnp.zeros((patch, 128), f32)
        for e in range(n):
            if e < count:
                unit, column = unit_and_mask(xl_ref[row, e, :, :width])
            elif e < count + cols:
                unit, column = None, own_mask[:, e - count : e - count + 1]
            else:
                unit, column = unit_and_mask(xr_ref[row, e - count - cols, :, :width])
            mask = at_lane(lane, e, column, mask)
            if unit is not None:
                unit_ref[e * patch : (e + 1) * patch, :] = unit
        masks.append(mask)
    mask = jnp.concatenate(masks, axis=0)
    ranges = [(1, GHOST + 1), (n - GHOST - 1, n - 1)]
    degree, diagonal = bands(ranges, patch, unit0_ref, unit1_ref, m_ref, sum_ref[0], sum_ref[1])
    degree = degree - FLOOR * absent_near(mask, 3 * both)
    stat_ref[0] = degree
    stat_ref[1] = diagonal
    stat_ref[2] = mask

def payload_rows(columns, patch):
    return columns * patch // 2 + patch // 2 + RANK * 3 // 2


def outside_affinity(unit0, unit1, m, tissue, sums, xl, xr, after):
    n, both, _ = m.shape
    unit = sds(unit0.shape, bf16)
    return pl.pallas_call(
        functools.partial(outside_kernel, n),
        in_specs=[VMEM_SPEC] * 7 + [ANY_SPEC],
        out_specs=[VMEM_SPEC] * 4,
        out_shape=(unit, unit, sds(m.shape, bf16), sds((3, both, 128), f32)),
        input_output_aliases={0: 0, 1: 1, 2: 2},
        compiler_params=pltpu.CompilerParams(vmem_limit_bytes=VMEM_BYTES),
    )(unit0, unit1, m, tissue, sums, xl, xr, after)


def start_kernel(factor, count, *refs):
    parts, (stat_ref, xl_ref, p_ref, xr_ref, panel_ref, pay_ref, base_ref) = refs[:count], refs[count:]
    rows, cols, patch, _ = p_ref.shape
    n = cols + 2 * GHOST
    half = patch // 2
    width = xl_ref.shape[3] - 4 * RANK
    inverse, root = inverse_factor(unpacked(balanced([part[...] for part in parts])), True)
    inverse, root = factor * inverse, root / factor
    error = identity(RANK).astype(f32) - turn_of(root, inverse)
    root = root + jnp.dot(error, root, precision=lax.Precision.HIGHEST, preferred_element_type=f32)
    base_ref[0], base_ref[1] = inverse, root
    for row in range(rows):
        tiles = [whole_of(xl_ref[row, c, :, width:]) for c in range(GHOST)]
        tiles += [p_ref[row, c] for c in range(cols)]
        tiles += [whole_of(xr_ref[row, c, :, width:]) for c in range(GHOST)]
        turned = lax.dot_general(
            jnp.concatenate(tiles, axis=0), inverse, ABT, precision=lax.Precision.HIGHEST, preferred_element_type=f32
        )
        for e in range(n):
            tile = turned[e * patch : (e + 1) * patch]
            panel_ref[row, e] = tile
            if row == 0 and 0 < e < n - 1:
                pay_ref[(e - 1) * half : e * half, :] = packed(tile).astype(bf16)
    tail = (n - 2) * half
    put_tail(pay_ref, tail, stat_ref[0, :patch], root)


def put_tail(pay_ref, tail, table, root):
    half = table.shape[0] // 2
    high, low = pair_of(jnp.where(iota(table.shape, 1) < 32, table, 0.0))
    both = high.astype(f32) + pltpu.roll(low.astype(f32), 32, 1)
    pay_ref[tail : tail + half, :] = (both[:half] + pltpu.roll(both[half:], 64, 1)).astype(bf16)
    pay_ref[tail + half :, :] = basis_rows(root)


def got_tail(got_ref, tail, patch):
    half = patch // 2
    both = got_ref[tail : tail + half, :].astype(f32)
    upper = both + pltpu.roll(both, 96, 1)
    lower = pltpu.roll(both, 64, 1) + pltpu.roll(both, 32, 1)
    return jnp.concatenate([upper, lower], axis=0), basis_of(got_ref[tail + half :, :])


def start_panel(factor, parts, stat, xl, own_panel, xr):
    rows, cols, patch, _ = own_panel.shape
    n = cols + 2 * GHOST
    return kernel_call(
        functools.partial(start_kernel, factor, len(parts)),
        (
            sds((rows, n, patch, RANK), f32),
            sds((payload_rows(n - 2, patch), 2 * RANK), bf16),
            sds((2, RANK, RANK), f32),
        ),
    )(*parts, stat, xl, own_panel, xr)


def cut_kernel(be_ref, after_ref, left_ref, right_ref):
    left_ref[...] = be_ref[:GHOST]
    right_ref[...] = be_ref[be_ref.shape[0] - GHOST :]


def cut(be, after):
    vmem = pl.BlockSpec(memory_space=pltpu.VMEM)
    side = sds((GHOST,) + be.shape[1:], be.dtype)
    return pl.pallas_call(
        cut_kernel,
        in_specs=[vmem, pl.BlockSpec(memory_space=pl.ANY)],
        out_specs=[vmem] * 2,
        out_shape=(side, side),
        compiler_params=pltpu.CompilerParams(vmem_limit_bytes=VMEM_BYTES),
    )(be, after)


def stages(n):
    middle = list(range(GHOST + EDGE, n - GHOST - EDGE))
    ends = [c for c in range(n) if c not in middle]
    arrived, seen, steps = set(), set(), []
    for tiles in (ends, middle):
        arrived |= set(tiles)
        columns = [e for e in range(1, n - 1) if {e - 1, e, e + 1} <= arrived and e not in seen]
        seen |= set(columns)
        steps.append((tiles, columns))
    return steps


def scale_of(stat_ref, sums):
    down_sum, _, mask = sums
    patch = mask.shape[0]
    degree = 1.0 + stat_ref[0, patch:] + down_sum - FLOOR * absent_near(mask, 3 * patch)
    return stat_ref[2, patch:] * lax.rsqrt(degree)


def pair_source(e, tiles):
    some = next(iter(tiles.values()))
    near = [tiles.get(c, jnp.zeros_like(some)) for c in range(e - 1, e + 3)]
    return jnp.concatenate(near, axis=0)


def pairs_of(columns):
    return sorted({e - (e + 1) % 2 for e in columns})


def pair_products(columns, block_ref, tiles):
    results = {}
    for e in pairs_of(columns):
        product = jnp.dot(block_ref[e // 2], pair_source(e, tiles), preferred_element_type=f32)
        patch = product.shape[0] // 2
        results[e], results[e + 1] = product[:patch], product[patch:]
    return results


def products(columns, up_ref, tiles, pay_ref, first):
    half = up_ref.shape[1] // 4
    results = pair_products(columns, up_ref, tiles)
    for e in columns:
        pay_ref[(e - first) * half : (e - first + 1) * half, :] = packed(results[e]).astype(bf16)


def cross_kernel(n, stage, *refs):
    steps = stages(n)
    tiles, columns = steps[stage]
    count = 3 if stage == 0 else 1
    pieces, (own_ref, stat_ref, p_ref, base_ref) = refs[:count], refs[count : count + 4]
    refs = refs[count + 4 :]
    patch = pieces[0].shape[1]
    lane = iota((patch, 128), 1)
    if stage == 0:
        v_ref, w_ref, sum_ref, u0_ref, pay_ref, unit_ref = refs
        empty = jnp.zeros((patch, 128), f32)
        down_sum, up_sum, mask = empty, empty, empty
    else:
        before, (v_ref, w_ref, sum_ref, u0_ref, pay_ref, unit_ref) = refs[:6], refs[6:12]
        down_sum, up_sum, mask = (before[2][i] for i in range(3))
        earlier = {e for _, reached in steps[:stage] for e in reached}
        for e in pairs_of(earlier):
            v_ref[e // 2] = before[0][e // 2]
            w_ref[e // 2] = before[1][e // 2]
        for e in sorted(earlier):
            u0_ref[e] = before[3][e]
        for e in sorted(e for e in earlier if e - 1 in earlier and e + 1 in earlier):
            span = slice((e - 2) * patch // 2, (e - 1) * patch // 2)
            pay_ref[span, :] = before[4][span, :]
        for c in sorted({c for e in columns for c in (e - 1, e, e + 1)} - set(tiles)):
            span = slice(c * patch, (c + 1) * patch)
            unit_ref[span, :] = before[5][span, :]
    sources = [(ref, i) for ref in pieces for i in range(ref.shape[0])]
    for c, (ref, i) in zip(tiles, sources):
        unit, column = unit_and_mask(ref[i])
        unit_ref[c * patch : (c + 1) * patch, :] = unit
        mask = at_lane(lane, c, column, mask)
    shape = (2 * patch, 4 * patch)
    apart = iota(shape, 1) // patch - iota(shape, 0) // patch
    beside = (apart >= 0) & (apart <= 2)
    for e in pairs_of(columns):
        around = slice((e - 1) * patch, (e + 3) * patch)
        here = slice(e * patch, (e + 2) * patch)
        down = jnp.where(beside, affinity_of(own_ref[here, :], unit_ref[around, :]), 0.0)
        up = jnp.where(beside, affinity_of(unit_ref[here, :], own_ref[around, :]), 0.0)
        v_ref[e // 2] = down.astype(bf16)
        w_ref[e // 2] = up.astype(bf16)
        down = jnp.sum(down, axis=1, keepdims=True)
        up = jnp.sum(up, axis=1, keepdims=True)
        for i in range(2):
            span = slice(i * patch, (i + 1) * patch)
            down_sum = at_lane(lane, e + i, down[span], down_sum)
            up_sum = at_lane(lane, e + i, up[span], up_sum)
    sums = (down_sum, up_sum, mask)
    scale = scale_of(stat_ref, sums)
    for e in columns:
        u0_ref[e] = (scale[:, e : e + 1] * p_ref[1, e]).astype(bf16)
    inner, known = [], []
    for last in (stage - 1, stage):
        known = [e for _, reached in steps[: last + 1] for e in reached]
        inner.append({e for e in range(2, n - 2) if {e - 1, e, e + 1} <= set(known)})
    fresh = sorted(inner[1] - inner[0])
    near = {c for e in fresh for c in (e - 1, e, e + 1)}
    products(fresh, w_ref, {e: u0_ref[e] for e in near}, pay_ref, 2)
    if stage < len(steps) - 1:
        for i in range(3):
            sum_ref[i] = sums[i]
        return
    shared = up_sum - FLOOR * absent_near(stat_ref[2, patch:], 3 * patch)
    sum_ref[0], sum_ref[1], sum_ref[2] = shared, mask, scale
    tail = (n - 4) * patch // 2
    put_tail(pay_ref, tail, shared, base_ref[1])


def cross_affinity(stage, pieces, u1, stat, panel, base, before=()):
    patch, width = pieces[0].shape[1:]
    n = u1.shape[0] // patch
    given = len(pieces) + 4
    return pl.pallas_call(
        functools.partial(cross_kernel, n, stage),
        out_shape=(
            sds((n // 2 - 1, 2 * patch, 4 * patch), bf16),
            sds((n // 2 - 1, 2 * patch, 4 * patch), bf16),
            sds((3, patch, 128), f32),
            sds((n, patch, RANK), bf16),
            sds((payload_rows(n - 4, patch), 2 * RANK), bf16),
            sds((n * patch, width), bf16),
        ),
        input_output_aliases={given + i: i for i in range(len(before))},
        compiler_params=pltpu.CompilerParams(vmem_limit_bytes=VMEM_BYTES),
    )(*pieces, u1, stat, panel, base, *before)


def before_first_kernel(
    n,
    got_ref, sum_ref, stat_ref, u0_ref, m_ref, v_ref, base_ref,
    z_ref, t_ref, gain_ref, own_ref, turn_ref,
):
    patch = u0_ref.shape[1]
    half = patch // 2
    tail = (n - 2) * half
    partial, theirs = got_tail(got_ref, tail, patch)
    below_scale = sum_ref[1] * lax.rsqrt(1.0 + partial + sum_ref[0])
    scale = sum_ref[2]
    gain = 1.0 + scale * scale * stat_ref[1, patch:]
    upper = stat_ref[1, :patch]
    turn = pair_of(turn_of(theirs, base_ref[0]))
    turn_ref[0], turn_ref[1] = turn
    tiles = [unpacked(got_ref[(e - 1) * half : e * half, :].astype(f32)) for e in range(1, n - 1)]
    tiles = turned([below_scale[:, e : e + 1] * tile for e, tile in zip(range(1, n - 1), tiles)], turn)
    lower = pair_products(range(2, n - 2), v_ref, {e: tile.astype(bf16) for e, tile in zip(range(1, n - 1), tiles)})
    for e in range(2, n - 2):
        own = u0_ref[e - 1 : e + 2].reshape(3 * patch, RANK)
        total = jnp.dot(m_ref[e, :, 3 * patch :], own, preferred_element_type=f32)
        z_ref[e, :patch] = total[:patch]
        z_ref[e, patch:] = total[patch:] + lower[e]
        for ref, table in ((t_ref, scale), (gain_ref, gain), (own_ref, upper)):
            ref[e] = jnp.broadcast_to(table[:, e : e + 1], (patch, RANK))


def before_first(got, sums, stat, u0, m, v, base):
    n, patch, _ = u0.shape
    spread = sds((n, patch, RANK), f32)
    return kernel_call(
        functools.partial(before_first_kernel, n),
        (sds((n, 2 * patch, RANK), f32), spread, spread, spread, sds((2, RANK, RANK), bf16)),
    )(got, sums, stat, u0, m, v, base)


def first_kernel(
    n,
    got_ref, stat_ref, t1_ref, gain1_ref, own_ref, z_ref, p_ref, m_ref, w_ref, base_ref,
    y_ref, u_ref, t0_ref, gain0_ref, up_ref, down_ref, turn_ref,
    start_ref,
):
    patch = t1_ref.shape[1]
    half = patch // 2
    tail = (n - 4) * half
    partial, theirs = got_tail(got_ref, tail, patch)
    turn = pair_of(turn_of(theirs, base_ref[0]))
    turn_ref[0], turn_ref[1] = turn
    above = turned([unpacked(got_ref[(e - 2) * half : (e - 1) * half, :]) for e in range(2, n - 2)], turn)
    scale = stat_ref[2, :patch] * lax.rsqrt(1.0 + stat_ref[0, :patch] + partial)
    for e in range(1, n - 1):
        t = jnp.broadcast_to(scale[:, e : e + 1], (patch, RANK))
        t0_ref[e] = t
        start_ref[e] = (t * p_ref[0, e]).astype(bf16)
    for e in range(2, n - 2):
        own = start_ref[e - 1 : e + 2].reshape(3 * patch, RANK)
        total = z_ref[e] + jnp.dot(m_ref[e, :, : 3 * patch], own, preferred_element_type=f32)
        upper = total[:patch] + above[e - 2]
        gain = 1.0 + t0_ref[e] * t0_ref[e] * own_ref[e]
        gain0_ref[e] = gain
        for row, piece, t, g in ((0, upper, t0_ref[e], gain), (1, total[patch:], t1_ref[e], gain1_ref[e])):
            image = p_ref[row, e] * g + t * piece
            y_ref[row, e] = image
            scaled = t * image
            u_ref[row, e] = scaled.astype(bf16)
            if row == 0:
                up_ref[(e - 2) * half : (e - 1) * half, :] = packed(scaled).astype(bf16)
    products(range(3, n - 3), w_ref, {e: u_ref[1, e] for e in range(2, n - 2)}, down_ref, 3)


def first_iteration(got, stat, t1, gain1, own, z, panel, m, w, base):
    n, both, _ = z.shape
    patch = both // 2
    half = patch // 2
    spread = sds((n, patch, RANK), f32)
    return kernel_call(
        functools.partial(first_kernel, n),
        (
            sds((2, n, patch, RANK), f32),
            sds((2, n, patch, RANK), bf16),
            spread,
            spread,
            sds(((n - 4) * half, 2 * RANK), bf16),
            sds(((n - 6) * half, 2 * RANK), bf16),
            sds((2, RANK, RANK), bf16),
        ),
        [pltpu.VMEM((n, patch, RANK), bf16)],
    )(got, stat, t1, gain1, own, z, panel, m, w, base)


def local_kernel(low, high, m_ref, u_ref, z_ref):
    patch = u_ref.shape[2]
    for e in range(low, high):
        upper = u_ref[0, e - 1 : e + 2].reshape(3 * patch, RANK)
        lower = u_ref[1, e - 1 : e + 2].reshape(3 * patch, RANK)
        z_ref[e] = jnp.dot(m_ref[e], jnp.concatenate([upper, lower], axis=0), preferred_element_type=f32)


def local_products(low, high, m, u):
    n, both, _ = m.shape
    return kernel_call(
        functools.partial(local_kernel, low, high),
        sds((n, both, RANK), f32),
    )(m, u)


def images_of(n, low, below_ref, above_ref, z_ref, y_ref, scales, gains, turns, v_ref):
    patch = y_ref.shape[2]
    half = patch // 2
    count = n - 2 * low
    down, up = ((ref[0], ref[1]) for ref in turns)
    near = turned([unpacked(below_ref[i * half : (i + 1) * half, :]) for i in range(count + 2)], down)
    near = {low - 1 + i: tile.astype(bf16) for i, tile in enumerate(near)}
    lower = pair_products(range(low, n - low), v_ref, near)
    upper = turned([unpacked(above_ref[i * half : (i + 1) * half, :]) for i in range(count)], up)
    for e in range(low, n - low):
        pieces = (z_ref[e, :patch] + upper[e - low], z_ref[e, patch:] + lower[e])
        yield e, [y_ref[row, e] * gains[row][e] + scales[row][e] * pieces[row] for row in range(2)]


def middle_step_kernel(
    n, low,
    below_ref, above_ref, z_ref, y_ref, t0_ref, t1_ref, gain0_ref, gain1_ref, turn0_ref, turn1_ref, v_ref, w_ref,
    new_ref, u_ref, up_ref, down_ref,
):
    patch = y_ref.shape[2]
    half = patch // 2
    scales, gains = (t0_ref, t1_ref), (gain0_ref, gain1_ref)
    turns = (turn0_ref, turn1_ref)
    for e, images in images_of(n, low, below_ref, above_ref, z_ref, y_ref, scales, gains, turns, v_ref):
        for row in range(2):
            new_ref[row, e] = images[row]
            scaled = scales[row][e] * images[row]
            u_ref[row, e] = scaled.astype(bf16)
            if row == 0:
                up_ref[(e - low) * half : (e - low + 1) * half, :] = packed(scaled).astype(bf16)
    products(
        range(low + 1, n - low - 1), w_ref, {e: u_ref[1, e] for e in range(low, n - low)}, down_ref, low + 1
    )


def middle_step(low, below, above, z, y, spread, v, w):
    _, n, patch, _ = y.shape
    half = patch // 2
    return kernel_call(
        functools.partial(middle_step_kernel, n, low),
        (
            sds((2, n, patch, RANK), f32),
            sds((2, n, patch, RANK), bf16),
            sds(((n - 2 * low) * half, 2 * RANK), bf16),
            sds(((n - 2 * low - 2) * half, 2 * RANK), bf16),
        ),
    )(below, above, z, y, *spread, v, w)


def last_step_kernel(
    n, low,
    below_ref, above_ref, z_ref, y_ref, t0_ref, t1_ref, gain0_ref, gain1_ref, turn0_ref, turn1_ref, v_ref,
    new_ref, gram_ref, side_ref,
):
    patch = y_ref.shape[2]
    scales, gains = (t0_ref, t1_ref), (gain0_ref, gain1_ref)
    wide = 2 * RANK
    turns = (turn0_ref, turn1_ref)
    for e, images in images_of(n, low, below_ref, above_ref, z_ref, y_ref, scales, gains, turns, v_ref):
        for row in range(2):
            new_ref[row, e - low] = images[row]
        span = slice((e - low) * patch, (e - low + 1) * patch)
        side_ref[span, :wide], side_ref[span, wide:] = pair_of(jnp.concatenate(images, axis=1))
    gram_ref[...] = folded_gram(side_ref[...])


def last_step(low, below, above, z, y, spread, v):
    _, n, patch, _ = y.shape
    cols = n - 2 * low
    return kernel_call(
        functools.partial(last_step_kernel, n, low),
        (sds((2, cols, patch, RANK), f32), sds((RANK // 2, 2 * RANK), f32)),
        [pltpu.VMEM((cols * patch, 4 * RANK), bf16)],
    )(below, above, z, y, *spread, v)


def inverse_factor(gram, bounded=False):
    size = gram.shape[0]
    least = 0.0
    if bounded:
        least = 1e-6 * jnp.sum(jnp.where(identity(size), gram, 0.0), axis=1, keepdims=True) + 1e-16
    step = 8
    row = iota((size, 2 * size), 0)
    lane = iota((size, 2 * size), 1)
    table = jnp.concatenate([gram, identity(size).astype(f32)], axis=1)
    for k in range(0, size, step):
        cols = [jnp.broadcast_to(table[:, k + i : k + i + 1], table.shape) for i in range(step)]
        lines = [table[k + i : k + i + 1, :] for i in range(step)]
        for i in range(step):
            pivot = cols[i][k + i : k + i + 1, :]
            inverse = 1.0 / (jnp.maximum(pivot, least[k + i : k + i + 1, :]) if bounded else pivot)
            for j in range(i + 1, step):
                lines[j] = lines[j] - lines[i] * (cols[i][k + j : k + j + 1, :] * inverse)
                cols[j] = cols[j] - cols[i] * (cols[j][k + i : k + i + 1, :] * inverse)
            table = table - jnp.where(row > k + i, cols[i], 0.0) * (lines[i] * inverse)
    pivots = jnp.sum(jnp.where(row == lane, table, 0.0), axis=1, keepdims=True)
    if not bounded:
        return table[:, size:] * lax.rsqrt(pivots)
    pivots = jnp.maximum(pivots, least)
    row, lane = row[:, :size], lane[:, :size]
    upper = jnp.where(lane > row, table[:, :size], jnp.where(lane == row, pivots, 0.0))
    return table[:, size:] * lax.rsqrt(pivots), upper * lax.rsqrt(pivots)


def balanced(parts):
    while len(parts) > 1:
        parts = [a + b for a, b in zip(parts[::2], parts[1::2])]
    return parts[0]


def joint_gram(parts, base_ref):
    size = RANK // 2
    turns = turn_of(jnp.concatenate([unpacked(part[size:, :]) for part in parts[1:]], axis=0), base_ref[0])
    first = []
    for i, part in enumerate(parts[1:]):
        turn = turns[i * RANK : (i + 1) * RANK]
        first.append(
            jnp.dot(
                unpacked(part[:size, :]), turn, precision=lax.Precision.HIGHEST, preferred_element_type=f32
            )
        )
    others = lax.dot_general(
        turns, jnp.concatenate(first, axis=0), ATB, precision=lax.Precision.HIGHEST, preferred_element_type=f32
    )
    return unpacked(parts[0][:size, :]) + others


def joint_kernel(count, *refs):
    refs[-1][: RANK // 2, :] = packed(joint_gram(refs[:count], refs[count]))
    refs[-1][RANK // 2 :, :] = packed(refs[count][1])


def joint(parts, base):
    return kernel_call(functools.partial(joint_kernel, len(parts)), sds(parts[0].shape, f32))(*parts, base)


def finish_kernel(factor, count, *refs):
    parts, (base_ref, y_ref, out_ref) = refs[:count], refs[count:]
    inverse = factor * inverse_factor(joint_gram(parts, base_ref))
    zero = jnp.zeros_like(inverse)
    both = jnp.concatenate(
        [jnp.concatenate([inverse, zero], axis=1), jnp.concatenate([zero, inverse], axis=1)], axis=0
    )
    wide = 2 * RANK
    tiles, width = y_ref.shape
    pieces = [y_ref[:, q * wide : (q + 1) * wide] for q in range(width // wide)]
    y_high, y_low = pair_of(jnp.concatenate(pieces, axis=0))
    t_high, t_low = pair_of(both)

    def times(a, b):
        return lax.dot_general(a, b, ABT, preferred_element_type=f32)

    out = times(y_high, t_high) + (times(y_low, t_high) + times(y_high, t_low))
    for q in range(width // wide):
        out_ref[:, q * wide : (q + 1) * wide] = out[q * tiles : (q + 1) * tiles]


def finish(factor, parts, base, y):
    return kernel_call(
        functools.partial(finish_kernel, factor, len(parts)),
        sds(y.shape, f32),
    )(*parts, base, y)


def exchange_stages(axis):
    size = lax.axis_size(axis)
    stages, bit = [], 1
    if axis == "col":
        stages.append([1])
        bit = 2
    while bit < size:
        if 2 * bit < size:
            stages.append([bit, 2 * bit, 3 * bit])
            bit *= 4
        else:
            stages.append([bit])
            bit *= 2
    return stages


def summed_parts(gram, axis, combine):
    size = lax.axis_size(axis)
    parts = [gram]
    for partners in exchange_stages(axis):
        gram = combine(parts) if len(parts) > 1 else gram
        parts = [gram] + [lax.ppermute(gram, axis, [(i, i ^ p) for i in range(size)]) for p in partners]
    return parts


def passed_along(shard, axis, by):
    count = lax.axis_size(axis)
    pairs = [(i, i + by) for i in range(count) if 0 <= i + by < count]
    return lax.ppermute(shard, axis, pairs)


def local(features, tissue, probe):
    tile_rows, tile_cols, patches, width = features.shape
    total = tile_rows * lax.axis_size("row") * tile_cols * lax.axis_size("col") * patches
    factor = math.sqrt(float(total))
    edges = mark_edges(features, tissue)
    below_edges = passed_along(edges, "row", -1)
    parts = summed_parts(start_gram(probe), "col", balanced)
    own_panel = probe.reshape(tile_rows, tile_cols, patches, RANK)
    left_end, right_end, middle, unit0, unit1 = own_units(features, tissue, own_panel, edges)
    left_end, right_end = gate((left_end, right_end), parts)
    from_left = passed_along(right_end, "col", 1)
    from_right = passed_along(left_end, "col", -1)
    below_middle = passed_along(middle, "row", -1)
    m, sums = inside_affinity(unit0, unit1, patches)
    below_left, below_right = cut(below_edges, sums)
    _, u1, m, stat = outside_affinity(unit0, unit1, m, tissue, sums, from_left, from_right, below_left)
    panel, payload, base = start_panel(factor, parts, stat, from_left, own_panel, from_right)
    below_left, below_right = passed_along(below_right, "col", 1), passed_along(below_left, "col", -1)
    got_below = passed_along(payload, "row", -1)
    n = tile_cols + 2 * GHOST
    cross = cross_affinity(0, (below_left, below_edges, below_right), u1, stat, panel, base)
    v, w, sums, u0, payload, _ = cross_affinity(1, (below_middle,), u1, stat, panel, base, cross)
    got_above = passed_along(payload, "row", 1)
    z, t1, gain1, own, turn0 = before_first(got_below, sums, stat, u0, m, v, base)
    y, u, t0, gain0, up, down, turn1 = first_iteration(got_above, stat, t1, gain1, own, z, panel, m, w, base)
    spread = (t0, t1, gain0, gain1, turn0, turn1)
    below, above = passed_along(up, "row", -1), passed_along(down, "row", 1)
    z = local_products(3, n - 3, m, u)
    y, u, up, down = middle_step(3, below, above, z, y, spread, v, w)
    below, above = passed_along(up, "row", -1), passed_along(down, "row", 1)
    z = local_products(4, n - 4, m, u)
    y, gram = last_step(4, below, above, z, y, spread, v)

    gram = balanced(summed_parts(gram, "col", balanced))
    root = jnp.concatenate([base[1, : RANK // 2], base[1, RANK // 2 :]], axis=1)
    parts = summed_parts(jnp.concatenate([gram, root], axis=0), "row", lambda parts: joint(parts, base))
    flat = y.reshape(tile_rows * tile_cols, patches * RANK)
    out = finish(factor, parts, base, flat)
    return out.reshape(tile_rows, tile_cols, patches * RANK)


def solution(mesh):
    placed = (P("row", "col", None, None), P("row", "col", None), P("row", "col", None))
    return jax.shard_map(
        local, mesh=mesh, in_specs=placed, out_specs=P("row", "col", None), check_vma=False
    )
```

```python
import functools
import math

import jax
import jax.numpy as jnp
from jax import lax
from jax.experimental import pallas as pl
from jax.experimental.pallas import tpu as pltpu
from jax.sharding import PartitionSpec as P

RANK = 64
ITERS = 3
AFFINITY_TEMP = 4.0

GHOST = ITERS + 1
EDGE = 4
TINY = 1e-30
VMEM_BYTES = 16 * 1024 * 1024
FLOOR = math.exp(-AFFINITY_TEMP)
ABT = (((1,), (1,)), ((), ()))
ATB = (((0,), (0,)), ((), ()))

f32 = jnp.float32
bf16 = jnp.bfloat16


def kernel_call(body, out_shape, scratch=()):
    return pl.pallas_call(
        body,
        out_shape=out_shape,
        scratch_shapes=list(scratch),
        compiler_params=pltpu.CompilerParams(vmem_limit_bytes=VMEM_BYTES),
    )


def sds(shape, dtype):
    return jax.ShapeDtypeStruct(shape, dtype)


def iota(shape, dim):
    return lax.broadcasted_iota(jnp.int32, shape, dim)


def identity(n):
    return iota((n, n), 0) == iota((n, n), 1)


def unit_and_mask(block):
    values = block.astype(f32)
    scaled = values * lax.rsqrt(jnp.sum(values * values, axis=-1, keepdims=True) + 1e-06)
    return scaled.astype(bf16), (values[:, :1] != 0.0).astype(f32)


def affinity_of(left, right):
    scores = lax.dot_general(left, right, ABT, preferred_element_type=f32)
    return jnp.exp(AFFINITY_TEMP * scores - AFFINITY_TEMP)


def at_lane(lane, e, column, table):
    return jnp.where(lane == e, column, table)


def absent_near(mask, width):
    count = jnp.sum(mask, axis=0, keepdims=True)
    return width - (pltpu.roll(count, 1, 1) + count + pltpu.roll(count, 127, 1))


def packed(block):
    half = block.shape[0] // 2
    return jnp.concatenate([block[:half], block[half:]], axis=1)


def unpacked(block):
    return jnp.concatenate([block[:, :RANK], block[:, RANK:]], axis=0)


def pair_of(values):
    high = values.astype(bf16)
    return high, (values - high.astype(f32)).astype(bf16)


def four_of(values):
    high, middle = pair_of(values)
    low = (values - high.astype(f32) - middle.astype(f32)).astype(bf16)
    return jnp.concatenate([high, middle, low, jnp.zeros_like(low)], axis=1)


def basis_rows(table):
    parts = four_of(table)
    return jnp.concatenate([parts[:, : 2 * RANK], packed(parts[:, 2 * RANK : 3 * RANK])], axis=0)


def basis_of(rows):
    rows = rows.astype(f32)
    return rows[:RANK, :RANK] + rows[:RANK, RANK:] + unpacked(rows[RANK:])


def turn_of(theirs, inverse):
    return lax.dot_general(
        theirs, inverse, ABT, precision=lax.Precision.HIGHEST, preferred_element_type=f32
    )


def turned(tiles, turn):
    patch = tiles[0].shape[0]
    stack = jnp.concatenate(tiles, axis=0).astype(bf16)
    high, low = turn
    result = jnp.dot(stack, high, preferred_element_type=f32) + jnp.dot(stack, low, preferred_element_type=f32)
    return [result[i * patch : (i + 1) * patch] for i in range(len(tiles))]


def whole_of(parts):
    parts = parts.astype(f32)
    return parts[:, :RANK] + parts[:, RANK : 2 * RANK] + parts[:, 2 * RANK : 3 * RANK]


def by_sublane(tissue):
    mask = (tissue != 0).astype(bf16)
    return lax.dot_general(mask, identity(mask.shape[0]).astype(bf16), ATB, preferred_element_type=f32)


def marked(tile, column):
    zero = (iota(tile.shape, 1) == 0) & (tile == 0)
    return jnp.where(zero, jnp.asarray(TINY, bf16), tile) * column.astype(bf16)


def fetched(sources, slots, sems):
    copies = [pltpu.make_async_copy(source, slot, sems.at[i]) for i, (source, slot) in enumerate(zip(sources, slots))]
    for copy in copies:
        copy.start()
    return copies


def in_hbm(*arrays):
    return tuple(pltpu.with_memory_space_constraint(array, pltpu.HBM) for array in arrays)


VMEM_SPEC = pl.BlockSpec(memory_space=pltpu.VMEM)
HBM_SPEC = pl.BlockSpec(memory_space=pltpu.HBM)
ANY_SPEC = pl.BlockSpec(memory_space=pl.ANY)


def folded_gram(side):
    wide = 2 * RANK
    gram = lax.dot_general(side, side, ATB, preferred_element_type=f32)
    gram = gram[:wide] + gram[wide:]
    gram = gram[:, :wide] + gram[:, wide:]
    return packed(gram[:RANK, :RANK] + gram[RANK:, RANK:])


def start_gram_kernel(probe_ref, gram_ref, flat_ref, sems):
    rows, cols, width = probe_ref.shape
    (copy,) = fetched([probe_ref], [flat_ref], sems)
    copy.wait()
    wide = 2 * RANK
    spans = [slice(q * wide, (q + 1) * wide) for q in range(width // wide)]
    side = jnp.concatenate([flat_ref[row, :, span] for row in range(rows) for span in spans], axis=0)
    gram_ref[...] = folded_gram(jnp.concatenate(pair_of(side), axis=1))


def start_gram(probe):
    return pl.pallas_call(
        start_gram_kernel,
        in_specs=[HBM_SPEC],
        out_specs=VMEM_SPEC,
        out_shape=sds((RANK // 2, 2 * RANK), f32),
        scratch_shapes=[pltpu.VMEM(probe.shape, f32), pltpu.SemaphoreType.DMA((1,))],
        compiler_params=pltpu.CompilerParams(vmem_limit_bytes=VMEM_BYTES),
    )(*in_hbm(probe))


def mark_edges_kernel(x_ref, tissue_ref, edge_ref, tile_ref, mask_ref, sems):
    cols = x_ref.shape[1]
    sources = [tissue_ref.at[0], x_ref.at[0, :EDGE], x_ref.at[0, cols - EDGE :]]
    copies = fetched(sources, [mask_ref, tile_ref.at[:EDGE], tile_ref.at[EDGE:]], sems)
    copies[0].wait()
    mask = by_sublane(mask_ref[...])
    for side, first in ((0, 0), (1, cols - EDGE)):
        copies[1 + side].wait()
        for i in range(EDGE):
            at = side * EDGE + i
            edge_ref[at] = marked(tile_ref[at], mask[:, first + i : first + i + 1])


def mark_edges(x, tissue):
    rows, cols, patch, width = x.shape
    shape = (2 * EDGE, patch, width)
    return pl.pallas_call(
        mark_edges_kernel,
        in_specs=[HBM_SPEC, HBM_SPEC],
        out_specs=VMEM_SPEC,
        out_shape=sds(shape, bf16),
        scratch_shapes=[
            pltpu.VMEM(shape, bf16),
            pltpu.VMEM((cols, patch), jnp.int32),
            pltpu.SemaphoreType.DMA((3,)),
        ],
        compiler_params=pltpu.CompilerParams(vmem_limit_bytes=VMEM_BYTES),
    )(*in_hbm(x, tissue))


def gate_kernel(count, *refs):
    for x_ref, out_ref in zip(refs[:count], refs[len(refs) - count :]):
        out_ref[...] = x_ref[...]


def gate(arrays, after):
    count = len(arrays)
    return pl.pallas_call(
        functools.partial(gate_kernel, count),
        in_specs=[VMEM_SPEC] * count + [ANY_SPEC] * len(after),
        out_specs=[VMEM_SPEC] * count,
        out_shape=tuple(sds(x.shape, x.dtype) for x in arrays),
        input_output_aliases={i: i for i in range(count)},
        compiler_params=pltpu.CompilerParams(vmem_limit_bytes=VMEM_BYTES),
    )(*arrays, *after)


def ends_kernel(x_ref, tissue_ref, probe_ref, left_ref, right_ref, tile_ref, sems):
    rows, cols, patch, width = x_ref.shape
    order = [(row, c) for row in range(rows) for c in (0, cols - GHOST)]
    sources = [x_ref.at[row, c : c + GHOST] for row, c in order]
    copies = fetched(sources, [tile_ref.at[i] for i in range(len(order))], sems)
    masks = [by_sublane(tissue_ref[row]) for row in range(rows)]
    for i, (row, first) in enumerate(order):
        copies[i].wait()
        side_ref = right_ref if first else left_ref
        for k in range(GHOST):
            c = first + k
            side_ref[row, k, :, :width] = marked(tile_ref[i, k], masks[row][:, c : c + 1])
            side_ref[row, k, :, width:] = four_of(probe_ref[row, c])


def mark_ends(x, tissue, probe):
    rows, cols, patch, width = x.shape
    side = sds((rows, GHOST, patch, width + 4 * RANK), bf16)
    return pl.pallas_call(
        ends_kernel,
        in_specs=[HBM_SPEC, VMEM_SPEC, VMEM_SPEC],
        out_specs=[VMEM_SPEC] * 2,
        out_shape=(side, side),
        scratch_shapes=[
            pltpu.VMEM((2 * rows, GHOST, patch, width), bf16),
            pltpu.SemaphoreType.DMA((2 * rows,)),
        ],
        compiler_params=pltpu.CompilerParams(vmem_limit_bytes=VMEM_BYTES),
    )(*in_hbm(x), tissue, probe)


def units_kernel(x_ref, tissue_ref, after_ref, middle_ref, unit0_ref, unit1_ref, tile_ref, sems):
    rows, cols, patch, width = x_ref.shape
    run = GHOST
    order = [(row, c) for row in range(rows) for c in range(0, cols, run)]
    copies = fetched([x_ref.at[row, c : c + run] for row, c in order], [tile_ref.at[i] for i in range(len(order))], sems)
    masks = [by_sublane(tissue_ref[row]) for row in range(rows)]
    for i, (row, first) in enumerate(order):
        copies[i].wait()
        for k in range(run):
            c = first + k
            tile, column = tile_ref[i, k], masks[row][:, c : c + 1]
            unit, _ = unit_and_mask(tile)
            at = (GHOST + c) * patch
            (unit0_ref, unit1_ref)[row][at : at + patch, :] = unit * column.astype(bf16)
            if row == 0 and EDGE <= c < cols - EDGE:
                middle_ref[c - EDGE] = marked(tile, column)


def own_units(x, tissue, after):
    rows, cols, patch, width = x.shape
    n = cols + 2 * GHOST
    unit = sds((n * patch, width), bf16)
    return pl.pallas_call(
        units_kernel,
        in_specs=[HBM_SPEC, VMEM_SPEC, ANY_SPEC],
        out_specs=[VMEM_SPEC] * 3,
        out_shape=(sds((cols - 2 * EDGE, patch, width), bf16), unit, unit),
        scratch_shapes=[
            pltpu.VMEM((rows * cols // GHOST, GHOST, patch, width), bf16),
            pltpu.SemaphoreType.DMA((rows * cols // GHOST,)),
        ],
        compiler_params=pltpu.CompilerParams(vmem_limit_bytes=VMEM_BYTES),
    )(*in_hbm(x), tissue, after)


def bands(ranges, patch, unit0_ref, unit1_ref, m_ref, degree, diagonal):
    both = 2 * patch
    shape = (both, 3 * both)
    patch_of = iota(shape, 0)
    own = iota(shape, 1) == jnp.where(patch_of < patch, patch_of + patch, patch_of + 3 * patch)
    lane = iota((both, 128), 1)

    def band(e, carry):
        degree, diagonal = carry
        around = slice((e - 1) * patch, (e + 2) * patch)
        here = slice(e * patch, (e + 1) * patch)
        left = jnp.concatenate([unit0_ref[here, :], unit1_ref[here, :]], axis=0)
        right = jnp.concatenate([unit0_ref[around, :], unit1_ref[around, :]], axis=0)
        weights = affinity_of(left, right)
        others = jnp.where(own, 0.0, weights)
        m_ref[e] = others.astype(bf16)
        itself = jnp.sum(weights - others, axis=1, keepdims=True)
        degree = at_lane(lane, e, jnp.sum(weights, axis=1, keepdims=True), degree)
        diagonal = at_lane(lane, e, itself, diagonal)
        return degree, diagonal

    carry = (degree, diagonal)
    for low, high in ranges:
        for e in range(low, high):
            carry = band(e, carry)
    return carry


def inside_kernel(n, unit0_ref, unit1_ref, m_ref, sum_ref):
    patch = m_ref.shape[1] // 2
    empty = jnp.zeros((2 * patch, 128), f32)
    sum_ref[0], sum_ref[1] = bands([(GHOST + 1, n - GHOST - 1)], patch, unit0_ref, unit1_ref, m_ref, empty, empty)


def inside_affinity(unit0, unit1, patch):
    n = unit0.shape[0] // patch
    both = 2 * patch
    return pl.pallas_call(
        functools.partial(inside_kernel, n),
        out_shape=(sds((n, both, 3 * both), bf16), sds((2, both, 128), f32)),
        compiler_params=pltpu.CompilerParams(vmem_limit_bytes=VMEM_BYTES),
    )(unit0, unit1)


def outside_kernel(
    n,
    start0_ref, start1_ref, some_ref, tissue_ref, sum_ref, xl_ref, xr_ref, after_ref,
    unit0_ref, unit1_ref, m_ref, stat_ref,
):
    rows, count, patch, _ = xl_ref.shape
    width = unit0_ref.shape[1]
    cols = n - 2 * count
    both = rows * patch
    lane = iota((patch, 128), 1)

    kept = slice(count * patch, (count + cols) * patch)
    unit0_ref[kept, :] = start0_ref[kept, :]
    unit1_ref[kept, :] = start1_ref[kept, :]
    for e in range(count + 1, n - count - 1):
        m_ref[e] = some_ref[e]
    masks = []
    for row, unit_ref in ((0, unit0_ref), (1, unit1_ref)):
        own_mask = by_sublane(tissue_ref[row])
        mask = jnp.zeros((patch, 128), f32)
        for e in range(n):
            if e < count:
                unit, column = unit_and_mask(xl_ref[row, e, :, :width])
            elif e < count + cols:
                unit, column = None, own_mask[:, e - count : e - count + 1]
            else:
                unit, column = unit_and_mask(xr_ref[row, e - count - cols, :, :width])
            mask = at_lane(lane, e, column, mask)
            if unit is not None:
                unit_ref[e * patch : (e + 1) * patch, :] = unit
        masks.append(mask)
    mask = jnp.concatenate(masks, axis=0)
    ranges = [(1, GHOST + 1), (n - GHOST - 1, n - 1)]
    degree, diagonal = bands(ranges, patch, unit0_ref, unit1_ref, m_ref, sum_ref[0], sum_ref[1])
    degree = degree - FLOOR * absent_near(mask, 3 * both)
    stat_ref[0] = degree
    stat_ref[1] = diagonal
    stat_ref[2] = mask

def payload_rows(columns, patch):
    return columns * patch // 2 + patch // 2 + RANK * 3 // 2


def outside_affinity(unit0, unit1, m, tissue, sums, xl, xr, after):
    n, both, _ = m.shape
    unit = sds(unit0.shape, bf16)
    return pl.pallas_call(
        functools.partial(outside_kernel, n),
        in_specs=[VMEM_SPEC] * 7 + [ANY_SPEC],
        out_specs=[VMEM_SPEC] * 4,
        out_shape=(unit, unit, sds(m.shape, bf16), sds((3, both, 128), f32)),
        input_output_aliases={0: 0, 1: 1, 2: 2},
        compiler_params=pltpu.CompilerParams(vmem_limit_bytes=VMEM_BYTES),
    )(unit0, unit1, m, tissue, sums, xl, xr, after)


def start_kernel(factor, count, *refs):
    parts, (stat_ref, xl_ref, p_ref, xr_ref, panel_ref, pay_ref, base_ref) = refs[:count], refs[count:]
    rows, cols, patch, _ = p_ref.shape
    n = cols + 2 * GHOST
    half = patch // 2
    width = xl_ref.shape[3] - 4 * RANK
    inverse, root = inverse_factor(unpacked(balanced([part[...] for part in parts])), True)
    inverse, root = factor * inverse, root / factor
    error = identity(RANK).astype(f32) - turn_of(root, inverse)
    root = root + jnp.dot(error, root, precision=lax.Precision.HIGHEST, preferred_element_type=f32)
    base_ref[0], base_ref[1] = inverse, root
    for row in range(rows):
        tiles = [whole_of(xl_ref[row, c, :, width:]) for c in range(GHOST)]
        tiles += [p_ref[row, c] for c in range(cols)]
        tiles += [whole_of(xr_ref[row, c, :, width:]) for c in range(GHOST)]
        turned = lax.dot_general(
            jnp.concatenate(tiles, axis=0), inverse, ABT, precision=lax.Precision.HIGHEST, preferred_element_type=f32
        )
        for e in range(n):
            tile = turned[e * patch : (e + 1) * patch]
            panel_ref[row, e] = tile
            if row == 0 and 0 < e < n - 1:
                pay_ref[(e - 1) * half : e * half, :] = packed(tile).astype(bf16)
    tail = (n - 2) * half
    put_tail(pay_ref, tail, stat_ref[0, :patch], root)


def put_tail(pay_ref, tail, table, root):
    half = table.shape[0] // 2
    high, low = pair_of(jnp.where(iota(table.shape, 1) < 32, table, 0.0))
    both = high.astype(f32) + pltpu.roll(low.astype(f32), 32, 1)
    pay_ref[tail : tail + half, :] = (both[:half] + pltpu.roll(both[half:], 64, 1)).astype(bf16)
    pay_ref[tail + half :, :] = basis_rows(root)


def got_tail(got_ref, tail, patch):
    half = patch // 2
    both = got_ref[tail : tail + half, :].astype(f32)
    upper = both + pltpu.roll(both, 96, 1)
    lower = pltpu.roll(both, 64, 1) + pltpu.roll(both, 32, 1)
    return jnp.concatenate([upper, lower], axis=0), basis_of(got_ref[tail + half :, :])


def start_panel(factor, parts, stat, xl, own_panel, xr):
    rows, cols, patch, _ = own_panel.shape
    n = cols + 2 * GHOST
    return kernel_call(
        functools.partial(start_kernel, factor, len(parts)),
        (
            sds((rows, n, patch, RANK), f32),
            sds((payload_rows(n - 2, patch), 2 * RANK), bf16),
            sds((2, RANK, RANK), f32),
        ),
    )(*parts, stat, xl, own_panel, xr)


def cut_kernel(be_ref, after_ref, left_ref, right_ref):
    left_ref[...] = be_ref[:GHOST]
    right_ref[...] = be_ref[be_ref.shape[0] - GHOST :]


def cut(be, after):
    vmem = pl.BlockSpec(memory_space=pltpu.VMEM)
    side = sds((GHOST,) + be.shape[1:], be.dtype)
    return pl.pallas_call(
        cut_kernel,
        in_specs=[vmem, pl.BlockSpec(memory_space=pl.ANY)],
        out_specs=[vmem] * 2,
        out_shape=(side, side),
        compiler_params=pltpu.CompilerParams(vmem_limit_bytes=VMEM_BYTES),
    )(be, after)


def stages(n):
    middle = list(range(GHOST + EDGE, n - GHOST - EDGE))
    ends = [c for c in range(n) if c not in middle]
    arrived, seen, steps = set(), set(), []
    for tiles in (ends, middle):
        arrived |= set(tiles)
        columns = [e for e in range(1, n - 1) if {e - 1, e, e + 1} <= arrived and e not in seen]
        seen |= set(columns)
        steps.append((tiles, columns))
    return steps


def scale_of(stat_ref, sums):
    down_sum, _, mask = sums
    patch = mask.shape[0]
    degree = 1.0 + stat_ref[0, patch:] + down_sum - FLOOR * absent_near(mask, 3 * patch)
    return stat_ref[2, patch:] * lax.rsqrt(degree)


def pair_source(e, tiles):
    some = next(iter(tiles.values()))
    near = [tiles.get(c, jnp.zeros_like(some)) for c in range(e - 1, e + 3)]
    return jnp.concatenate(near, axis=0)


def pairs_of(columns):
    return sorted({e - (e + 1) % 2 for e in columns})


def pair_products(columns, block_ref, tiles):
    results = {}
    for e in pairs_of(columns):
        product = jnp.dot(block_ref[e // 2], pair_source(e, tiles), preferred_element_type=f32)
        patch = product.shape[0] // 2
        results[e], results[e + 1] = product[:patch], product[patch:]
    return results


def products(columns, up_ref, tiles, pay_ref, first):
    half = up_ref.shape[1] // 4
    results = pair_products(columns, up_ref, tiles)
    for e in columns:
        pay_ref[(e - first) * half : (e - first + 1) * half, :] = packed(results[e]).astype(bf16)


def cross_kernel(n, stage, *refs):
    steps = stages(n)
    tiles, columns = steps[stage]
    count = 3 if stage == 0 else 1
    pieces, (own_ref, stat_ref, p_ref, base_ref) = refs[:count], refs[count : count + 4]
    refs = refs[count + 4 :]
    patch = pieces[0].shape[1]
    lane = iota((patch, 128), 1)
    if stage == 0:
        v_ref, w_ref, sum_ref, u0_ref, pay_ref, unit_ref = refs
        empty = jnp.zeros((patch, 128), f32)
        down_sum, up_sum, mask = empty, empty, empty
    else:
        before, (v_ref, w_ref, sum_ref, u0_ref, pay_ref, unit_ref) = refs[:6], refs[6:12]
        down_sum, up_sum, mask = (before[2][i] for i in range(3))
        earlier = {e for _, reached in steps[:stage] for e in reached}
        for e in pairs_of(earlier):
            v_ref[e // 2] = before[0][e // 2]
            w_ref[e // 2] = before[1][e // 2]
        for e in sorted(earlier):
            u0_ref[e] = before[3][e]
        for e in sorted(e for e in earlier if e - 1 in earlier and e + 1 in earlier):
            span = slice((e - 2) * patch // 2, (e - 1) * patch // 2)
            pay_ref[span, :] = before[4][span, :]
        for c in sorted({c for e in columns for c in (e - 1, e, e + 1)} - set(tiles)):
            span = slice(c * patch, (c + 1) * patch)
            unit_ref[span, :] = before[5][span, :]
    sources = [(ref, i) for ref in pieces for i in range(ref.shape[0])]
    for c, (ref, i) in zip(tiles, sources):
        unit, column = unit_and_mask(ref[i])
        unit_ref[c * patch : (c + 1) * patch, :] = unit
        mask = at_lane(lane, c, column, mask)
    shape = (2 * patch, 4 * patch)
    apart = iota(shape, 1) // patch - iota(shape, 0) // patch
    beside = (apart >= 0) & (apart <= 2)
    for e in pairs_of(columns):
        around = slice((e - 1) * patch, (e + 3) * patch)
        here = slice(e * patch, (e + 2) * patch)
        down = jnp.where(beside, affinity_of(own_ref[here, :], unit_ref[around, :]), 0.0)
        up = jnp.where(beside, affinity_of(unit_ref[here, :], own_ref[around, :]), 0.0)
        v_ref[e // 2] = down.astype(bf16)
        w_ref[e // 2] = up.astype(bf16)
        down = jnp.sum(down, axis=1, keepdims=True)
        up = jnp.sum(up, axis=1, keepdims=True)
        for i in range(2):
            span = slice(i * patch, (i + 1) * patch)
            down_sum = at_lane(lane, e + i, down[span], down_sum)
            up_sum = at_lane(lane, e + i, up[span], up_sum)
    sums = (down_sum, up_sum, mask)
    scale = scale_of(stat_ref, sums)
    for e in columns:
        u0_ref[e] = (scale[:, e : e + 1] * p_ref[1, e]).astype(bf16)
    inner, known = [], []
    for last in (stage - 1, stage):
        known = [e for _, reached in steps[: last + 1] for e in reached]
        inner.append({e for e in range(2, n - 2) if {e - 1, e, e + 1} <= set(known)})
    fresh = sorted(inner[1] - inner[0])
    near = {c for e in fresh for c in (e - 1, e, e + 1)}
    products(fresh, w_ref, {e: u0_ref[e] for e in near}, pay_ref, 2)
    if stage < len(steps) - 1:
        for i in range(3):
            sum_ref[i] = sums[i]
        return
    shared = up_sum - FLOOR * absent_near(stat_ref[2, patch:], 3 * patch)
    sum_ref[0], sum_ref[1], sum_ref[2] = shared, mask, scale
    tail = (n - 4) * patch // 2
    put_tail(pay_ref, tail, shared, base_ref[1])


def cross_affinity(stage, pieces, u1, stat, panel, base, before=()):
    patch, width = pieces[0].shape[1:]
    n = u1.shape[0] // patch
    given = len(pieces) + 4
    return pl.pallas_call(
        functools.partial(cross_kernel, n, stage),
        out_shape=(
            sds((n // 2 - 1, 2 * patch, 4 * patch), bf16),
            sds((n // 2 - 1, 2 * patch, 4 * patch), bf16),
            sds((3, patch, 128), f32),
            sds((n, patch, RANK), bf16),
            sds((payload_rows(n - 4, patch), 2 * RANK), bf16),
            sds((n * patch, width), bf16),
        ),
        input_output_aliases={given + i: i for i in range(len(before))},
        compiler_params=pltpu.CompilerParams(vmem_limit_bytes=VMEM_BYTES),
    )(*pieces, u1, stat, panel, base, *before)


def before_first_kernel(
    n,
    got_ref, sum_ref, stat_ref, u0_ref, m_ref, v_ref, base_ref,
    z_ref, t_ref, gain_ref, own_ref, turn_ref,
):
    patch = u0_ref.shape[1]
    half = patch // 2
    tail = (n - 2) * half
    partial, theirs = got_tail(got_ref, tail, patch)
    below_scale = sum_ref[1] * lax.rsqrt(1.0 + partial + sum_ref[0])
    scale = sum_ref[2]
    gain = 1.0 + scale * scale * stat_ref[1, patch:]
    upper = stat_ref[1, :patch]
    turn = pair_of(turn_of(theirs, base_ref[0]))
    turn_ref[0], turn_ref[1] = turn
    tiles = [unpacked(got_ref[(e - 1) * half : e * half, :].astype(f32)) for e in range(1, n - 1)]
    tiles = turned([below_scale[:, e : e + 1] * tile for e, tile in zip(range(1, n - 1), tiles)], turn)
    lower = pair_products(range(2, n - 2), v_ref, {e: tile.astype(bf16) for e, tile in zip(range(1, n - 1), tiles)})
    for e in range(2, n - 2):
        own = u0_ref[e - 1 : e + 2].reshape(3 * patch, RANK)
        total = jnp.dot(m_ref[e, :, 3 * patch :], own, preferred_element_type=f32)
        z_ref[e, :patch] = total[:patch]
        z_ref[e, patch:] = total[patch:] + lower[e]
        for ref, table in ((t_ref, scale), (gain_ref, gain), (own_ref, upper)):
            ref[e] = jnp.broadcast_to(table[:, e : e + 1], (patch, RANK))


def before_first(got, sums, stat, u0, m, v, base):
    n, patch, _ = u0.shape
    spread = sds((n, patch, RANK), f32)
    return kernel_call(
        functools.partial(before_first_kernel, n),
        (sds((n, 2 * patch, RANK), f32), spread, spread, spread, sds((2, RANK, RANK), bf16)),
    )(got, sums, stat, u0, m, v, base)


def first_kernel(
    n,
    got_ref, stat_ref, t1_ref, gain1_ref, own_ref, z_ref, p_ref, m_ref, w_ref, base_ref,
    y_ref, u_ref, t0_ref, gain0_ref, up_ref, down_ref, turn_ref,
    start_ref,
):
    patch = t1_ref.shape[1]
    half = patch // 2
    tail = (n - 4) * half
    partial, theirs = got_tail(got_ref, tail, patch)
    turn = pair_of(turn_of(theirs, base_ref[0]))
    turn_ref[0], turn_ref[1] = turn
    above = turned([unpacked(got_ref[(e - 2) * half : (e - 1) * half, :]) for e in range(2, n - 2)], turn)
    scale = stat_ref[2, :patch] * lax.rsqrt(1.0 + stat_ref[0, :patch] + partial)
    for e in range(1, n - 1):
        t = jnp.broadcast_to(scale[:, e : e + 1], (patch, RANK))
        t0_ref[e] = t
        start_ref[e] = (t * p_ref[0, e]).astype(bf16)
    for e in range(2, n - 2):
        own = start_ref[e - 1 : e + 2].reshape(3 * patch, RANK)
        total = z_ref[e] + jnp.dot(m_ref[e, :, : 3 * patch], own, preferred_element_type=f32)
        upper = total[:patch] + above[e - 2]
        gain = 1.0 + t0_ref[e] * t0_ref[e] * own_ref[e]
        gain0_ref[e] = gain
        for row, piece, t, g in ((0, upper, t0_ref[e], gain), (1, total[patch:], t1_ref[e], gain1_ref[e])):
            image = p_ref[row, e] * g + t * piece
            y_ref[row, e] = image
            scaled = t * image
            u_ref[row, e] = scaled.astype(bf16)
            if row == 0:
                up_ref[(e - 2) * half : (e - 1) * half, :] = packed(scaled).astype(bf16)
    products(range(3, n - 3), w_ref, {e: u_ref[1, e] for e in range(2, n - 2)}, down_ref, 3)


def first_iteration(got, stat, t1, gain1, own, z, panel, m, w, base):
    n, both, _ = z.shape
    patch = both // 2
    half = patch // 2
    spread = sds((n, patch, RANK), f32)
    return kernel_call(
        functools.partial(first_kernel, n),
        (
            sds((2, n, patch, RANK), f32),
            sds((2, n, patch, RANK), bf16),
            spread,
            spread,
            sds(((n - 4) * half, 2 * RANK), bf16),
            sds(((n - 6) * half, 2 * RANK), bf16),
            sds((2, RANK, RANK), bf16),
        ),
        [pltpu.VMEM((n, patch, RANK), bf16)],
    )(got, stat, t1, gain1, own, z, panel, m, w, base)


def local_kernel(low, high, m_ref, u_ref, z_ref):
    patch = u_ref.shape[2]
    for e in range(low, high):
        upper = u_ref[0, e - 1 : e + 2].reshape(3 * patch, RANK)
        lower = u_ref[1, e - 1 : e + 2].reshape(3 * patch, RANK)
        z_ref[e] = jnp.dot(m_ref[e], jnp.concatenate([upper, lower], axis=0), preferred_element_type=f32)


def local_products(low, high, m, u):
    n, both, _ = m.shape
    return kernel_call(
        functools.partial(local_kernel, low, high),
        sds((n, both, RANK), f32),
    )(m, u)


def images_of(n, low, below_ref, above_ref, z_ref, y_ref, scales, gains, turns, v_ref):
    patch = y_ref.shape[2]
    half = patch // 2
    count = n - 2 * low
    down, up = ((ref[0], ref[1]) for ref in turns)
    near = turned([unpacked(below_ref[i * half : (i + 1) * half, :]) for i in range(count + 2)], down)
    near = {low - 1 + i: tile.astype(bf16) for i, tile in enumerate(near)}
    lower = pair_products(range(low, n - low), v_ref, near)
    upper = turned([unpacked(above_ref[i * half : (i + 1) * half, :]) for i in range(count)], up)
    for e in range(low, n - low):
        pieces = (z_ref[e, :patch] + upper[e - low], z_ref[e, patch:] + lower[e])
        yield e, [y_ref[row, e] * gains[row][e] + scales[row][e] * pieces[row] for row in range(2)]


def middle_step_kernel(
    n, low,
    below_ref, above_ref, z_ref, y_ref, t0_ref, t1_ref, gain0_ref, gain1_ref, turn0_ref, turn1_ref, v_ref, w_ref,
    new_ref, u_ref, up_ref, down_ref,
):
    patch = y_ref.shape[2]
    half = patch // 2
    scales, gains = (t0_ref, t1_ref), (gain0_ref, gain1_ref)
    turns = (turn0_ref, turn1_ref)
    for e, images in images_of(n, low, below_ref, above_ref, z_ref, y_ref, scales, gains, turns, v_ref):
        for row in range(2):
            new_ref[row, e] = images[row]
            scaled = scales[row][e] * images[row]
            u_ref[row, e] = scaled.astype(bf16)
            if row == 0:
                up_ref[(e - low) * half : (e - low + 1) * half, :] = packed(scaled).astype(bf16)
    products(
        range(low + 1, n - low - 1), w_ref, {e: u_ref[1, e] for e in range(low, n - low)}, down_ref, low + 1
    )


def middle_step(low, below, above, z, y, spread, v, w):
    _, n, patch, _ = y.shape
    half = patch // 2
    return kernel_call(
        functools.partial(middle_step_kernel, n, low),
        (
            sds((2, n, patch, RANK), f32),
            sds((2, n, patch, RANK), bf16),
            sds(((n - 2 * low) * half, 2 * RANK), bf16),
            sds(((n - 2 * low - 2) * half, 2 * RANK), bf16),
        ),
    )(below, above, z, y, *spread, v, w)


def last_step_kernel(
    n, low,
    below_ref, above_ref, z_ref, y_ref, t0_ref, t1_ref, gain0_ref, gain1_ref, turn0_ref, turn1_ref, v_ref,
    new_ref, gram_ref, side_ref,
):
    patch = y_ref.shape[2]
    scales, gains = (t0_ref, t1_ref), (gain0_ref, gain1_ref)
    wide = 2 * RANK
    turns = (turn0_ref, turn1_ref)
    for e, images in images_of(n, low, below_ref, above_ref, z_ref, y_ref, scales, gains, turns, v_ref):
        for row in range(2):
            new_ref[row, e - low] = images[row]
        span = slice((e - low) * patch, (e - low + 1) * patch)
        side_ref[span, :wide], side_ref[span, wide:] = pair_of(jnp.concatenate(images, axis=1))
    gram_ref[...] = folded_gram(side_ref[...])


def last_step(low, below, above, z, y, spread, v):
    _, n, patch, _ = y.shape
    cols = n - 2 * low
    return kernel_call(
        functools.partial(last_step_kernel, n, low),
        (sds((2, cols, patch, RANK), f32), sds((RANK // 2, 2 * RANK), f32)),
        [pltpu.VMEM((cols * patch, 4 * RANK), bf16)],
    )(below, above, z, y, *spread, v)


def inverse_factor(gram, bounded=False):
    size = gram.shape[0]
    least = 0.0
    if bounded:
        least = 1e-6 * jnp.sum(jnp.where(identity(size), gram, 0.0), axis=1, keepdims=True) + 1e-16
    step = 8
    row = iota((size, 2 * size), 0)
    lane = iota((size, 2 * size), 1)
    table = jnp.concatenate([gram, identity(size).astype(f32)], axis=1)
    for k in range(0, size, step):
        cols = [jnp.broadcast_to(table[:, k + i : k + i + 1], table.shape) for i in range(step)]
        lines = [table[k + i : k + i + 1, :] for i in range(step)]
        for i in range(step):
            pivot = cols[i][k + i : k + i + 1, :]
            inverse = 1.0 / (jnp.maximum(pivot, least[k + i : k + i + 1, :]) if bounded else pivot)
            for j in range(i + 1, step):
                lines[j] = lines[j] - lines[i] * (cols[i][k + j : k + j + 1, :] * inverse)
                cols[j] = cols[j] - cols[i] * (cols[j][k + i : k + i + 1, :] * inverse)
            table = table - jnp.where(row > k + i, cols[i], 0.0) * (lines[i] * inverse)
    pivots = jnp.sum(jnp.where(row == lane, table, 0.0), axis=1, keepdims=True)
    if not bounded:
        return table[:, size:] * lax.rsqrt(pivots)
    pivots = jnp.maximum(pivots, least)
    row, lane = row[:, :size], lane[:, :size]
    upper = jnp.where(lane > row, table[:, :size], jnp.where(lane == row, pivots, 0.0))
    return table[:, size:] * lax.rsqrt(pivots), upper * lax.rsqrt(pivots)


def balanced(parts):
    while len(parts) > 1:
        parts = [a + b for a, b in zip(parts[::2], parts[1::2])]
    return parts[0]


def joint_gram(parts, base_ref):
    size = RANK // 2
    turns = turn_of(jnp.concatenate([unpacked(part[size:, :]) for part in parts[1:]], axis=0), base_ref[0])
    first = []
    for i, part in enumerate(parts[1:]):
        turn = turns[i * RANK : (i + 1) * RANK]
        first.append(
            jnp.dot(
                unpacked(part[:size, :]), turn, precision=lax.Precision.HIGHEST, preferred_element_type=f32
            )
        )
    others = lax.dot_general(
        turns, jnp.concatenate(first, axis=0), ATB, precision=lax.Precision.HIGHEST, preferred_element_type=f32
    )
    return unpacked(parts[0][:size, :]) + others


def joint_kernel(count, *refs):
    refs[-1][: RANK // 2, :] = packed(joint_gram(refs[:count], refs[count]))
    refs[-1][RANK // 2 :, :] = packed(refs[count][1])


def joint(parts, base):
    return kernel_call(functools.partial(joint_kernel, len(parts)), sds(parts[0].shape, f32))(*parts, base)


def finish_kernel(factor, count, *refs):
    parts, (base_ref, y_ref, out_ref) = refs[:count], refs[count:]
    inverse = factor * inverse_factor(joint_gram(parts, base_ref))
    zero = jnp.zeros_like(inverse)
    both = jnp.concatenate(
        [jnp.concatenate([inverse, zero], axis=1), jnp.concatenate([zero, inverse], axis=1)], axis=0
    )
    wide = 2 * RANK
    tiles, width = y_ref.shape
    pieces = [y_ref[:, q * wide : (q + 1) * wide] for q in range(width // wide)]
    y_high, y_low = pair_of(jnp.concatenate(pieces, axis=0))
    t_high, t_low = pair_of(both)

    def times(a, b):
        return lax.dot_general(a, b, ABT, preferred_element_type=f32)

    out = times(y_high, t_high) + (times(y_low, t_high) + times(y_high, t_low))
    for q in range(width // wide):
        out_ref[:, q * wide : (q + 1) * wide] = out[q * tiles : (q + 1) * tiles]


def finish(factor, parts, base, y):
    return kernel_call(
        functools.partial(finish_kernel, factor, len(parts)),
        sds(y.shape, f32),
    )(*parts, base, y)


def exchange_stages(axis):
    size = lax.axis_size(axis)
    stages, bit = [], 1
    if axis == "col":
        stages.append([1])
        bit = 2
    while bit < size:
        if 2 * bit < size:
            stages.append([bit, 2 * bit, 3 * bit])
            bit *= 4
        else:
            stages.append([bit])
            bit *= 2
    return stages


def summed_parts(gram, axis, combine):
    size = lax.axis_size(axis)
    parts = [gram]
    for partners in exchange_stages(axis):
        gram = combine(parts) if len(parts) > 1 else gram
        parts = [gram] + [lax.ppermute(gram, axis, [(i, i ^ p) for i in range(size)]) for p in partners]
    return parts


def passed_along(shard, axis, by):
    count = lax.axis_size(axis)
    pairs = [(i, i + by) for i in range(count) if 0 <= i + by < count]
    return lax.ppermute(shard, axis, pairs)


def local(features, tissue, probe):
    tile_rows, tile_cols, patches, width = features.shape
    total = tile_rows * lax.axis_size("row") * tile_cols * lax.axis_size("col") * patches
    factor = math.sqrt(float(total))
    edges = mark_edges(features, tissue)
    below_edges = passed_along(edges, "row", -1)
    parts = summed_parts(start_gram(probe), "col", balanced)
    own_panel = probe.reshape(tile_rows, tile_cols, patches, RANK)
    left_end, right_end = gate(mark_ends(features, tissue, own_panel), parts)
    middle, unit0, unit1 = own_units(features, tissue, left_end)
    from_left = passed_along(right_end, "col", 1)
    from_right = passed_along(left_end, "col", -1)
    below_middle = passed_along(middle, "row", -1)
    m, sums = inside_affinity(unit0, unit1, patches)
    below_left, below_right = cut(below_edges, sums)
    _, u1, m, stat = outside_affinity(unit0, unit1, m, tissue, sums, from_left, from_right, below_left)
    panel, payload, base = start_panel(factor, parts, stat, from_left, own_panel, from_right)
    below_left, below_right = passed_along(below_right, "col", 1), passed_along(below_left, "col", -1)
    got_below = passed_along(payload, "row", -1)
    n = tile_cols + 2 * GHOST
    cross = cross_affinity(0, (below_left, below_edges, below_right), u1, stat, panel, base)
    v, w, sums, u0, payload, _ = cross_affinity(1, (below_middle,), u1, stat, panel, base, cross)
    got_above = passed_along(payload, "row", 1)
    z, t1, gain1, own, turn0 = before_first(got_below, sums, stat, u0, m, v, base)
    y, u, t0, gain0, up, down, turn1 = first_iteration(got_above, stat, t1, gain1, own, z, panel, m, w, base)
    spread = (t0, t1, gain0, gain1, turn0, turn1)
    below, above = passed_along(up, "row", -1), passed_along(down, "row", 1)
    z = local_products(3, n - 3, m, u)
    y, u, up, down = middle_step(3, below, above, z, y, spread, v, w)
    below, above = passed_along(up, "row", -1), passed_along(down, "row", 1)
    z = local_products(4, n - 4, m, u)
    y, gram = last_step(4, below, above, z, y, spread, v)

    gram = balanced(summed_parts(gram, "col", balanced))
    root = jnp.concatenate([base[1, : RANK // 2], base[1, RANK // 2 :]], axis=1)
    parts = summed_parts(jnp.concatenate([gram, root], axis=0), "row", lambda parts: joint(parts, base))
    flat = y.reshape(tile_rows * tile_cols, patches * RANK)
    out = finish(factor, parts, base, flat)
    return out.reshape(tile_rows, tile_cols, patches * RANK)


def solution(mesh):
    placed = (P("row", "col", None, None), P("row", "col", None), P("row", "col", None))
    return jax.shard_map(
        local, mesh=mesh, in_specs=placed, out_specs=P("row", "col", None), check_vma=False
    )
```

```python
import functools
import math

import jax
import jax.numpy as jnp
from jax import lax
from jax.experimental import pallas as pl
from jax.experimental.pallas import tpu as pltpu
from jax.sharding import PartitionSpec as P

RANK = 64
ITERS = 3
AFFINITY_TEMP = 4.0

GHOST = ITERS + 1
EDGE = 4
TINY = 1e-30
VMEM_BYTES = 16 * 1024 * 1024
FLOOR = math.exp(-AFFINITY_TEMP)
ABT = (((1,), (1,)), ((), ()))
ATB = (((0,), (0,)), ((), ()))

f32 = jnp.float32
bf16 = jnp.bfloat16


def kernel_call(body, out_shape, scratch=()):
    return pl.pallas_call(
        body,
        out_shape=out_shape,
        scratch_shapes=list(scratch),
        compiler_params=pltpu.CompilerParams(vmem_limit_bytes=VMEM_BYTES),
    )


def sds(shape, dtype):
    return jax.ShapeDtypeStruct(shape, dtype)


def iota(shape, dim):
    return lax.broadcasted_iota(jnp.int32, shape, dim)


def identity(n):
    return iota((n, n), 0) == iota((n, n), 1)


def unit_and_mask(block):
    values = block.astype(f32)
    scaled = values * lax.rsqrt(jnp.sum(values * values, axis=-1, keepdims=True) + 1e-06)
    return scaled.astype(bf16), (values[:, :1] != 0.0).astype(f32)


def affinity_of(left, right):
    scores = lax.dot_general(left, right, ABT, preferred_element_type=f32)
    return jnp.exp(AFFINITY_TEMP * scores - AFFINITY_TEMP)


def at_lane(lane, e, column, table):
    return jnp.where(lane == e, column, table)


def absent_near(mask, width):
    count = jnp.sum(mask, axis=0, keepdims=True)
    return width - (pltpu.roll(count, 1, 1) + count + pltpu.roll(count, 127, 1))


def packed(block):
    half = block.shape[0] // 2
    return jnp.concatenate([block[:half], block[half:]], axis=1)


def unpacked(block):
    return jnp.concatenate([block[:, :RANK], block[:, RANK:]], axis=0)


def pair_of(values):
    high = values.astype(bf16)
    return high, (values - high.astype(f32)).astype(bf16)


def four_of(values):
    high, middle = pair_of(values)
    low = (values - high.astype(f32) - middle.astype(f32)).astype(bf16)
    return jnp.concatenate([high, middle, low, jnp.zeros_like(low)], axis=1)


def basis_rows(table):
    parts = four_of(table)
    return jnp.concatenate([parts[:, : 2 * RANK], packed(parts[:, 2 * RANK : 3 * RANK])], axis=0)


def basis_of(rows):
    rows = rows.astype(f32)
    return rows[:RANK, :RANK] + rows[:RANK, RANK:] + unpacked(rows[RANK:])


def turn_of(theirs, inverse):
    return lax.dot_general(
        theirs, inverse, ABT, precision=lax.Precision.HIGHEST, preferred_element_type=f32
    )


def turned(tiles, turn):
    patch = tiles[0].shape[0]
    stack = jnp.concatenate(tiles, axis=0).astype(bf16)
    high, low = turn
    result = jnp.dot(stack, high, preferred_element_type=f32) + jnp.dot(stack, low, preferred_element_type=f32)
    return [result[i * patch : (i + 1) * patch] for i in range(len(tiles))]


def whole_of(parts):
    parts = parts.astype(f32)
    return parts[:, :RANK] + parts[:, RANK : 2 * RANK] + parts[:, 2 * RANK : 3 * RANK]


def by_sublane(tissue):
    mask = (tissue != 0).astype(bf16)
    return lax.dot_general(mask, identity(mask.shape[0]).astype(bf16), ATB, preferred_element_type=f32)


def marked(tile, column):
    zero = (iota(tile.shape, 1) == 0) & (tile == 0)
    return jnp.where(zero, jnp.asarray(TINY, bf16), tile) * column.astype(bf16)


def fetched(sources, slots, sems):
    copies = [pltpu.make_async_copy(source, slot, sems.at[i]) for i, (source, slot) in enumerate(zip(sources, slots))]
    for copy in copies:
        copy.start()
    return copies


def in_hbm(*arrays):
    return tuple(pltpu.with_memory_space_constraint(array, pltpu.HBM) for array in arrays)


VMEM_SPEC = pl.BlockSpec(memory_space=pltpu.VMEM)
HBM_SPEC = pl.BlockSpec(memory_space=pltpu.HBM)
ANY_SPEC = pl.BlockSpec(memory_space=pl.ANY)


def folded_gram(side):
    wide = 2 * RANK
    gram = lax.dot_general(side, side, ATB, preferred_element_type=f32)
    gram = gram[:wide] + gram[wide:]
    gram = gram[:, :wide] + gram[:, wide:]
    return packed(gram[:RANK, :RANK] + gram[RANK:, RANK:])


def start_gram_kernel(probe_ref, gram_ref, flat_ref, sems):
    rows, cols, width = probe_ref.shape
    (copy,) = fetched([probe_ref], [flat_ref], sems)
    copy.wait()
    wide = 2 * RANK
    spans = [slice(q * wide, (q + 1) * wide) for q in range(width // wide)]
    side = jnp.concatenate([flat_ref[row, :, span] for row in range(rows) for span in spans], axis=0)
    gram_ref[...] = folded_gram(jnp.concatenate(pair_of(side), axis=1))


def start_gram(probe):
    return pl.pallas_call(
        start_gram_kernel,
        in_specs=[HBM_SPEC],
        out_specs=VMEM_SPEC,
        out_shape=sds((RANK // 2, 2 * RANK), f32),
        scratch_shapes=[pltpu.VMEM(probe.shape, f32), pltpu.SemaphoreType.DMA((1,))],
        compiler_params=pltpu.CompilerParams(vmem_limit_bytes=VMEM_BYTES),
    )(*in_hbm(probe))


def mark_edges_kernel(x_ref, tissue_ref, edge_ref, tile_ref, mask_ref, sems):
    cols = x_ref.shape[1]
    sources = [tissue_ref.at[0], x_ref.at[0, :EDGE], x_ref.at[0, cols - EDGE :]]
    copies = fetched(sources, [mask_ref, tile_ref.at[:EDGE], tile_ref.at[EDGE:]], sems)
    copies[0].wait()
    mask = by_sublane(mask_ref[...])
    for side, first in ((0, 0), (1, cols - EDGE)):
        copies[1 + side].wait()
        for i in range(EDGE):
            at = side * EDGE + i
            edge_ref[at] = marked(tile_ref[at], mask[:, first + i : first + i + 1])


def mark_edges(x, tissue):
    rows, cols, patch, width = x.shape
    shape = (2 * EDGE, patch, width)
    return pl.pallas_call(
        mark_edges_kernel,
        in_specs=[HBM_SPEC, HBM_SPEC],
        out_specs=VMEM_SPEC,
        out_shape=sds(shape, bf16),
        scratch_shapes=[
            pltpu.VMEM(shape, bf16),
            pltpu.VMEM((cols, patch), jnp.int32),
            pltpu.SemaphoreType.DMA((3,)),
        ],
        compiler_params=pltpu.CompilerParams(vmem_limit_bytes=VMEM_BYTES),
    )(*in_hbm(x, tissue))


def gate_kernel(count, *refs):
    for x_ref, out_ref in zip(refs[:count], refs[len(refs) - count :]):
        out_ref[...] = x_ref[...]


def gate(arrays, after):
    count = len(arrays)
    return pl.pallas_call(
        functools.partial(gate_kernel, count),
        in_specs=[VMEM_SPEC] * count + [ANY_SPEC] * len(after),
        out_specs=[VMEM_SPEC] * count,
        out_shape=tuple(sds(x.shape, x.dtype) for x in arrays),
        input_output_aliases={i: i for i in range(count)},
        compiler_params=pltpu.CompilerParams(vmem_limit_bytes=VMEM_BYTES),
    )(*arrays, *after)


def ends_kernel(x_ref, tissue_ref, probe_ref, left_ref, right_ref, tile_ref, sems):
    rows, cols, patch, width = x_ref.shape
    order = [(row, c) for row in range(rows) for c in (0, cols - GHOST)]
    sources = [x_ref.at[row, c : c + GHOST] for row, c in order]
    copies = fetched(sources, [tile_ref.at[i] for i in range(len(order))], sems)
    masks = [by_sublane(tissue_ref[row]) for row in range(rows)]
    for i, (row, first) in enumerate(order):
        copies[i].wait()
        side_ref = right_ref if first else left_ref
        for k in range(GHOST):
            c = first + k
            side_ref[row, k, :, :width] = marked(tile_ref[i, k], masks[row][:, c : c + 1])
            side_ref[row, k, :, width:] = four_of(probe_ref[row, c])


def mark_ends(x, tissue, probe):
    rows, cols, patch, width = x.shape
    side = sds((rows, GHOST, patch, width + 4 * RANK), bf16)
    return pl.pallas_call(
        ends_kernel,
        in_specs=[HBM_SPEC, VMEM_SPEC, VMEM_SPEC],
        out_specs=[VMEM_SPEC] * 2,
        out_shape=(side, side),
        scratch_shapes=[
            pltpu.VMEM((2 * rows, GHOST, patch, width), bf16),
            pltpu.SemaphoreType.DMA((2 * rows,)),
        ],
        compiler_params=pltpu.CompilerParams(vmem_limit_bytes=VMEM_BYTES),
    )(*in_hbm(x), tissue, probe)


def units_kernel(x_ref, tissue_ref, after_ref, middle_ref, unit0_ref, unit1_ref, tile_ref, sems):
    rows, cols, patch, width = x_ref.shape
    run = GHOST
    order = [(row, c) for row in range(rows) for c in range(0, cols, run)]
    copies = fetched([x_ref.at[row, c : c + run] for row, c in order], [tile_ref.at[i] for i in range(len(order))], sems)
    masks = [by_sublane(tissue_ref[row]) for row in range(rows)]
    for i, (row, first) in enumerate(order):
        copies[i].wait()
        for k in range(run):
            c = first + k
            tile, column = tile_ref[i, k], masks[row][:, c : c + 1]
            unit, _ = unit_and_mask(tile)
            at = (GHOST + c) * patch
            (unit0_ref, unit1_ref)[row][at : at + patch, :] = unit * column.astype(bf16)
            if row == 0 and EDGE <= c < cols - EDGE:
                middle_ref[c - EDGE] = marked(tile, column)


def own_units(x, tissue, after):
    rows, cols, patch, width = x.shape
    n = cols + 2 * GHOST
    unit = sds((n * patch, width), bf16)
    return pl.pallas_call(
        units_kernel,
        in_specs=[HBM_SPEC, VMEM_SPEC, ANY_SPEC],
        out_specs=[VMEM_SPEC] * 3,
        out_shape=(sds((cols - 2 * EDGE, patch, width), bf16), unit, unit),
        scratch_shapes=[
            pltpu.VMEM((rows * cols // GHOST, GHOST, patch, width), bf16),
            pltpu.SemaphoreType.DMA((rows * cols // GHOST,)),
        ],
        compiler_params=pltpu.CompilerParams(vmem_limit_bytes=VMEM_BYTES),
    )(*in_hbm(x), tissue, after)


def bands(ranges, patch, unit0_ref, unit1_ref, m_ref, degree, diagonal):
    both = 2 * patch
    shape = (both, 3 * both)
    patch_of = iota(shape, 0)
    own = iota(shape, 1) == jnp.where(patch_of < patch, patch_of + patch, patch_of + 3 * patch)
    lane = iota((both, 128), 1)

    def band(e, carry):
        degree, diagonal = carry
        around = slice((e - 1) * patch, (e + 2) * patch)
        here = slice(e * patch, (e + 1) * patch)
        left = jnp.concatenate([unit0_ref[here, :], unit1_ref[here, :]], axis=0)
        right = jnp.concatenate([unit0_ref[around, :], unit1_ref[around, :]], axis=0)
        weights = affinity_of(left, right)
        others = jnp.where(own, 0.0, weights)
        m_ref[e] = others.astype(bf16)
        itself = jnp.sum(weights - others, axis=1, keepdims=True)
        degree = at_lane(lane, e, jnp.sum(weights, axis=1, keepdims=True), degree)
        diagonal = at_lane(lane, e, itself, diagonal)
        return degree, diagonal

    carry = (degree, diagonal)
    for low, high in ranges:
        for e in range(low, high):
            carry = band(e, carry)
    return carry


def inside_kernel(n, unit0_ref, unit1_ref, m_ref, sum_ref):
    patch = m_ref.shape[1] // 2
    empty = jnp.zeros((2 * patch, 128), f32)
    sum_ref[0], sum_ref[1] = bands([(GHOST + 1, n - GHOST - 1)], patch, unit0_ref, unit1_ref, m_ref, empty, empty)


def inside_affinity(unit0, unit1, patch):
    n = unit0.shape[0] // patch
    both = 2 * patch
    return pl.pallas_call(
        functools.partial(inside_kernel, n),
        out_shape=(sds((n, both, 3 * both), bf16), sds((2, both, 128), f32)),
        compiler_params=pltpu.CompilerParams(vmem_limit_bytes=VMEM_BYTES),
    )(unit0, unit1)


def outside_kernel(
    n,
    start0_ref, start1_ref, some_ref, tissue_ref, sum_ref, xl_ref, xr_ref, after_ref,
    unit0_ref, unit1_ref, m_ref, stat_ref,
):
    rows, count, patch, _ = xl_ref.shape
    width = unit0_ref.shape[1]
    cols = n - 2 * count
    both = rows * patch
    lane = iota((patch, 128), 1)

    kept = slice(count * patch, (count + cols) * patch)
    unit0_ref[kept, :] = start0_ref[kept, :]
    unit1_ref[kept, :] = start1_ref[kept, :]
    for e in range(count + 1, n - count - 1):
        m_ref[e] = some_ref[e]
    masks = []
    for row, unit_ref in ((0, unit0_ref), (1, unit1_ref)):
        own_mask = by_sublane(tissue_ref[row])
        mask = jnp.zeros((patch, 128), f32)
        for e in range(n):
            if e < count:
                unit, column = unit_and_mask(xl_ref[row, e, :, :width])
            elif e < count + cols:
                unit, column = None, own_mask[:, e - count : e - count + 1]
            else:
                unit, column = unit_and_mask(xr_ref[row, e - count - cols, :, :width])
            mask = at_lane(lane, e, column, mask)
            if unit is not None:
                unit_ref[e * patch : (e + 1) * patch, :] = unit
        masks.append(mask)
    mask = jnp.concatenate(masks, axis=0)
    ranges = [(1, GHOST + 1), (n - GHOST - 1, n - 1)]
    degree, diagonal = bands(ranges, patch, unit0_ref, unit1_ref, m_ref, sum_ref[0], sum_ref[1])
    degree = degree - FLOOR * absent_near(mask, 3 * both)
    stat_ref[0] = degree
    stat_ref[1] = diagonal
    stat_ref[2] = mask

def payload_rows(columns, patch):
    return columns * patch // 2 + patch // 2 + RANK * 3 // 2


def outside_affinity(unit0, unit1, m, tissue, sums, xl, xr, after):
    n, both, _ = m.shape
    unit = sds(unit0.shape, bf16)
    return pl.pallas_call(
        functools.partial(outside_kernel, n),
        in_specs=[VMEM_SPEC] * 7 + [ANY_SPEC],
        out_specs=[VMEM_SPEC] * 4,
        out_shape=(unit, unit, sds(m.shape, bf16), sds((3, both, 128), f32)),
        input_output_aliases={0: 0, 1: 1, 2: 2},
        compiler_params=pltpu.CompilerParams(vmem_limit_bytes=VMEM_BYTES),
    )(unit0, unit1, m, tissue, sums, xl, xr, after)


def start_kernel(factor, count, *refs):
    parts, (stat_ref, xl_ref, p_ref, xr_ref, panel_ref, pay_ref, base_ref) = refs[:count], refs[count:]
    rows, cols, patch, _ = p_ref.shape
    n = cols + 2 * GHOST
    half = patch // 2
    width = xl_ref.shape[3] - 4 * RANK
    inverse, root = inverse_factor(unpacked(balanced([part[...] for part in parts])), True)
    inverse, root = factor * inverse, root / factor
    error = identity(RANK).astype(f32) - turn_of(root, inverse)
    root = root + jnp.dot(error, root, precision=lax.Precision.HIGHEST, preferred_element_type=f32)
    base_ref[0], base_ref[1] = inverse, root
    for row in range(rows):
        tiles = [whole_of(xl_ref[row, c, :, width:]) for c in range(GHOST)]
        tiles += [p_ref[row, c] for c in range(cols)]
        tiles += [whole_of(xr_ref[row, c, :, width:]) for c in range(GHOST)]
        turned = lax.dot_general(
            jnp.concatenate(tiles, axis=0), inverse, ABT, precision=lax.Precision.HIGHEST, preferred_element_type=f32
        )
        for e in range(n):
            tile = turned[e * patch : (e + 1) * patch]
            panel_ref[row, e] = tile
            if row == 0 and 0 < e < n - 1:
                pay_ref[(e - 1) * half : e * half, :] = packed(tile).astype(bf16)
    tail = (n - 2) * half
    put_tail(pay_ref, tail, stat_ref[0, :patch], root)


def put_tail(pay_ref, tail, table, root):
    half = table.shape[0] // 2
    high, low = pair_of(jnp.where(iota(table.shape, 1) < 32, table, 0.0))
    both = high.astype(f32) + pltpu.roll(low.astype(f32), 32, 1)
    pay_ref[tail : tail + half, :] = (both[:half] + pltpu.roll(both[half:], 64, 1)).astype(bf16)
    pay_ref[tail + half :, :] = basis_rows(root)


def got_tail(got_ref, tail, patch):
    half = patch // 2
    both = got_ref[tail : tail + half, :].astype(f32)
    upper = both + pltpu.roll(both, 96, 1)
    lower = pltpu.roll(both, 64, 1) + pltpu.roll(both, 32, 1)
    return jnp.concatenate([upper, lower], axis=0), basis_of(got_ref[tail + half :, :])


def start_panel(factor, parts, stat, xl, own_panel, xr):
    rows, cols, patch, _ = own_panel.shape
    n = cols + 2 * GHOST
    return kernel_call(
        functools.partial(start_kernel, factor, len(parts)),
        (
            sds((rows, n, patch, RANK), f32),
            sds((payload_rows(n - 2, patch), 2 * RANK), bf16),
            sds((2, RANK, RANK), f32),
        ),
    )(*parts, stat, xl, own_panel, xr)


def cut_kernel(be_ref, after_ref, left_ref, right_ref):
    left_ref[...] = be_ref[:GHOST]
    right_ref[...] = be_ref[be_ref.shape[0] - GHOST :]


def cut(be, after):
    vmem = pl.BlockSpec(memory_space=pltpu.VMEM)
    side = sds((GHOST,) + be.shape[1:], be.dtype)
    return pl.pallas_call(
        cut_kernel,
        in_specs=[vmem, pl.BlockSpec(memory_space=pl.ANY)],
        out_specs=[vmem] * 2,
        out_shape=(side, side),
        compiler_params=pltpu.CompilerParams(vmem_limit_bytes=VMEM_BYTES),
    )(be, after)


def stages(n):
    middle = list(range(GHOST + EDGE, n - GHOST - EDGE))
    ends = [c for c in range(n) if c not in middle]
    arrived, seen, steps = set(), set(), []
    for tiles in (ends, middle):
        arrived |= set(tiles)
        columns = [e for e in range(1, n - 1) if {e - 1, e, e + 1} <= arrived and e not in seen]
        seen |= set(columns)
        steps.append((tiles, columns))
    return steps


def scale_of(stat_ref, sums):
    down_sum, _, mask = sums
    patch = mask.shape[0]
    degree = 1.0 + stat_ref[0, patch:] + down_sum - FLOOR * absent_near(mask, 3 * patch)
    return stat_ref[2, patch:] * lax.rsqrt(degree)


def pair_source(e, tiles):
    some = next(iter(tiles.values()))
    near = [tiles.get(c, jnp.zeros_like(some)) for c in range(e - 1, e + 3)]
    return jnp.concatenate(near, axis=0)


def pairs_of(columns):
    return sorted({e - (e + 1) % 2 for e in columns})


def pair_products(columns, block_ref, tiles):
    results = {}
    for e in pairs_of(columns):
        product = jnp.dot(block_ref[e // 2], pair_source(e, tiles), preferred_element_type=f32)
        patch = product.shape[0] // 2
        results[e], results[e + 1] = product[:patch], product[patch:]
    return results


def products(columns, up_ref, tiles, pay_ref, first):
    half = up_ref.shape[1] // 4
    results = pair_products(columns, up_ref, tiles)
    for e in columns:
        pay_ref[(e - first) * half : (e - first + 1) * half, :] = packed(results[e]).astype(bf16)


def cross_kernel(n, stage, *refs):
    steps = stages(n)
    tiles, columns = steps[stage]
    count = 3 if stage == 0 else 1
    pieces, (own_ref, stat_ref, p_ref, base_ref) = refs[:count], refs[count : count + 4]
    refs = refs[count + 4 :]
    patch = pieces[0].shape[1]
    lane = iota((patch, 128), 1)
    if stage == 0:
        v_ref, w_ref, sum_ref, u0_ref, pay_ref, unit_ref = refs
        empty = jnp.zeros((patch, 128), f32)
        down_sum, up_sum, mask = empty, empty, empty
    else:
        before, (v_ref, w_ref, sum_ref, u0_ref, pay_ref, unit_ref) = refs[:6], refs[6:12]
        down_sum, up_sum, mask = (before[2][i] for i in range(3))
        earlier = {e for _, reached in steps[:stage] for e in reached}
        for e in pairs_of(earlier):
            v_ref[e // 2] = before[0][e // 2]
            w_ref[e // 2] = before[1][e // 2]
        for e in sorted(earlier):
            u0_ref[e] = before[3][e]
        for e in sorted(e for e in earlier if e - 1 in earlier and e + 1 in earlier):
            span = slice((e - 2) * patch // 2, (e - 1) * patch // 2)
            pay_ref[span, :] = before[4][span, :]
        for c in sorted({c for e in columns for c in (e - 1, e, e + 1)} - set(tiles)):
            span = slice(c * patch, (c + 1) * patch)
            unit_ref[span, :] = before[5][span, :]
    sources = [(ref, i) for ref in pieces for i in range(ref.shape[0])]
    for c, (ref, i) in zip(tiles, sources):
        unit, column = unit_and_mask(ref[i])
        unit_ref[c * patch : (c + 1) * patch, :] = unit
        mask = at_lane(lane, c, column, mask)
    shape = (2 * patch, 4 * patch)
    apart = iota(shape, 1) // patch - iota(shape, 0) // patch
    beside = (apart >= 0) & (apart <= 2)
    for e in pairs_of(columns):
        around = slice((e - 1) * patch, (e + 3) * patch)
        here = slice(e * patch, (e + 2) * patch)
        down = jnp.where(beside, affinity_of(own_ref[here, :], unit_ref[around, :]), 0.0)
        up = jnp.where(beside, affinity_of(unit_ref[here, :], own_ref[around, :]), 0.0)
        v_ref[e // 2] = down.astype(bf16)
        w_ref[e // 2] = up.astype(bf16)
        down = jnp.sum(down, axis=1, keepdims=True)
        up = jnp.sum(up, axis=1, keepdims=True)
        for i in range(2):
            span = slice(i * patch, (i + 1) * patch)
            down_sum = at_lane(lane, e + i, down[span], down_sum)
            up_sum = at_lane(lane, e + i, up[span], up_sum)
    sums = (down_sum, up_sum, mask)
    scale = scale_of(stat_ref, sums)
    for e in columns:
        u0_ref[e] = (scale[:, e : e + 1] * p_ref[1, e]).astype(bf16)
    inner, known = [], []
    for last in (stage - 1, stage):
        known = [e for _, reached in steps[: last + 1] for e in reached]
        inner.append({e for e in range(2, n - 2) if {e - 1, e, e + 1} <= set(known)})
    fresh = sorted(inner[1] - inner[0])
    near = {c for e in fresh for c in (e - 1, e, e + 1)}
    products(fresh, w_ref, {e: u0_ref[e] for e in near}, pay_ref, 2)
    if stage < len(steps) - 1:
        for i in range(3):
            sum_ref[i] = sums[i]
        return
    shared = up_sum - FLOOR * absent_near(stat_ref[2, patch:], 3 * patch)
    sum_ref[0], sum_ref[1], sum_ref[2] = shared, mask, scale
    tail = (n - 4) * patch // 2
    put_tail(pay_ref, tail, shared, base_ref[1])


def cross_affinity(stage, pieces, u1, stat, panel, base, before=()):
    patch, width = pieces[0].shape[1:]
    n = u1.shape[0] // patch
    given = len(pieces) + 4
    return pl.pallas_call(
        functools.partial(cross_kernel, n, stage),
        out_shape=(
            sds((n // 2 - 1, 2 * patch, 4 * patch), bf16),
            sds((n // 2 - 1, 2 * patch, 4 * patch), bf16),
            sds((3, patch, 128), f32),
            sds((n, patch, RANK), bf16),
            sds((payload_rows(n - 4, patch), 2 * RANK), bf16),
            sds((n * patch, width), bf16),
        ),
        input_output_aliases={given + i: i for i in range(len(before))},
        compiler_params=pltpu.CompilerParams(vmem_limit_bytes=VMEM_BYTES),
    )(*pieces, u1, stat, panel, base, *before)


def before_first_kernel(
    n,
    got_ref, sum_ref, stat_ref, u0_ref, m_ref, v_ref, base_ref,
    z_ref, t_ref, gain_ref, own_ref, turn_ref,
):
    patch = u0_ref.shape[1]
    half = patch // 2
    tail = (n - 2) * half
    partial, theirs = got_tail(got_ref, tail, patch)
    below_scale = sum_ref[1] * lax.rsqrt(1.0 + partial + sum_ref[0])
    scale = sum_ref[2]
    gain = 1.0 + scale * scale * stat_ref[1, patch:]
    upper = stat_ref[1, :patch]
    turn = pair_of(turn_of(theirs, base_ref[0]))
    turn_ref[0], turn_ref[1] = turn
    tiles = [unpacked(got_ref[(e - 1) * half : e * half, :].astype(f32)) for e in range(1, n - 1)]
    tiles = turned([below_scale[:, e : e + 1] * tile for e, tile in zip(range(1, n - 1), tiles)], turn)
    lower = pair_products(range(2, n - 2), v_ref, {e: tile.astype(bf16) for e, tile in zip(range(1, n - 1), tiles)})
    for e in range(2, n - 2):
        own = u0_ref[e - 1 : e + 2].reshape(3 * patch, RANK)
        total = jnp.dot(m_ref[e, :, 3 * patch :], own, preferred_element_type=f32)
        z_ref[e, :patch] = total[:patch]
        z_ref[e, patch:] = total[patch:] + lower[e]
        for ref, table in ((t_ref, scale), (gain_ref, gain), (own_ref, upper)):
            ref[e] = jnp.broadcast_to(table[:, e : e + 1], (patch, RANK))


def before_first(got, sums, stat, u0, m, v, base):
    n, patch, _ = u0.shape
    spread = sds((n, patch, RANK), f32)
    return kernel_call(
        functools.partial(before_first_kernel, n),
        (sds((n, 2 * patch, RANK), f32), spread, spread, spread, sds((2, RANK, RANK), bf16)),
    )(got, sums, stat, u0, m, v, base)


def first_kernel(
    n,
    got_ref, stat_ref, t1_ref, gain1_ref, own_ref, z_ref, p_ref, m_ref, w_ref, base_ref,
    y_ref, u_ref, t0_ref, gain0_ref, up_ref, down_ref, turn_ref,
    start_ref,
):
    patch = t1_ref.shape[1]
    half = patch // 2
    tail = (n - 4) * half
    partial, theirs = got_tail(got_ref, tail, patch)
    turn = pair_of(turn_of(theirs, base_ref[0]))
    turn_ref[0], turn_ref[1] = turn
    above = turned([unpacked(got_ref[(e - 2) * half : (e - 1) * half, :]) for e in range(2, n - 2)], turn)
    scale = stat_ref[2, :patch] * lax.rsqrt(1.0 + stat_ref[0, :patch] + partial)
    for e in range(1, n - 1):
        t = jnp.broadcast_to(scale[:, e : e + 1], (patch, RANK))
        t0_ref[e] = t
        start_ref[e] = (t * p_ref[0, e]).astype(bf16)
    for e in range(2, n - 2):
        own = start_ref[e - 1 : e + 2].reshape(3 * patch, RANK)
        total = z_ref[e] + jnp.dot(m_ref[e, :, : 3 * patch], own, preferred_element_type=f32)
        upper = total[:patch] + above[e - 2]
        gain = 1.0 + t0_ref[e] * t0_ref[e] * own_ref[e]
        gain0_ref[e] = gain
        for row, piece, t, g in ((0, upper, t0_ref[e], gain), (1, total[patch:], t1_ref[e], gain1_ref[e])):
            image = p_ref[row, e] * g + t * piece
            y_ref[row, e] = image
            scaled = t * image
            u_ref[row, e] = scaled.astype(bf16)
            if row == 0:
                up_ref[(e - 2) * half : (e - 1) * half, :] = packed(scaled).astype(bf16)
    products(range(3, n - 3), w_ref, {e: u_ref[1, e] for e in range(2, n - 2)}, down_ref, 3)


def first_iteration(got, stat, t1, gain1, own, z, panel, m, w, base):
    n, both, _ = z.shape
    patch = both // 2
    half = patch // 2
    spread = sds((n, patch, RANK), f32)
    return kernel_call(
        functools.partial(first_kernel, n),
        (
            sds((2, n, patch, RANK), f32),
            sds((2, n, patch, RANK), bf16),
            spread,
            spread,
            sds(((n - 4) * half, 2 * RANK), bf16),
            sds(((n - 6) * half, 2 * RANK), bf16),
            sds((2, RANK, RANK), bf16),
        ),
        [pltpu.VMEM((n, patch, RANK), bf16)],
    )(got, stat, t1, gain1, own, z, panel, m, w, base)


def local_kernel(low, high, m_ref, u_ref, z_ref):
    patch = u_ref.shape[2]
    for e in range(low, high):
        upper = u_ref[0, e - 1 : e + 2].reshape(3 * patch, RANK)
        lower = u_ref[1, e - 1 : e + 2].reshape(3 * patch, RANK)
        z_ref[e] = jnp.dot(m_ref[e], jnp.concatenate([upper, lower], axis=0), preferred_element_type=f32)


def local_products(low, high, m, u):
    n, both, _ = m.shape
    return kernel_call(
        functools.partial(local_kernel, low, high),
        sds((n, both, RANK), f32),
    )(m, u)


def images_of(n, low, below_ref, above_ref, z_ref, y_ref, scales, gains, turns, v_ref):
    patch = y_ref.shape[2]
    half = patch // 2
    count = n - 2 * low
    down, up = ((ref[0], ref[1]) for ref in turns)
    near = turned([unpacked(below_ref[i * half : (i + 1) * half, :]) for i in range(count + 2)], down)
    near = {low - 1 + i: tile.astype(bf16) for i, tile in enumerate(near)}
    lower = pair_products(range(low, n - low), v_ref, near)
    upper = turned([unpacked(above_ref[i * half : (i + 1) * half, :]) for i in range(count)], up)
    for e in range(low, n - low):
        pieces = (z_ref[e, :patch] + upper[e - low], z_ref[e, patch:] + lower[e])
        yield e, [y_ref[row, e] * gains[row][e] + scales[row][e] * pieces[row] for row in range(2)]


def middle_step_kernel(
    n, low,
    below_ref, above_ref, z_ref, y_ref, t0_ref, t1_ref, gain0_ref, gain1_ref, turn0_ref, turn1_ref, v_ref, w_ref,
    new_ref, u_ref, up_ref, down_ref,
):
    patch = y_ref.shape[2]
    half = patch // 2
    scales, gains = (t0_ref, t1_ref), (gain0_ref, gain1_ref)
    turns = (turn0_ref, turn1_ref)
    for e, images in images_of(n, low, below_ref, above_ref, z_ref, y_ref, scales, gains, turns, v_ref):
        for row in range(2):
            new_ref[row, e] = images[row]
            scaled = scales[row][e] * images[row]
            u_ref[row, e] = scaled.astype(bf16)
            if row == 0:
                up_ref[(e - low) * half : (e - low + 1) * half, :] = packed(scaled).astype(bf16)
    products(
        range(low + 1, n - low - 1), w_ref, {e: u_ref[1, e] for e in range(low, n - low)}, down_ref, low + 1
    )


def middle_step(low, below, above, z, y, spread, v, w):
    _, n, patch, _ = y.shape
    half = patch // 2
    return kernel_call(
        functools.partial(middle_step_kernel, n, low),
        (
            sds((2, n, patch, RANK), f32),
            sds((2, n, patch, RANK), bf16),
            sds(((n - 2 * low) * half, 2 * RANK), bf16),
            sds(((n - 2 * low - 2) * half, 2 * RANK), bf16),
        ),
    )(below, above, z, y, *spread, v, w)


def last_step_kernel(
    n, low,
    below_ref, above_ref, z_ref, y_ref, t0_ref, t1_ref, gain0_ref, gain1_ref, turn0_ref, turn1_ref, v_ref,
    new_ref, gram_ref, side_ref,
):
    patch = y_ref.shape[2]
    scales, gains = (t0_ref, t1_ref), (gain0_ref, gain1_ref)
    wide = 2 * RANK
    turns = (turn0_ref, turn1_ref)
    for e, images in images_of(n, low, below_ref, above_ref, z_ref, y_ref, scales, gains, turns, v_ref):
        for row in range(2):
            new_ref[row, e - low] = images[row]
        span = slice((e - low) * patch, (e - low + 1) * patch)
        side_ref[span, :wide], side_ref[span, wide:] = pair_of(jnp.concatenate(images, axis=1))
    gram_ref[...] = folded_gram(side_ref[...])


def last_step(low, below, above, z, y, spread, v):
    _, n, patch, _ = y.shape
    cols = n - 2 * low
    return kernel_call(
        functools.partial(last_step_kernel, n, low),
        (sds((2, cols, patch, RANK), f32), sds((RANK // 2, 2 * RANK), f32)),
        [pltpu.VMEM((cols * patch, 4 * RANK), bf16)],
    )(below, above, z, y, *spread, v)


def inverse_factor(gram, bounded=False):
    size = gram.shape[0]
    least = 0.0
    if bounded:
        least = 1e-6 * jnp.sum(jnp.where(identity(size), gram, 0.0), axis=1, keepdims=True) + 1e-16
    step = 8
    row = iota((size, 2 * size), 0)
    lane = iota((size, 2 * size), 1)
    table = jnp.concatenate([gram, identity(size).astype(f32)], axis=1)
    for k in range(0, size, step):
        cols = [jnp.broadcast_to(table[:, k + i : k + i + 1], table.shape) for i in range(step)]
        lines = [table[k + i : k + i + 1, :] for i in range(step)]
        for i in range(step):
            pivot = cols[i][k + i : k + i + 1, :]
            inverse = 1.0 / (jnp.maximum(pivot, least[k + i : k + i + 1, :]) if bounded else pivot)
            for j in range(i + 1, step):
                lines[j] = lines[j] - lines[i] * (cols[i][k + j : k + j + 1, :] * inverse)
                cols[j] = cols[j] - cols[i] * (cols[j][k + i : k + i + 1, :] * inverse)
            table = table - jnp.where(row > k + i, cols[i], 0.0) * (lines[i] * inverse)
    pivots = jnp.sum(jnp.where(row == lane, table, 0.0), axis=1, keepdims=True)
    if not bounded:
        return table[:, size:] * lax.rsqrt(pivots)
    pivots = jnp.maximum(pivots, least)
    row, lane = row[:, :size], lane[:, :size]
    upper = jnp.where(lane > row, table[:, :size], jnp.where(lane == row, pivots, 0.0))
    return table[:, size:] * lax.rsqrt(pivots), upper * lax.rsqrt(pivots)


def balanced(parts):
    while len(parts) > 1:
        parts = [a + b for a, b in zip(parts[::2], parts[1::2])]
    return parts[0]


def joint_gram(parts, base_ref):
    size = RANK // 2
    turns = turn_of(jnp.concatenate([unpacked(part[size:, :]) for part in parts[1:]], axis=0), base_ref[0])
    first = []
    for i, part in enumerate(parts[1:]):
        turn = turns[i * RANK : (i + 1) * RANK]
        first.append(
            jnp.dot(
                unpacked(part[:size, :]), turn, precision=lax.Precision.HIGHEST, preferred_element_type=f32
            )
        )
    others = lax.dot_general(
        turns, jnp.concatenate(first, axis=0), ATB, precision=lax.Precision.HIGHEST, preferred_element_type=f32
    )
    return unpacked(parts[0][:size, :]) + others


def joint_kernel(count, *refs):
    refs[-1][: RANK // 2, :] = packed(joint_gram(refs[:count], refs[count]))
    refs[-1][RANK // 2 :, :] = packed(refs[count][1])


def joint(parts, base):
    return kernel_call(functools.partial(joint_kernel, len(parts)), sds(parts[0].shape, f32))(*parts, base)


def finish_kernel(factor, count, *refs):
    parts, (base_ref, y_ref, out_ref) = refs[:count], refs[count:]
    inverse = factor * inverse_factor(joint_gram(parts, base_ref))
    zero = jnp.zeros_like(inverse)
    both = jnp.concatenate(
        [jnp.concatenate([inverse, zero], axis=1), jnp.concatenate([zero, inverse], axis=1)], axis=0
    )
    wide = 2 * RANK
    tiles, width = y_ref.shape
    pieces = [y_ref[:, q * wide : (q + 1) * wide] for q in range(width // wide)]
    y_high, y_low = pair_of(jnp.concatenate(pieces, axis=0))
    t_high, t_low = pair_of(both)

    def times(a, b):
        return lax.dot_general(a, b, ABT, preferred_element_type=f32)

    out = times(y_high, t_high) + (times(y_low, t_high) + times(y_high, t_low))
    for q in range(width // wide):
        out_ref[:, q * wide : (q + 1) * wide] = out[q * tiles : (q + 1) * tiles]


def finish(factor, parts, base, y):
    return kernel_call(
        functools.partial(finish_kernel, factor, len(parts)),
        sds(y.shape, f32),
    )(*parts, base, y)


def exchange_stages(axis):
    size = lax.axis_size(axis)
    stages, bit = [], 1
    if axis == "col":
        stages.append([1])
        bit = 2
    while bit < size:
        if 2 * bit < size:
            stages.append([bit, 2 * bit, 3 * bit])
            bit *= 4
        else:
            stages.append([bit])
            bit *= 2
    return stages


def summed_parts(gram, axis, combine):
    size = lax.axis_size(axis)
    parts = [gram]
    for partners in exchange_stages(axis):
        gram = combine(parts) if len(parts) > 1 else gram
        parts = [gram] + [lax.ppermute(gram, axis, [(i, i ^ p) for i in range(size)]) for p in partners]
    return parts


def passed_along(shard, axis, by):
    count = lax.axis_size(axis)
    pairs = [(i, i + by) for i in range(count) if 0 <= i + by < count]
    return lax.ppermute(shard, axis, pairs)


def local(features, tissue, probe):
    tile_rows, tile_cols, patches, width = features.shape
    total = tile_rows * lax.axis_size("row") * tile_cols * lax.axis_size("col") * patches
    factor = math.sqrt(float(total))
    edges = mark_edges(features, tissue)
    below_edges = passed_along(edges, "row", -1)
    parts = summed_parts(start_gram(probe), "col", balanced)
    own_panel = probe.reshape(tile_rows, tile_cols, patches, RANK)
    left_end, right_end = gate(mark_ends(features, tissue, own_panel), parts)
    middle, unit0, unit1 = own_units(features, tissue, edges)
    from_left = passed_along(right_end, "col", 1)
    from_right = passed_along(left_end, "col", -1)
    below_middle = passed_along(middle, "row", -1)
    m, sums = inside_affinity(unit0, unit1, patches)
    below_left, below_right = cut(below_edges, sums)
    _, u1, m, stat = outside_affinity(unit0, unit1, m, tissue, sums, from_left, from_right, below_left)
    panel, payload, base = start_panel(factor, parts, stat, from_left, own_panel, from_right)
    below_left, below_right = passed_along(below_right, "col", 1), passed_along(below_left, "col", -1)
    got_below = passed_along(payload, "row", -1)
    n = tile_cols + 2 * GHOST
    cross = cross_affinity(0, (below_left, below_edges, below_right), u1, stat, panel, base)
    v, w, sums, u0, payload, _ = cross_affinity(1, (below_middle,), u1, stat, panel, base, cross)
    got_above = passed_along(payload, "row", 1)
    z, t1, gain1, own, turn0 = before_first(got_below, sums, stat, u0, m, v, base)
    y, u, t0, gain0, up, down, turn1 = first_iteration(got_above, stat, t1, gain1, own, z, panel, m, w, base)
    spread = (t0, t1, gain0, gain1, turn0, turn1)
    below, above = passed_along(up, "row", -1), passed_along(down, "row", 1)
    z = local_products(3, n - 3, m, u)
    y, u, up, down = middle_step(3, below, above, z, y, spread, v, w)
    below, above = passed_along(up, "row", -1), passed_along(down, "row", 1)
    z = local_products(4, n - 4, m, u)
    y, gram = last_step(4, below, above, z, y, spread, v)

    gram = balanced(summed_parts(gram, "col", balanced))
    root = jnp.concatenate([base[1, : RANK // 2], base[1, RANK // 2 :]], axis=1)
    parts = summed_parts(jnp.concatenate([gram, root], axis=0), "row", lambda parts: joint(parts, base))
    flat = y.reshape(tile_rows * tile_cols, patches * RANK)
    out = finish(factor, parts, base, flat)
    return out.reshape(tile_rows, tile_cols, patches * RANK)


def solution(mesh):
    placed = (P("row", "col", None, None), P("row", "col", None), P("row", "col", None))
    return jax.shard_map(
        local, mesh=mesh, in_specs=placed, out_specs=P("row", "col", None), check_vma=False
    )
```
